32 devices in a mesh: mid: 8 (over y, x, core), sub: 4 (over z).
Axes of the slice: x: 2, y: 2, z: 4, core: 2. Of those that a mesh axis runs over, the one named last changes fastest.
Arguments:
- signal: bfloat16 [24576, 1152], P(('mid', 'sub')), may hold values from -6 to 6
- col_basis: bfloat16 [24576, 256], P(('mid', 'sub')), may hold values from -0.21875 to 0.21875
- right_coupling: bfloat16 [32, 2, 256, 256], P(('mid', 'sub')), may hold values from -0.375 to 0.375
- middle_coupling: bfloat16 [32, 256, 256], P(('mid', 'sub')), may hold values from -0.375 to 0.375
- left_coupling: bfloat16 [32, 2, 256, 256], P(('mid', 'sub')), may hold values from -0.375 to 0.375
- row_basis: bfloat16 [24576, 256], P(('mid', 'sub')), may hold values from -0.375 to 0.375
- node_order: int32 [8], replicated, may hold values from 0 to 7, each once
Outputs:
- product: bfloat16 [24576, 1152], P(('mid', 'sub'))
The draws below stay inside these ranges and needn't reach their ends.
Inputs may be any that keep to these rules, and one draw needn't show every extreme that they name: node_order holds each of 0 to 7 exactly once.
All inputs are finite; a program needn't handle non-finite values.
Results may differ from the reference program's by a relative error of at most 0.013.
Values may be sent and summed in bfloat16 or wider, within the bound.
No kernel may reach another device: no remote copies, remote signals or barrier semaphores. Data moves between devices by JAX's collectives and lax.ppermute only.
A program may use at most 64 MiB of HBM per device.

```python
import jax
import jax.numpy as jnp
from jax import lax

K = 256
LEAF = 768
R = 1152
NODES = 32
UNKNOWNS = 24576
N_MID = 8
N_SUB = 4


def shard_levels(own_key, extent, cuts, low, high):
    def one(dim, blocks):
        steps = jax.random.uniform(jax.random.fold_in(jax.random.fold_in(own_key, 6), dim), (blocks,), jnp.float32, low / len(cuts), high / len(cuts))
        return jnp.repeat(jnp.exp(steps), extent[dim] // blocks).reshape((-1,) + (1,) * (len(extent) - dim - 1))

    gain = one(*cuts[0])
    for cut in cuts[1:]:
        gain = gain * one(*cut)
    return gain


def centred(key, dims, spread, most, shards=(), kind=jnp.bfloat16):
    level = shard_levels(key, dims, shards, -0.22, 0.18) if shards else 1.0
    values = jax.random.normal(key, dims, jnp.float32) * spread * level
    return jnp.minimum(jnp.maximum(values, -most), most).astype(kind)


def setup_inputs(seed: int = 0) -> dict:
    key_list = jax.random.split(jax.random.key(seed), 8)
    return {
        "signal": centred(key_list[0], (UNKNOWNS, R), 1.0, 6.0, ((0, 32),)),
        "col_basis": centred(key_list[1], (UNKNOWNS, K), LEAF ** -0.5, 0.21875, ((0, 32),)),
        "right_coupling": centred(key_list[2], (NODES, 2, K, K), K ** -0.5, 0.375, ((0, 32),)),
        "middle_coupling": centred(key_list[3], (NODES, K, K), K ** -0.5, 0.375, ((0, 32),)),
        "left_coupling": centred(key_list[4], (NODES, 2, K, K), K ** -0.5, 0.375, ((0, 32),)),
        "row_basis": centred(key_list[5], (UNKNOWNS, K), K ** -0.5, 0.375, ((0, 32),)),
        "node_order": jax.random.permutation(key_list[6], N_MID).astype(jnp.int32),
    }


def apply_level(coeffs, coupling, bit):
    half = K // 2
    nodes = jnp.arange(N_SUB, dtype=jnp.int32)
    bitval = (nodes >> bit) & 1
    lower = nodes - bitval * (1 << bit)
    upper = lower + (1 << bit)
    top = coeffs[:, :half]
    bottom = coeffs[:, half:]
    chooser = (bitval == 1)[:, None, None]
    first = jnp.where(chooser, bottom[lower], top[lower])
    second = jnp.where(chooser, bottom[upper], top[upper])
    stacked = jnp.concatenate([first, second], axis=1)
    mixed = jnp.einsum("sij,sjr->sir", coupling.astype(jnp.float32), stacked.astype(jnp.float32))
    return mixed.astype(jnp.bfloat16)


def right_side(items):
    signal_blk, col_blk, right_blk = items
    coeffs = jnp.einsum("slk,slr->skr", col_blk.astype(jnp.float32), signal_blk.astype(jnp.float32)).astype(jnp.bfloat16)
    coeffs = apply_level(coeffs, right_blk[:, 0], 0)
    coeffs = apply_level(coeffs, right_blk[:, 1], 1)
    return coeffs


def left_side(items):
    gathered_blk, middle_blk, left_blk, row_blk = items
    coeffs = jnp.einsum("sij,sjr->sir", middle_blk.astype(jnp.float32), gathered_blk.astype(jnp.float32)).astype(jnp.bfloat16)
    coeffs = apply_level(coeffs, left_blk[:, 0], 1)
    coeffs = apply_level(coeffs, left_blk[:, 1], 0)
    result = jnp.einsum("slk,skr->slr", row_blk.astype(jnp.float32), coeffs.astype(jnp.float32))
    return result.astype(jnp.bfloat16)


def reference(signal, col_basis, right_coupling, middle_coupling, left_coupling, row_basis, node_order):
    pieces = K // N_MID
    signal_g = signal.reshape(N_MID, N_SUB, LEAF, R)
    col_g = col_basis.reshape(N_MID, N_SUB, LEAF, K)
    right_g = right_coupling.reshape(N_MID, N_SUB, 2, K, K)
    coeffs2 = lax.map(right_side, (signal_g, col_g, right_g))
    split = coeffs2.reshape(N_MID, N_SUB, N_MID, pieces, R)
    chosen = split[:, :, node_order.astype(jnp.int32)]
    gathered = jnp.transpose(chosen, (2, 1, 0, 3, 4)).reshape(N_MID, N_SUB, K, R)
    middle_g = middle_coupling.reshape(N_MID, N_SUB, K, K)
    left_g = left_coupling.reshape(N_MID, N_SUB, 2, K, K)
    row_g = row_basis.reshape(N_MID, N_SUB, LEAF, K)
    result = lax.map(left_side, (gathered, middle_g, left_g, row_g))
    return result.reshape(N_MID * N_SUB * LEAF, R)
```

```python
import jax
import jax.numpy as jnp
from jax import lax
from jax.sharding import PartitionSpec as P

LANES = 128
CHUNKS = 3


def cuts(columns):
    tiles = max(columns // LANES, 1)
    count = min(CHUNKS, tiles)
    edges = [tiles * i // count * LANES for i in range(count)] + [columns]
    return list(zip(edges[:-1], edges[1:]))


def swap(block, axis, distance):
    count = lax.axis_size(axis)
    return lax.ppermute(block, axis, [(i, i ^ distance) for i in range(count)])


def relative_rows(matrix, order):
    blocks = matrix.reshape((order.shape[0], -1) + matrix.shape[1:])
    return jnp.take(blocks, order, axis=0, mode="clip").reshape(matrix.shape)


def relative_columns(matrix, order):
    rows = matrix.shape[0]
    blocks = matrix.reshape(rows, order.shape[0], -1)
    return jnp.take(blocks, order, axis=1, mode="clip").reshape(matrix.shape)


def halves(matrix, axis, bitval):
    low, high = jnp.split(matrix, 2, axis=axis)
    return jnp.where(bitval == 1, jnp.concatenate([high, low], axis=axis), matrix)


def product(left, right):
    return jnp.dot(left, right, preferred_element_type=jnp.float32).astype(jnp.bfloat16)


def exchange(coeffs, axis, distance, block):
    rows, columns = coeffs.shape
    slots = coeffs.reshape(-1, 2, block, columns)
    keep, send = slots[:, 0], slots[:, 1]
    got = swap(send, axis, distance)
    return jnp.stack([keep, got], axis=1).reshape(rows, columns)


def local(signal, col_basis, right_coupling, middle_coupling, left_coupling, row_basis, node_order):
    place = lax.axis_index("sub")
    group = lax.axis_index("mid")
    groups = lax.axis_size("mid")
    width = col_basis.shape[1]
    bit0 = place & 1
    bit1 = place >> 1 & 1
    order = jnp.arange(groups, dtype=jnp.int32) ^ group

    first = halves(col_basis, 1, bit0)
    right0 = halves(halves(right_coupling[0, 0], 1, bit0), 0, bit1)
    right1 = relative_rows(halves(right_coupling[0, 1], 1, bit1), node_order[order])
    middle = halves(relative_columns(middle_coupling[0], order), 0, bit1)
    left0 = halves(halves(left_coupling[0, 0], 1, bit1), 0, bit0)
    left1 = halves(left_coupling[0, 1], 1, bit0)

    outs = []
    for low, high in cuts(signal.shape[1]):
        coeffs = lax.dot_general(
            first, signal[:, low:high], (((0,), (0,)), ((), ())), preferred_element_type=jnp.float32
        ).astype(jnp.bfloat16)
        coeffs = product(right0, exchange(coeffs, "sub", 1, width // 2))
        coeffs = product(right1, exchange(coeffs, "sub", 2, width // 2))
        distance = groups // 2
        while distance:
            coeffs = exchange(coeffs, "mid", distance, width // groups * distance)
            distance //= 2
        coeffs = product(middle, coeffs)
        coeffs = product(left0, exchange(coeffs, "sub", 2, width // 2))
        coeffs = product(left1, exchange(coeffs, "sub", 1, width // 2))
        outs.append(product(row_basis, coeffs))
    return jnp.concatenate(outs, axis=1)


def solution(mesh):
    return jax.shard_map(
        local,
        mesh=mesh,
        in_specs=(
            P(("mid", "sub"), None),
            P(("mid", "sub"), None),
            P(("mid", "sub"), None, None, None),
            P(("mid", "sub"), None, None),
            P(("mid", "sub"), None, None, None),
            P(("mid", "sub"), None),
            P(),
        ),
        out_specs=P(("mid", "sub"), None),
        check_vma=False,
    )
```

```python
import jax
import jax.numpy as jnp
from jax import lax
from jax.sharding import PartitionSpec as P

LANES = 128
CHUNKS = 3


def cuts(columns):
    tiles = max(columns // LANES, 1)
    count = min(CHUNKS, tiles)
    edges = [tiles * i // count * LANES for i in range(count)] + [columns]
    return list(zip(edges[:-1], edges[1:]))


def swap(block, axis, distance):
    count = lax.axis_size(axis)
    return lax.ppermute(block, axis, [(i, i ^ distance) for i in range(count)])


def gathered(block, axis, distance):
    count = lax.axis_size(axis)
    pairs = [[i, i ^ distance] for i in range(count) if not i & distance]
    both = lax.all_gather(block, axis, axis_index_groups=pairs)
    upper = lax.axis_index(axis) & distance
    return jnp.where(upper != 0, both[0], both[1])


def relative_rows(matrix, order):
    blocks = matrix.reshape((order.shape[0], -1) + matrix.shape[1:])
    return jnp.take(blocks, order, axis=0, mode="clip").reshape(matrix.shape)


def relative_columns(matrix, order):
    rows = matrix.shape[0]
    blocks = matrix.reshape(rows, order.shape[0], -1)
    return jnp.take(blocks, order, axis=1, mode="clip").reshape(matrix.shape)


def halves(matrix, axis, bitval):
    low, high = jnp.split(matrix, 2, axis=axis)
    return jnp.where(bitval == 1, jnp.concatenate([high, low], axis=axis), matrix)


def product(left, right):
    return jnp.dot(left, right, preferred_element_type=jnp.float32).astype(jnp.bfloat16)


def exchange(coeffs, axis, distance, block):
    rows, columns = coeffs.shape
    slots = coeffs.reshape(-1, 2, block, columns)
    keep, send = slots[:, 0], slots[:, 1]
    got = swap(send, axis, distance) if axis == "sub" else gathered(send, axis, distance)
    return jnp.stack([keep, got], axis=1).reshape(rows, columns)


def local(signal, col_basis, right_coupling, middle_coupling, left_coupling, row_basis, node_order):
    place = lax.axis_index("sub")
    group = lax.axis_index("mid")
    groups = lax.axis_size("mid")
    width = col_basis.shape[1]
    bit0 = place & 1
    bit1 = place >> 1 & 1
    order = jnp.arange(groups, dtype=jnp.int32) ^ group

    first = halves(col_basis, 1, bit0)
    right0 = halves(halves(right_coupling[0, 0], 1, bit0), 0, bit1)
    right1 = relative_rows(halves(right_coupling[0, 1], 1, bit1), node_order[order])
    middle = halves(relative_columns(middle_coupling[0], order), 0, bit1)
    left0 = halves(halves(left_coupling[0, 0], 1, bit1), 0, bit0)
    left1 = halves(left_coupling[0, 1], 1, bit0)

    outs = []
    for low, high in cuts(signal.shape[1]):
        coeffs = lax.dot_general(
            first, signal[:, low:high], (((0,), (0,)), ((), ())), preferred_element_type=jnp.float32
        ).astype(jnp.bfloat16)
        coeffs = product(right0, exchange(coeffs, "sub", 1, width // 2))
        coeffs = product(right1, exchange(coeffs, "sub", 2, width // 2))
        distance = groups // 2
        while distance:
            coeffs = exchange(coeffs, "mid", distance, width // groups * distance)
            distance //= 2
        coeffs = product(middle, coeffs)
        coeffs = product(left0, exchange(coeffs, "sub", 2, width // 2))
        coeffs = product(left1, exchange(coeffs, "sub", 1, width // 2))
        outs.append(product(row_basis, coeffs))
    return jnp.concatenate(outs, axis=1)


def solution(mesh):
    return jax.shard_map(
        local,
        mesh=mesh,
        in_specs=(
            P(("mid", "sub"), None),
            P(("mid", "sub"), None),
            P(("mid", "sub"), None, None, None),
            P(("mid", "sub"), None, None),
            P(("mid", "sub"), None, None, None),
            P(("mid", "sub"), None),
            P(),
        ),
        out_specs=P(("mid", "sub"), None),
        check_vma=False,
    )
```

```python
import jax
import jax.numpy as jnp
from jax import lax
from jax.sharding import PartitionSpec as P

LANES = 128
CHUNKS = 3


def cuts(columns):
    tiles = max(columns // LANES, 1)
    count = min(CHUNKS, tiles)
    edges = [tiles * i // count * LANES for i in range(count)] + [columns]
    return list(zip(edges[:-1], edges[1:]))


def swap(block, axis, distance):
    count = lax.axis_size(axis)
    return lax.ppermute(block, axis, [(i, i ^ distance) for i in range(count)])


def relative_rows(matrix, order):
    blocks = matrix.reshape((order.shape[0], -1) + matrix.shape[1:])
    return jnp.take(blocks, order, axis=0, mode="clip").reshape(matrix.shape)


def relative_columns(matrix, order):
    rows = matrix.shape[0]
    blocks = matrix.reshape(rows, order.shape[0], -1)
    return jnp.take(blocks, order, axis=1, mode="clip").reshape(matrix.shape)


def halves(matrix, axis, bitval):
    low, high = jnp.split(matrix, 2, axis=axis)
    return jnp.where(bitval == 1, jnp.concatenate([high, low], axis=axis), matrix)


def product(left, right):
    return jnp.dot(left, right, preferred_element_type=jnp.float32).astype(jnp.bfloat16)


def exchange(coeffs, axis, distance, block):
    rows, columns = coeffs.shape
    slots = coeffs.reshape(-1, 2, block, columns)
    keep, send = slots[:, 0], slots[:, 1]
    got = swap(send, axis, distance)
    return jnp.stack([keep, got], axis=1).reshape(rows, columns)


def local(signal, col_basis, right_coupling, middle_coupling, left_coupling, row_basis, node_order):
    place = lax.axis_index("sub")
    groups = lax.axis_size("mid")
    width = col_basis.shape[1]
    bit0 = place & 1
    bit1 = place >> 1 & 1

    first = halves(col_basis, 1, bit0)
    right0 = halves(halves(right_coupling[0, 0], 1, bit0), 0, bit1)
    right1 = relative_rows(halves(right_coupling[0, 1], 1, bit1), node_order)
    middle = halves(middle_coupling[0], 0, bit1)
    left0 = halves(halves(left_coupling[0, 0], 1, bit1), 0, bit0)
    left1 = halves(left_coupling[0, 1], 1, bit0)

    outs = []
    for low, high in cuts(signal.shape[1]):
        coeffs = lax.dot_general(
            first, signal[:, low:high], (((0,), (0,)), ((), ())), preferred_element_type=jnp.float32
        ).astype(jnp.bfloat16)
        coeffs = product(right0, exchange(coeffs, "sub", 1, width // 2))
        coeffs = product(right1, exchange(coeffs, "sub", 2, width // 2))
        coeffs = lax.all_to_all(coeffs.reshape(groups, -1, high - low), "mid", 0, 0, tiled=True).reshape(coeffs.shape)
        distance = 0
        while distance:
            coeffs = exchange(coeffs, "mid", distance, width // groups * distance)
            distance //= 2
        coeffs = product(middle, coeffs)
        coeffs = product(left0, exchange(coeffs, "sub", 2, width // 2))
        coeffs = product(left1, exchange(coeffs, "sub", 1, width // 2))
        outs.append(product(row_basis, coeffs))
    return jnp.concatenate(outs, axis=1)


def solution(mesh):
    return jax.shard_map(
        local,
        mesh=mesh,
        in_specs=(
            P(("mid", "sub"), None),
            P(("mid", "sub"), None),
            P(("mid", "sub"), None, None, None),
            P(("mid", "sub"), None, None),
            P(("mid", "sub"), None, None, None),
            P(("mid", "sub"), None),
            P(),
        ),
        out_specs=P(("mid", "sub"), None),
        check_vma=False,
    )
```

```python
import jax
import jax.numpy as jnp
from jax import lax
from jax.experimental import pallas as pl
from jax.experimental.pallas import tpu as pltpu
from jax.sharding import PartitionSpec as P

LANES = 128
CHUNKS = 3
ROWS = 16
F32 = jnp.float32
BF16 = jnp.bfloat16
WHOLE = pl.BlockSpec(memory_space=pltpu.VMEM)
SCALARS = pl.BlockSpec(memory_space=pltpu.SMEM)
PLACE = pl.BlockSpec(memory_space=pl.ANY)
HBM = pl.BlockSpec(memory_space=pltpu.HBM)


def cuts(columns):
    tiles = max(columns // LANES, 1)
    count = min(CHUNKS, tiles)
    edges = [tiles * i // count * LANES for i in range(count)] + [columns]
    return list(zip(edges[:-1], edges[1:]))


def swap(block, axis, distance):
    count = lax.axis_size(axis)
    return lax.ppermute(block, axis, [(i, i ^ distance) for i in range(count)])


def swapped(matrix, axis, flag):
    half = matrix.shape[axis] // 2
    low = lax.slice_in_dim(matrix, 0, half, axis=axis)
    high = lax.slice_in_dim(matrix, half, 2 * half, axis=axis)
    return jnp.where(flag == 1, jnp.concatenate([high, low], axis=axis), matrix)


def matmul(left, right):
    return lax.dot_general(left, right, (((1,), (0,)), ((), ())), preferred_element_type=F32)


def cost(flops, moved):
    return pl.CostEstimate(flops=flops, bytes_accessed=moved, transcendentals=0)


def call(kernel, outs, specs, operands, after, **more):
    extra = [] if after is None else [after]

    def body(*refs):
        kernel(*refs[: len(operands)], *refs[len(operands) + len(extra) :])

    return pl.pallas_call(
        body,
        in_specs=specs + [PLACE] * len(extra),
        out_shape=outs,
        **more,
    )(*operands, *extra)


def prepare(bits, rows, columns, right, middle, left, after):
    width = middle.shape[-1]

    def kernel(bits, rows, columns, right, middle, left, right0, right1, middle0, left0, left1):
        bit0, bit1 = bits[0], bits[1]
        right0[...] = swapped(swapped(right[0, 0], 1, bit0), 0, bit1)
        place = lax.broadcasted_iota(jnp.int32, (width, width), 1)
        pick = jnp.where(place == rows[...], 1.0, 0.0).astype(BF16)
        right1[...] = matmul(pick, swapped(right[0, 1], 1, bit1)).astype(BF16)
        place = lax.broadcasted_iota(jnp.int32, (width, width), 0)
        pick = jnp.where(place == columns[...], 1.0, 0.0).astype(BF16)
        middle0[...] = swapped(matmul(middle[0], pick).astype(BF16), 0, bit1)
        left0[...] = swapped(swapped(left[0, 0], 1, bit1), 0, bit0)
        left1[...] = swapped(left[0, 1], 1, bit0)

    return call(
        kernel,
        [jax.ShapeDtypeStruct((width, width), BF16)] * 5,
        [SCALARS] + [WHOLE] * 5,
        [bits, rows, columns, right, middle, left],
        after,
        out_specs=[WHOLE] * 5,
        cost_estimate=cost(4 * width**3, 20 * width**2),
    )


def first(bits, basis, signal, low, high, after):
    rows, width = basis.shape
    half, columns = width // 2, high - low
    pieces = 3 if rows % (3 * ROWS) == 0 else 1
    depth = rows // pieces

    def kernel(bits, basis, signal, kept, send, basis_here, signal_here, arrived):
        copies = []
        for i in range(pieces):
            part = pl.ds(i * depth, depth)
            copies.append(
                [
                    pltpu.make_async_copy(basis.at[part], basis_here.at[part], arrived.at[i, 0]),
                    pltpu.make_async_copy(
                        signal.at[part, pl.ds(low, columns)], signal_here.at[part], arrived.at[i, 1]
                    ),
                ]
            )
            for copy in copies[-1]:
                copy.start()
        total = jnp.zeros((width, columns), F32)
        for i in range(pieces):
            part = pl.ds(i * depth, depth)
            for copy in copies[i]:
                copy.wait()
            total += lax.dot_general(
                basis_here[part, :],
                signal_here[part, :],
                (((0,), (0,)), ((), ())),
                preferred_element_type=F32,
            )
        top, bottom = total[:half].astype(BF16), total[half:].astype(BF16)
        kept[...] = jnp.where(bits[0] == 1, bottom, top)
        send[...] = jnp.where(bits[0] == 1, top, bottom)

    return call(
        kernel,
        [jax.ShapeDtypeStruct((half, columns), BF16)] * 2,
        [SCALARS, HBM, HBM],
        [bits, basis, signal],
        after,
        out_specs=[WHOLE] * 2,
        scratch_shapes=[
            pltpu.VMEM((rows, width), BF16),
            pltpu.VMEM((rows, columns), BF16),
            pltpu.SemaphoreType.DMA((pieces, 2)),
        ],
        cost_estimate=cost(2 * rows * width * columns, 2 * rows * (columns + width)),
    )


def level(weight, keep, got, after):
    half, columns = keep.shape

    def kernel(weight, keep, got, kept, send):
        total = matmul(weight[:, :half], keep[...]) + matmul(weight[:, half:], got[...])
        kept[...] = total[:half].astype(BF16)
        send[...] = total[half:].astype(BF16)

    return call(
        kernel,
        [jax.ShapeDtypeStruct((half, columns), BF16)] * 2,
        [WHOLE] * 3,
        [weight, keep, got],
        after,
        out_specs=[WHOLE] * 2,
        cost_estimate=cost(8 * half * half * columns, 8 * half * columns),
    )


def regroup(keep, got, block, after):
    half, columns = keep.shape

    def parts(value, which):
        return [value[i * block : (i + 1) * block] for i in range(which, half // block, 2)]

    def both(keep, got, which):
        return jnp.concatenate(parts(keep, which) + parts(got, which), axis=0)

    if block % ROWS:
        return both(keep, got, 0), both(keep, got, 1)

    def kernel(keep, got, kept, send):
        kept[...] = both(keep[...], got[...], 0)
        send[...] = both(keep[...], got[...], 1)

    return call(
        kernel,
        [jax.ShapeDtypeStruct((half, columns), BF16)] * 2,
        [WHOLE] * 2,
        [keep, got],
        after,
        out_specs=[WHOLE] * 2,
        cost_estimate=cost(0, 8 * half * columns),
    )


def last(weight, basis, keep, got, before, low, columns, after):
    rows, width = basis.shape
    half, wide = keep.shape
    pieces = 3 if rows % (3 * ROWS) == 0 else 1
    depth = rows // pieces
    given = [] if before is None else [before]

    def kernel(weight, basis, keep, got, *refs):
        out, here, left = refs[len(given) :]
        coeffs = matmul(weight[:, :half], keep[...]) + matmul(weight[:, half:], got[...])
        coeffs = coeffs.astype(BF16)
        copies = []
        for i in range(pieces):
            part = pl.ds(i * depth, depth)
            here[part, :] = matmul(basis[part, :], coeffs).astype(BF16)
            copy = pltpu.make_async_copy(here.at[part], out.at[part, pl.ds(low, wide)], left.at[i])
            copy.start()
            copies.append(copy)
        for copy in copies:
            copy.wait()

    return call(
        kernel,
        jax.ShapeDtypeStruct((rows, columns), BF16),
        [WHOLE] * 4 + [HBM] * len(given),
        [weight, basis, keep, got] + given,
        after,
        out_specs=HBM,
        scratch_shapes=[pltpu.VMEM((rows, wide), BF16), pltpu.SemaphoreType.DMA((pieces,))],
        input_output_aliases={4: 0} if given else {},
        cost_estimate=cost(2 * rows * width * wide, 2 * rows * wide),
    )


def slot_bits(groups):
    bits = []
    while 1 << len(bits) < groups:
        bits.insert(0, len(bits))
    return bits


def final_slots(groups):
    order = list(range(groups))
    half = groups // 2
    keep, got = order[:half], order[half:]
    block = half // 2
    while block:
        one = [[x[i : i + block] for i in range(0, half, block)] for x in (keep, got)]
        keep = sum(one[0][0::2] + one[1][0::2], [])
        got = sum(one[0][1::2] + one[1][1::2], [])
        block //= 2
    return keep + got


def stage_order(count, steps):
    times = [(0.0, 0.1), (4.0, 2.0), (9.5, 4.0)]
    times += [(9.5 + 2.6 * i, 4.0) for i in range(1, steps)]
    times += [(9.5 + 2.6 * steps, 4.0), (15.5 + 2.6 * steps, 4.0), (18.5 + 2.6 * steps, 4.0)]
    entries = [(t + i * gap, i, s) for s, (t, gap) in enumerate(times) for i in range(count)]
    return [(i, s) for _, i, s in sorted(entries)]


def local(signal, col_basis, right_coupling, middle_coupling, left_coupling, row_basis, node_order):
    place = lax.axis_index("sub")
    group = lax.axis_index("mid")
    groups = lax.axis_size("mid")
    width = col_basis.shape[1]
    block = width // groups
    steps = len(slot_bits(groups))
    columns = signal.shape[1]
    chunks = cuts(columns)
    bits = jnp.stack([place & 1, place >> 1 & 1])
    inside = jnp.arange(block, dtype=jnp.int32)
    slots = jnp.arange(groups, dtype=jnp.int32) ^ group
    rows = (node_order[slots][:, None] * block + inside).reshape(width, 1)
    slots = jnp.array(final_slots(groups), dtype=jnp.int32) ^ group
    picked = (slots[:, None] * block + inside).reshape(1, width)

    keep, got = [None] * len(chunks), [None] * len(chunks)
    weights, out, after = None, None, None
    for i, stage in stage_order(len(chunks), steps):
        low, high = chunks[i]
        if stage == 0:
            keep[i], send = first(bits, col_basis, signal, low, high, after)
            got[i] = swap(send, "sub", 1)
            after = keep[i]
            continue
        if weights is None:
            weights = prepare(
                bits, rows, picked, right_coupling, middle_coupling, left_coupling, after
            )
            right0, right1, middle, left0, left1 = weights
            after = right0
        if stage == 1:
            keep[i], send = level(right0, keep[i], got[i], after)
            got[i] = swap(send, "sub", 2)
        elif stage == 2:
            keep[i], send = level(right1, keep[i], got[i], after)
            got[i] = swap(send, "mid", groups // 2)
        elif stage < 2 + steps:
            slot = groups >> stage - 1
            keep[i], send = regroup(keep[i], got[i], slot * block, after)
            got[i] = swap(send, "mid", slot)
        elif stage == 2 + steps:
            keep[i], send = level(middle, keep[i], got[i], after)
            got[i] = swap(send, "sub", 2)
        elif stage == 3 + steps:
            keep[i], send = level(left0, keep[i], got[i], after)
            got[i] = swap(send, "sub", 1)
        else:
            out = last(left1, row_basis, keep[i], got[i], out, low, columns, after)
        after = keep[i]
    return out


def solution(mesh):
    return jax.shard_map(
        local,
        mesh=mesh,
        in_specs=(
            P(("mid", "sub"), None),
            P(("mid", "sub"), None),
            P(("mid", "sub"), None, None, None),
            P(("mid", "sub"), None, None),
            P(("mid", "sub"), None, None, None),
            P(("mid", "sub"), None),
            P(),
        ),
        out_specs=P(("mid", "sub"), None),
        check_vma=False,
    )
```

```python
import jax
import jax.numpy as jnp
from jax import lax
from jax.experimental import pallas as pl
from jax.experimental.pallas import tpu as pltpu
from jax.sharding import PartitionSpec as P

LANES = 128
CHUNKS = 3
ROWS = 16
SCOPED = 8 * 2**20
F32 = jnp.float32
BF16 = jnp.bfloat16
WHOLE = pl.BlockSpec(memory_space=pltpu.VMEM)
SCALARS = pl.BlockSpec(memory_space=pltpu.SMEM)
PLACE = pl.BlockSpec(memory_space=pl.ANY)
HBM = pl.BlockSpec(memory_space=pltpu.HBM)


def cuts(columns):
    tiles = max(columns // LANES, 1)
    count = min(CHUNKS, tiles)
    edges = [tiles * i // count * LANES for i in range(count)] + [columns]
    return list(zip(edges[:-1], edges[1:]))


def swap(block, axis, distance):
    count = lax.axis_size(axis)
    return lax.ppermute(block, axis, [(i, i ^ distance) for i in range(count)])


def swapped(matrix, axis, flag):
    half = matrix.shape[axis] // 2
    low = lax.slice_in_dim(matrix, 0, half, axis=axis)
    high = lax.slice_in_dim(matrix, half, 2 * half, axis=axis)
    return jnp.where(flag == 1, jnp.concatenate([high, low], axis=axis), matrix)


def matmul(left, right):
    return lax.dot_general(left, right, (((1,), (0,)), ((), ())), preferred_element_type=F32)


def cost(flops, moved):
    return pl.CostEstimate(flops=flops, bytes_accessed=moved, transcendentals=0)


def call(kernel, outs, specs, operands, after, **more):
    extra = [] if after is None else [after]

    def body(*refs):
        kernel(*refs[: len(operands)], *refs[len(operands) + len(extra) :])

    return pl.pallas_call(
        body,
        in_specs=specs + [PLACE] * len(extra),
        out_shape=outs,
        compiler_params=pltpu.CompilerParams(vmem_limit_bytes=SCOPED),
        **more,
    )(*operands, *extra)


def prepare(bits, rows, columns, right, middle, left, after):
    width = middle.shape[-1]

    def kernel(bits, rows, columns, right, middle, left, right0, right1, middle0, left0, left1):
        bit0, bit1 = bits[0], bits[1]
        right0[...] = swapped(swapped(right[0, 0], 1, bit0), 0, bit1)
        place = lax.broadcasted_iota(jnp.int32, (width, width), 1)
        pick = jnp.where(place == rows[...], 1.0, 0.0).astype(BF16)
        right1[...] = matmul(pick, swapped(right[0, 1], 1, bit1)).astype(BF16)
        place = lax.broadcasted_iota(jnp.int32, (width, width), 0)
        pick = jnp.where(place == columns[...], 1.0, 0.0).astype(BF16)
        middle0[...] = swapped(matmul(middle[0], pick).astype(BF16), 0, bit1)
        left0[...] = swapped(swapped(left[0, 0], 1, bit1), 0, bit0)
        left1[...] = swapped(left[0, 1], 1, bit0)

    return call(
        kernel,
        [jax.ShapeDtypeStruct((width, width), BF16)] * 5,
        [SCALARS] + [WHOLE] * 5,
        [bits, rows, columns, right, middle, left],
        after,
        out_specs=[WHOLE] * 5,
        cost_estimate=cost(4 * width**3, 20 * width**2),
    )


def first(bits, basis, signal, low, high, after):
    rows, width = basis.shape
    half, columns = width // 2, high - low
    pieces = 3 if rows % (3 * ROWS) == 0 else 1
    depth = rows // pieces

    def kernel(bits, basis, signal, kept, send, basis_here, signal_here, arrived):
        copies = []
        for i in range(pieces):
            part = pl.ds(i * depth, depth)
            copies.append(
                [
                    pltpu.make_async_copy(basis.at[part], basis_here.at[part], arrived.at[i, 0]),
                    pltpu.make_async_copy(
                        signal.at[part, pl.ds(low, columns)], signal_here.at[part], arrived.at[i, 1]
                    ),
                ]
            )
            for copy in copies[-1]:
                copy.start()
        total = jnp.zeros((width, columns), F32)
        for i in range(pieces):
            part = pl.ds(i * depth, depth)
            for copy in copies[i]:
                copy.wait()
            total += lax.dot_general(
                basis_here[part, :],
                signal_here[part, :],
                (((0,), (0,)), ((), ())),
                preferred_element_type=F32,
            )
        top, bottom = total[:half].astype(BF16), total[half:].astype(BF16)
        kept[...] = jnp.where(bits[0] == 1, bottom, top)
        send[...] = jnp.where(bits[0] == 1, top, bottom)

    return call(
        kernel,
        [jax.ShapeDtypeStruct((half, columns), BF16)] * 2,
        [SCALARS, HBM, HBM],
        [bits, basis, signal],
        after,
        out_specs=[WHOLE] * 2,
        scratch_shapes=[
            pltpu.VMEM((rows, width), BF16),
            pltpu.VMEM((rows, columns), BF16),
            pltpu.SemaphoreType.DMA((pieces, 2)),
        ],
        cost_estimate=cost(2 * rows * width * columns, 2 * rows * (columns + width)),
    )


def level(weight, keep, got, after):
    half, columns = keep.shape

    def kernel(weight, keep, got, kept, send):
        total = matmul(weight[:, :half], keep[...]) + matmul(weight[:, half:], got[...])
        kept[...] = total[:half].astype(BF16)
        send[...] = total[half:].astype(BF16)

    return call(
        kernel,
        [jax.ShapeDtypeStruct((half, columns), BF16)] * 2,
        [WHOLE] * 3,
        [weight, keep, got],
        after,
        out_specs=[WHOLE] * 2,
        cost_estimate=cost(8 * half * half * columns, 8 * half * columns),
    )


def regroup(keep, got, block, after):
    half, columns = keep.shape

    def parts(value, which):
        return [value[i * block : (i + 1) * block] for i in range(which, half // block, 2)]

    def both(keep, got, which):
        return jnp.concatenate(parts(keep, which) + parts(got, which), axis=0)

    if block % ROWS:
        return both(keep, got, 0), both(keep, got, 1)

    def kernel(keep, got, kept, send):
        kept[...] = both(keep[...], got[...], 0)
        send[...] = both(keep[...], got[...], 1)

    return call(
        kernel,
        [jax.ShapeDtypeStruct((half, columns), BF16)] * 2,
        [WHOLE] * 2,
        [keep, got],
        after,
        out_specs=[WHOLE] * 2,
        cost_estimate=cost(0, 8 * half * columns),
    )


def last(weight, basis, keep, got, before, low, columns, after):
    rows, width = basis.shape
    half, wide = keep.shape
    pieces = 3 if rows % (3 * ROWS) == 0 else 1
    depth = rows // pieces
    given = [] if before is None else [before]

    def kernel(weight, basis, keep, got, *refs):
        out, here, left = refs[len(given) :]
        coeffs = matmul(weight[:, :half], keep[...]) + matmul(weight[:, half:], got[...])
        coeffs = coeffs.astype(BF16)
        copies = []
        for i in range(pieces):
            part = pl.ds(i * depth, depth)
            here[part, :] = matmul(basis[part, :], coeffs).astype(BF16)
            copy = pltpu.make_async_copy(here.at[part], out.at[part, pl.ds(low, wide)], left.at[i])
            copy.start()
            copies.append(copy)
        for copy in copies:
            copy.wait()

    return call(
        kernel,
        jax.ShapeDtypeStruct((rows, columns), BF16),
        [WHOLE] * 4 + [HBM] * len(given),
        [weight, basis, keep, got] + given,
        after,
        out_specs=HBM,
        scratch_shapes=[pltpu.VMEM((rows, wide), BF16), pltpu.SemaphoreType.DMA((pieces,))],
        input_output_aliases={4: 0} if given else {},
        cost_estimate=cost(2 * rows * width * wide, 2 * rows * wide),
    )


def slot_bits(groups):
    bits = []
    while 1 << len(bits) < groups:
        bits.insert(0, len(bits))
    return bits


def final_slots(groups):
    order = list(range(groups))
    half = groups // 2
    keep, got = order[:half], order[half:]
    block = half // 2
    while block:
        one = [[x[i : i + block] for i in range(0, half, block)] for x in (keep, got)]
        keep = sum(one[0][0::2] + one[1][0::2], [])
        got = sum(one[0][1::2] + one[1][1::2], [])
        block //= 2
    return keep + got


def stage_order(count, steps):
    times = [(0.0, 0.1), (4.0, 2.0), (9.5, 4.0)]
    times += [(9.5 + 2.6 * i, 4.0) for i in range(1, steps)]
    times += [(9.5 + 2.6 * steps, 4.0), (15.5 + 2.6 * steps, 4.0), (18.5 + 2.6 * steps, 4.0)]
    entries = [(t + i * gap, i, s) for s, (t, gap) in enumerate(times) for i in range(count)]
    return [(i, s) for _, i, s in sorted(entries)]


def local(signal, col_basis, right_coupling, middle_coupling, left_coupling, row_basis, node_order):
    place = lax.axis_index("sub")
    group = lax.axis_index("mid")
    groups = lax.axis_size("mid")
    width = col_basis.shape[1]
    block = width // groups
    steps = len(slot_bits(groups))
    columns = signal.shape[1]
    chunks = cuts(columns)
    bits = jnp.stack([place & 1, place >> 1 & 1])
    inside = jnp.arange(block, dtype=jnp.int32)
    slots = jnp.arange(groups, dtype=jnp.int32) ^ group
    rows = (node_order[slots][:, None] * block + inside).reshape(width, 1)
    slots = jnp.array(final_slots(groups), dtype=jnp.int32) ^ group
    picked = (slots[:, None] * block + inside).reshape(1, width)

    keep, got = [None] * len(chunks), [None] * len(chunks)
    weights, out, after = None, None, None
    for i, stage in stage_order(len(chunks), steps):
        low, high = chunks[i]
        if stage == 0:
            keep[i], send = first(bits, col_basis, signal, low, high, after)
            got[i] = swap(send, "sub", 1)
            after = keep[i]
            continue
        if weights is None:
            weights = prepare(
                bits, rows, picked, right_coupling, middle_coupling, left_coupling, after
            )
            right0, right1, middle, left0, left1 = weights
            after = right0
        if stage == 1:
            keep[i], send = level(right0, keep[i], got[i], after)
            got[i] = swap(send, "sub", 2)
        elif stage == 2:
            keep[i], send = level(right1, keep[i], got[i], after)
            got[i] = swap(send, "mid", groups // 2)
        elif stage < 2 + steps:
            slot = groups >> stage - 1
            keep[i], send = regroup(keep[i], got[i], slot * block, after)
            got[i] = swap(send, "mid", slot)
        elif stage == 2 + steps:
            keep[i], send = level(middle, keep[i], got[i], after)
            got[i] = swap(send, "sub", 2)
        elif stage == 3 + steps:
            keep[i], send = level(left0, keep[i], got[i], after)
            got[i] = swap(send, "sub", 1)
        else:
            out = last(left1, row_basis, keep[i], got[i], out, low, columns, after)
        after = keep[i]
    return out


def solution(mesh):
    return jax.shard_map(
        local,
        mesh=mesh,
        in_specs=(
            P(("mid", "sub"), None),
            P(("mid", "sub"), None),
            P(("mid", "sub"), None, None, None),
            P(("mid", "sub"), None, None),
            P(("mid", "sub"), None, None, None),
            P(("mid", "sub"), None),
            P(),
        ),
        out_specs=P(("mid", "sub"), None),
        check_vma=False,
    )
```

```python
import jax
import jax.numpy as jnp
from jax import lax
from jax.experimental import pallas as pl
from jax.experimental.pallas import tpu as pltpu
from jax.sharding import PartitionSpec as P

LANES = 128
CHUNKS = 3
ENTRY = (0, 0, 1)
ROWS = 16
SCOPED = 8 * 2**20
MOST = 59 * 2**20
F32 = jnp.float32
BF16 = jnp.bfloat16
WHOLE = pl.BlockSpec(memory_space=pltpu.VMEM)
SCALARS = pl.BlockSpec(memory_space=pltpu.SMEM)
PLACE = pl.BlockSpec(memory_space=pl.ANY)
HBM = pl.BlockSpec(memory_space=pltpu.HBM)


def cuts(columns):
    tiles = max(columns // LANES, 1)
    count = min(CHUNKS, tiles)
    edges = [tiles * i // count * LANES for i in range(count)] + [columns]
    return list(zip(edges[:-1], edges[1:]))


def swap(block, axis, distance):
    count = lax.axis_size(axis)
    return lax.ppermute(block, axis, [(i, i ^ distance) for i in range(count)])


def swapped(matrix, axis, flag):
    half = matrix.shape[axis] // 2
    low = lax.slice_in_dim(matrix, 0, half, axis=axis)
    high = lax.slice_in_dim(matrix, half, 2 * half, axis=axis)
    return jnp.where(flag == 1, jnp.concatenate([high, low], axis=axis), matrix)


def matmul(left, right):
    return lax.dot_general(left, right, (((1,), (0,)), ((), ())), preferred_element_type=F32)


def cost(flops, moved):
    return pl.CostEstimate(flops=flops, bytes_accessed=moved, transcendentals=0)


def call(kernel, name, outs, specs, operands, after, limit=SCOPED, **more):
    extra = [] if after is None else [after]

    def body(*refs):
        kernel(*refs[: len(operands)], *refs[len(operands) + len(extra) :])

    return pl.pallas_call(
        body,
        name=name,
        in_specs=specs + [PLACE] * len(extra),
        out_shape=outs,
        compiler_params=pltpu.CompilerParams(vmem_limit_bytes=limit),
        **more,
    )(*operands, *extra)


def prepare(name, info, node_order, right, middle, left, after):
    width = middle.shape[-1]
    groups = node_order.shape[0]
    block = width // groups
    last_slots = final_slots(groups)

    def kernel(info, node_order, right, middle, left, right0, right1, middle0, left0, left1):
        bit0, bit1, group = info[0], info[1], info[2]
        right0[...] = swapped(swapped(right[0, 0], 1, bit0), 0, bit1)
        place = lax.broadcasted_iota(jnp.int32, (width, 1), 0)
        source = place % block
        for slot in range(groups):
            piece = node_order[slot ^ group] * block
            source += jnp.where(place // block == slot, piece, 0)
        across = lax.broadcasted_iota(jnp.int32, (width, width), 1)
        pick = jnp.where(across == source, 1.0, 0.0).astype(BF16)
        right1[...] = matmul(pick, swapped(right[0, 1], 1, bit1)).astype(BF16)
        place = lax.broadcasted_iota(jnp.int32, (1, width), 1)
        source = place % block
        for i, slot in enumerate(last_slots):
            source += jnp.where(place // block == i, (slot ^ group) * block, 0)
        down = lax.broadcasted_iota(jnp.int32, (width, width), 0)
        pick = jnp.where(down == source, 1.0, 0.0).astype(BF16)
        middle0[...] = swapped(matmul(middle[0], pick).astype(BF16), 0, bit1)
        left0[...] = swapped(swapped(left[0, 0], 1, bit1), 0, bit0)
        left1[...] = swapped(left[0, 1], 1, bit0)

    return call(
        kernel,
        name,
        [jax.ShapeDtypeStruct((width, width), BF16)] * 5,
        [SCALARS] * 2 + [WHOLE] * 3,
        [info, node_order, right, middle, left],
        after,
        out_specs=[WHOLE] * 5,
        cost_estimate=cost(4 * width**3, 20 * width**2),
    )


def selected(total, flag, kept, send):
    half = total.shape[0] // 2
    top, bottom = total[:half].astype(BF16), total[half:].astype(BF16)
    kept[...] = jnp.where(flag == 1, bottom, top)
    send[...] = jnp.where(flag == 1, top, bottom)


def transposed_matmul(left, right):
    return lax.dot_general(left, right, (((0,), (0,)), ((), ())), preferred_element_type=F32)


def first(name, info, basis, signal, low, high, after):
    rows, width = basis.shape
    half, columns = width // 2, high - low

    def kernel(info, basis, signal, kept, send):
        total = transposed_matmul(basis[...], signal[:, low:high])
        selected(total, info[0], kept, send)

    return call(
        kernel,
        name,
        [jax.ShapeDtypeStruct((half, columns), BF16)] * 2,
        [SCALARS, WHOLE, WHOLE],
        [info, basis, signal],
        after,
        out_specs=[WHOLE] * 2,
        cost_estimate=cost(2 * rows * width * columns, 2 * rows * (columns + width)),
    )


def opening(name, info, basis, signal, low, high):
    rows, width = basis.shape
    half, columns = width // 2, high - low
    pieces = 3 if rows % (3 * ROWS) == 0 else 1
    depth = rows // pieces

    def kernel(info, basis, signal, kept, send, basis_here, signal_here, arrived):
        copies = []
        for i in range(pieces):
            part = pl.ds(i * depth, depth)
            columns_part = pl.ds(low, columns)
            copies += [
                pltpu.make_async_copy(basis.at[part], basis_here.at[part], arrived.at[i, 0]),
                pltpu.make_async_copy(
                    signal.at[part, columns_part], signal_here.at[part], arrived.at[i, 1]
                ),
            ]
        for copy in copies:
            copy.start()
        total = jnp.zeros((width, columns), F32)
        for i in range(pieces):
            part = pl.ds(i * depth, depth)
            copies[2 * i].wait()
            copies[2 * i + 1].wait()
            total += transposed_matmul(basis_here[part, :], signal_here[part, :])
        selected(total, info[0], kept, send)

    return call(
        kernel,
        name,
        [jax.ShapeDtypeStruct((half, columns), BF16)] * 2,
        [SCALARS, HBM, HBM],
        [info, basis, signal],
        None,
        limit=MOST,
        out_specs=[WHOLE] * 2,
        scratch_shapes=[
            pltpu.VMEM((rows, width), BF16),
            pltpu.VMEM((rows, columns), BF16),
            pltpu.SemaphoreType.DMA((pieces, 2)),
        ],
        cost_estimate=cost(2 * rows * width * columns, 2 * rows * (columns + width)),
    )


def level(name, weight, keep, got, after):
    half, columns = keep.shape

    def kernel(weight, keep, got, kept, send):
        total = matmul(weight[:, :half], keep[...]) + matmul(weight[:, half:], got[...])
        kept[...] = total[:half].astype(BF16)
        send[...] = total[half:].astype(BF16)

    return call(
        kernel,
        name,
        [jax.ShapeDtypeStruct((half, columns), BF16)] * 2,
        [WHOLE] * 3,
        [weight, keep, got],
        after,
        out_specs=[WHOLE] * 2,
        cost_estimate=cost(8 * half * half * columns, 8 * half * columns),
    )


def regroup(name, keep, got, block, after):
    half, columns = keep.shape

    def parts(value, which):
        return [value[i * block : (i + 1) * block] for i in range(which, half // block, 2)]

    def both(keep, got, which):
        return jnp.concatenate(parts(keep, which) + parts(got, which), axis=0)

    if block % ROWS:
        return both(keep, got, 0), both(keep, got, 1)

    def kernel(keep, got, kept, send):
        kept[...] = both(keep[...], got[...], 0)
        send[...] = both(keep[...], got[...], 1)

    return call(
        kernel,
        name,
        [jax.ShapeDtypeStruct((half, columns), BF16)] * 2,
        [WHOLE] * 2,
        [keep, got],
        after,
        out_specs=[WHOLE] * 2,
        cost_estimate=cost(0, 8 * half * columns),
    )


def last(name, weight, basis, keep, got, before, low, columns, after):
    rows, width = basis.shape
    half, wide = keep.shape
    pieces = 3 if rows % (3 * ROWS) == 0 else 1
    depth = rows // pieces
    given = [] if before is None else [before]

    def kernel(weight, basis, keep, got, *refs):
        out, here, left = refs[len(given) :]
        coeffs = matmul(weight[:, :half], keep[...]) + matmul(weight[:, half:], got[...])
        coeffs = coeffs.astype(BF16)
        copies = []
        for i in range(pieces):
            part = pl.ds(i * depth, depth)
            here[part, :] = matmul(basis[part, :], coeffs).astype(BF16)
            copy = pltpu.make_async_copy(here.at[part], out.at[part, pl.ds(low, wide)], left.at[i])
            copy.start()
            copies.append(copy)
        for copy in copies:
            copy.wait()

    return call(
        kernel,
        name,
        jax.ShapeDtypeStruct((rows, columns), BF16),
        [WHOLE] * 4 + [HBM] * len(given),
        [weight, basis, keep, got] + given,
        after,
        out_specs=HBM,
        scratch_shapes=[pltpu.VMEM((rows, wide), BF16), pltpu.SemaphoreType.DMA((pieces,))],
        input_output_aliases={4: 0} if given else {},
        cost_estimate=cost(2 * rows * width * wide, 2 * rows * wide),
    )


def final_slots(groups):
    order = list(range(groups))
    half = groups // 2
    keep, got = order[:half], order[half:]
    block = half // 2
    while block:
        one = [[x[i : i + block] for i in range(0, half, block)] for x in (keep, got)]
        keep = sum(one[0][0::2] + one[1][0::2], [])
        got = sum(one[0][1::2] + one[1][1::2], [])
        block //= 2
    return keep + got


def local(signal, col_basis, right_coupling, middle_coupling, left_coupling, row_basis, node_order):
    place = lax.axis_index("sub")
    group = lax.axis_index("mid")
    groups = lax.axis_size("mid")
    width = col_basis.shape[1]
    block = width // groups
    steps = groups.bit_length() - 1
    columns = signal.shape[1]
    chunks = cuts(columns)
    info = jnp.stack([place & 1, place >> 1 & 1, group])

    keep, got = [None] * len(chunks), [None] * len(chunks)
    weights, out, after = None, None, None
    waiting, pops, entered = [], 0, 0
    while waiting or entered < len(chunks):
        if entered < len(chunks) and pops >= ENTRY[entered]:
            i, entered = entered, entered + 1
            low, high = chunks[i]
            if i:
                keep[i], send = first(f"first{i}", info, col_basis, signal, low, high, after)
            else:
                keep[i], send = opening("opening", info, col_basis, signal, low, high)
            got[i] = swap(send, "sub", 1)
            waiting.append((i, 1))
            after = keep[i]
            continue
        i, stage = waiting.pop(0)
        pops += 1
        if weights is None:
            weights = prepare(
                "prepare", info, node_order, right_coupling, middle_coupling, left_coupling, after
            )
            right0, right1, middle, left0, left1 = weights
            after = right0
        if stage == 1:
            keep[i], send = level(f"right0_{i}", right0, keep[i], got[i], after)
            got[i] = swap(send, "sub", 2)
        elif stage == 2:
            keep[i], send = level(f"right1_{i}", right1, keep[i], got[i], after)
            got[i] = swap(send, "mid", groups // 2)
        elif stage < 2 + steps:
            slot = groups >> stage - 1
            keep[i], send = regroup(f"regroup{stage}_{i}", keep[i], got[i], slot * block, after)
            got[i] = swap(send, "mid", slot)
        elif stage == 2 + steps:
            keep[i], send = level(f"middle_{i}", middle, keep[i], got[i], after)
            got[i] = swap(send, "sub", 2)
        elif stage == 3 + steps:
            keep[i], send = level(f"left0_{i}", left0, keep[i], got[i], after)
            got[i] = swap(send, "sub", 1)
        else:
            low = chunks[i][0]
            out = last(f"last{i}", left1, row_basis, keep[i], got[i], out, low, columns, after)
            continue
        waiting.append((i, stage + 1))
        after = keep[i]
    return out


def solution(mesh):
    return jax.shard_map(
        local,
        mesh=mesh,
        in_specs=(
            P(("mid", "sub"), None),
            P(("mid", "sub"), None),
            P(("mid", "sub"), None, None, None),
            P(("mid", "sub"), None, None),
            P(("mid", "sub"), None, None, None),
            P(("mid", "sub"), None),
            P(),
        ),
        out_specs=P(("mid", "sub"), None),
        check_vma=False,
    )
```

```python
import jax
import jax.numpy as jnp
from jax import lax
from jax.experimental import pallas as pl
from jax.experimental.pallas import tpu as pltpu
from jax.sharding import PartitionSpec as P

LANES = 128
ENTRY_SHARES = (3, 3, 3)
ENTRY = (0, 0, 1)
MERGED = ((0,), (1,), (2,))
SPLIT = {}
ROWS = 16
SCOPED = 8 * 2**20
MOST = 107 * 2**19
F32 = jnp.float32
BF16 = jnp.bfloat16
WHOLE = pl.BlockSpec(memory_space=pltpu.VMEM)
SCALARS = pl.BlockSpec(memory_space=pltpu.SMEM)
PLACE = pl.BlockSpec(memory_space=pl.ANY)
HBM = pl.BlockSpec(memory_space=pltpu.HBM)


def shares(columns, weights):
    tiles = columns // LANES
    if tiles < len(weights):
        return [columns]
    edges = [round(tiles * sum(weights[:i]) / sum(weights)) * LANES for i in range(len(weights))]
    edges.append(columns)
    return [high - low for low, high in zip(edges[:-1], edges[1:])]


def swap(block, axis, distance):
    count = lax.axis_size(axis)
    return lax.ppermute(block, axis, [(i, i ^ distance) for i in range(count)])


def swapped(matrix, axis, flag):
    half = matrix.shape[axis] // 2
    low = lax.slice_in_dim(matrix, 0, half, axis=axis)
    high = lax.slice_in_dim(matrix, half, 2 * half, axis=axis)
    return jnp.where(flag == 1, jnp.concatenate([high, low], axis=axis), matrix)


def matmul(left, right):
    return lax.dot_general(left, right, (((1,), (0,)), ((), ())), preferred_element_type=F32)


def cost(flops, moved):
    return pl.CostEstimate(flops=flops, bytes_accessed=moved, transcendentals=0)


def call(kernel, name, outs, specs, operands, after, limit=SCOPED, **more):
    extra = [] if after is None else [after]

    def body(*refs):
        kernel(*refs[: len(operands)], *refs[len(operands) + len(extra) :])

    return pl.pallas_call(
        body,
        name=name,
        in_specs=specs + [PLACE] * len(extra),
        out_shape=outs,
        compiler_params=pltpu.CompilerParams(vmem_limit_bytes=limit),
        **more,
    )(*operands, *extra)


def prepare(name, node_order, right, middle, left, after):
    width = middle.shape[-1]
    groups = node_order.shape[0]
    block = width // groups
    last_slots = final_slots(groups)

    def kernel(node_order, right, middle, left, right0, right1, middle0, left0, left1):
        place, group = lax.axis_index("sub"), lax.axis_index("mid")
        bit0, bit1 = place & 1, place >> 1 & 1
        right0[...] = swapped(swapped(right[0, 0], 1, bit0), 0, bit1)
        place = lax.broadcasted_iota(jnp.int32, (width, 1), 0)
        source = place % block
        for slot in range(groups):
            piece = node_order[slot ^ group] * block
            source += jnp.where(place // block == slot, piece, 0)
        across = lax.broadcasted_iota(jnp.int32, (width, width), 1)
        pick = jnp.where(across == source, 1.0, 0.0).astype(BF16)
        right1[...] = matmul(pick, swapped(right[0, 1], 1, bit1)).astype(BF16)
        place = lax.broadcasted_iota(jnp.int32, (1, width), 1)
        source = place % block
        for i, slot in enumerate(last_slots):
            source += jnp.where(place // block == i, (slot ^ group) * block, 0)
        down = lax.broadcasted_iota(jnp.int32, (width, width), 0)
        pick = jnp.where(down == source, 1.0, 0.0).astype(BF16)
        middle0[...] = swapped(matmul(middle[0], pick).astype(BF16), 0, bit1)
        left0[...] = swapped(swapped(left[0, 0], 1, bit1), 0, bit0)
        left1[...] = swapped(left[0, 1], 1, bit0)

    return call(
        kernel,
        name,
        [jax.ShapeDtypeStruct((width, width), BF16)] * 5,
        [SCALARS] + [WHOLE] * 3,
        [node_order, right, middle, left],
        after,
        out_specs=[WHOLE] * 5,
        cost_estimate=cost(4 * width**3, 20 * width**2),
    )


def fetched(basis, signal, here, low, arrived, pieces):
    depth = signal.shape[0] // pieces
    columns = pl.ds(low, here[-1].shape[1])
    copies = []
    for i in range(pieces):
        part = pl.ds(i * depth, depth)
        both = [pltpu.make_async_copy(signal.at[part, columns], here[-1].at[part], arrived.at[i, 0])]
        if basis is not None:
            both.append(pltpu.make_async_copy(basis.at[part], here[0].at[part], arrived.at[i, 1]))
        for copy in both:
            copy.start()
        copies.append((part, both))
    return copies


def row_pieces(rows, pieces):
    return pieces if rows % (pieces * ROWS) == 0 else 1


def opening(name, basis, signal, low, high):
    rows, width = basis.shape
    half, columns = width // 2, high - low
    pieces = row_pieces(rows, 3)

    def kernel(basis, signal, kept, send, flipped, basis_here, signal_here, arrived):
        copies = fetched(basis, signal, (basis_here, signal_here), low, arrived, pieces)
        flag = lax.axis_index("sub") & 1
        total = jnp.zeros((width, columns), F32)
        for part, both in copies:
            for copy in both:
                copy.wait()
            flipped[:, part] = swapped(basis_here[part, :].T, 0, flag)
            total += matmul(flipped[:, part], signal_here[part, :])
        kept[...] = total[:half].astype(BF16)
        send[...] = total[half:].astype(BF16)

    return call(
        kernel,
        name,
        [jax.ShapeDtypeStruct((half, columns), BF16)] * 2
        + [jax.ShapeDtypeStruct((width, rows), BF16)],
        [HBM, HBM],
        [basis, signal],
        None,
        limit=MOST,
        out_specs=[WHOLE] * 3,
        scratch_shapes=[
            pltpu.VMEM((rows, width), BF16),
            pltpu.VMEM((rows, columns), BF16),
            pltpu.SemaphoreType.DMA((pieces, 2)),
        ],
        cost_estimate=cost(2 * rows * width * columns, 2 * rows * (columns + width)),
    )


def first(name, flipped, signal, low, high, after):
    width, rows = flipped.shape
    half, columns = width // 2, high - low
    pieces = row_pieces(rows, 3)

    def kernel(flipped, signal, kept, send, signal_here, arrived):
        copies = fetched(None, signal, (signal_here,), low, arrived, pieces)
        total = jnp.zeros((width, columns), F32)
        for part, both in copies:
            both[0].wait()
            total += matmul(flipped[:, part], signal_here[part, :])
        kept[...] = total[:half].astype(BF16)
        send[...] = total[half:].astype(BF16)

    return call(
        kernel,
        name,
        [jax.ShapeDtypeStruct((half, columns), BF16)] * 2,
        [WHOLE, HBM],
        [flipped, signal],
        after,
        limit=MOST,
        out_specs=[WHOLE] * 2,
        scratch_shapes=[pltpu.VMEM((rows, columns), BF16), pltpu.SemaphoreType.DMA((pieces, 1))],
        cost_estimate=cost(2 * rows * width * columns, 2 * rows * (columns + width)),
    )


def level(name, weight, pairs, widths, after):
    half = weight.shape[0] // 2
    columns = sum(widths)

    def kernel(weight, *refs):
        ins, outs = refs[: 2 * len(pairs)], refs[2 * len(pairs) :]
        keep = jnp.concatenate([ref[...] for ref in ins[0::2]], axis=1)
        got = jnp.concatenate([ref[...] for ref in ins[1::2]], axis=1)
        total = matmul(weight[:, :half], keep) + matmul(weight[:, half:], got)
        low = 0
        for i, wide in enumerate(widths):
            outs[2 * i][...] = total[:half, low : low + wide].astype(BF16)
            outs[2 * i + 1][...] = total[half:, low : low + wide].astype(BF16)
            low += wide

    flat = [block for pair in pairs for block in pair]
    outs = call(
        kernel,
        name,
        [jax.ShapeDtypeStruct((half, wide), BF16) for wide in widths for _ in range(2)],
        [WHOLE] * (1 + len(flat)),
        [weight] + flat,
        after,
        out_specs=[WHOLE] * (2 * len(widths)),
        cost_estimate=cost(8 * half * half * columns, 8 * half * columns),
    )
    return list(zip(outs[0::2], outs[1::2]))


def regroup(name, keep, got, block, after):
    half, columns = keep.shape

    def parts(value, which):
        return [value[i * block : (i + 1) * block] for i in range(which, half // block, 2)]

    def both(keep, got, which):
        return jnp.concatenate(parts(keep, which) + parts(got, which), axis=0)

    if block % ROWS:
        return [(both(keep, got, 0), both(keep, got, 1))]

    def kernel(keep, got, kept, send):
        kept[...] = both(keep[...], got[...], 0)
        send[...] = both(keep[...], got[...], 1)

    outs = call(
        kernel,
        name,
        [jax.ShapeDtypeStruct((half, columns), BF16)] * 2,
        [WHOLE] * 2,
        [keep, got],
        after,
        out_specs=[WHOLE] * 2,
        cost_estimate=cost(0, 8 * half * columns),
    )
    return [tuple(outs)]


def last(name, weight, basis, keep, got, before, low, columns, after):
    rows, width = basis.shape
    half, wide = keep.shape
    pieces = row_pieces(rows, 6)
    depth = rows // pieces
    given = [] if before is None else [before]

    def kernel(weight, basis, keep, got, *refs):
        out, here, left = refs[len(given) :]
        coeffs = matmul(weight[:, :half], keep[...]) + matmul(weight[:, half:], got[...])
        coeffs = coeffs.astype(BF16)
        copies = []
        for i in range(pieces):
            part = pl.ds(i * depth, depth)
            here[part, :] = matmul(basis[part, :], coeffs).astype(BF16)
            copy = pltpu.make_async_copy(here.at[part], out.at[part, pl.ds(low, wide)], left.at[i])
            copy.start()
            copies.append(copy)
        for copy in copies:
            copy.wait()

    return call(
        kernel,
        name,
        jax.ShapeDtypeStruct((rows, columns), BF16),
        [WHOLE] * 4 + [HBM] * len(given),
        [weight, basis, keep, got] + given,
        after,
        out_specs=HBM,
        scratch_shapes=[pltpu.VMEM((rows, wide), BF16), pltpu.SemaphoreType.DMA((pieces,))],
        input_output_aliases={4: 0} if given else {},
        cost_estimate=cost(2 * rows * width * wide, 2 * rows * wide),
    )


def final_slots(groups):
    order = list(range(groups))
    half = groups // 2
    keep, got = order[:half], order[half:]
    block = half // 2
    while block:
        one = [[x[i : i + block] for i in range(0, half, block)] for x in (keep, got)]
        keep = sum(one[0][0::2] + one[1][0::2], [])
        got = sum(one[0][1::2] + one[1][1::2], [])
        block //= 2
    return keep + got


def local(signal, col_basis, right_coupling, middle_coupling, left_coupling, row_basis, node_order):
    groups = lax.axis_size("mid")
    width = col_basis.shape[1]
    block = width // groups
    steps = groups.bit_length() - 1
    columns = signal.shape[1]
    chunks = shares(columns, ENTRY_SHARES)
    starts = [sum(chunks[:i]) for i in range(len(chunks))]
    merged = {i: group for group in MERGED for i in group}
    if len(chunks) < len(ENTRY_SHARES):
        merged = {i: (i,) for i in range(len(chunks))}

    couplings, out, after, flipped = None, None, None, None
    waiting, pops, entered = [], 0, 0
    parked = {}
    while waiting or entered < len(chunks):
        if entered < len(chunks) and (pops >= ENTRY[entered] or not waiting):
            i, entered = entered, entered + 1
            low, high = starts[i], starts[i] + chunks[i]
            if i:
                keep, send = first(f"first{i}", flipped, signal, low, high, after)
            else:
                keep, send, flipped = opening("opening", col_basis, signal, low, high)
            waiting.append((1, (i,), low, keep, swap(send, "sub", 1)))
            after = keep
            continue
        stage, ids, low, keep, got = waiting.pop(0)
        pops += 1
        wide = keep.shape[1]
        name = "".join(str(i) for i in ids)
        if couplings is None:
            couplings = prepare(
                "prepare", node_order, right_coupling, middle_coupling, left_coupling, after
            )
            right0, right1, middle, left0, left1 = couplings
            after = right0
        if stage == 1:
            pairs = level(f"right0_{name}", right0, [(keep, got)], [wide], after)
            route = ("sub", 2)
        elif stage == 2:
            parked[ids[0]] = (keep, got)
            ids = merged[ids[0]]
            if any(i not in parked for i in ids):
                continue
            wide = sum(chunks[i] for i in ids)
            low = starts[ids[0]]
            pairs = level(f"right1_{name}", right1, [parked[i] for i in ids], [wide], after)
            route = ("mid", groups // 2)
        elif stage < 2 + steps:
            slot = groups >> stage - 1
            pairs = regroup(f"regroup{stage}_{name}", keep, got, slot * block, after)
            route = ("mid", slot)
        elif stage == 2 + steps:
            widths = shares(wide, SPLIT.get(ids, (1,)))
            pairs = level(f"middle_{name}", middle, [(keep, got)], widths, after)
            route = ("sub", 2)
        elif stage == 3 + steps:
            pairs = level(f"left0_{name}", left0, [(keep, got)], [wide], after)
            route = ("sub", 1)
        else:
            out = last(f"last{low}", left1, row_basis, keep, got, out, low, columns, after)
            continue
        for keep, send in pairs:
            waiting.append((stage + 1, ids, low, keep, swap(send, *route)))
            low += keep.shape[1]
        after = pairs[0][0]
    return out


def solution(mesh):
    return jax.shard_map(
        local,
        mesh=mesh,
        in_specs=(
            P(("mid", "sub"), None),
            P(("mid", "sub"), None),
            P(("mid", "sub"), None, None, None),
            P(("mid", "sub"), None, None),
            P(("mid", "sub"), None, None, None),
            P(("mid", "sub"), None),
            P(),
        ),
        out_specs=P(("mid", "sub"), None),
        check_vma=False,
    )
```

```python
import jax
import jax.numpy as jnp
from jax import lax
from jax.experimental import pallas as pl
from jax.experimental.pallas import tpu as pltpu
from jax.sharding import PartitionSpec as P

LANES = 128
ENTRY_SHARES = (3, 3, 3)
ENTRY = (0, 0, 1)
MERGED = ((0,), (1,), (2,))
SPLIT = {}
ROWS = 16
SCOPED = 8 * 2**20
MOST = 213 * 2**18
F32 = jnp.float32
BF16 = jnp.bfloat16
WHOLE = pl.BlockSpec(memory_space=pltpu.VMEM)
SCALARS = pl.BlockSpec(memory_space=pltpu.SMEM)
PLACE = pl.BlockSpec(memory_space=pl.ANY)
HBM = pl.BlockSpec(memory_space=pltpu.HBM)


def shares(columns, weights):
    tiles = columns // LANES
    if tiles < len(weights):
        return [columns]
    edges = [round(tiles * sum(weights[:i]) / sum(weights)) * LANES for i in range(len(weights))]
    edges.append(columns)
    return [high - low for low, high in zip(edges[:-1], edges[1:])]


def swap(block, axis, distance):
    count = lax.axis_size(axis)
    return lax.ppermute(block, axis, [(i, i ^ distance) for i in range(count)])


def swapped(matrix, axis, flag):
    half = matrix.shape[axis] // 2
    low = lax.slice_in_dim(matrix, 0, half, axis=axis)
    high = lax.slice_in_dim(matrix, half, 2 * half, axis=axis)
    return jnp.where(flag == 1, jnp.concatenate([high, low], axis=axis), matrix)


def matmul(left, right):
    return lax.dot_general(left, right, (((1,), (0,)), ((), ())), preferred_element_type=F32)


def cost(flops, moved):
    return pl.CostEstimate(flops=flops, bytes_accessed=moved, transcendentals=0)


def call(kernel, name, outs, specs, operands, after, limit=SCOPED, **more):
    extra = [] if after is None else [after]

    def body(*refs):
        kernel(*refs[: len(operands)], *refs[len(operands) + len(extra) :])

    return pl.pallas_call(
        body,
        name=name,
        in_specs=specs + [PLACE] * len(extra),
        out_shape=outs,
        compiler_params=pltpu.CompilerParams(vmem_limit_bytes=limit),
        **more,
    )(*operands, *extra)


def prepare(name, node_order, slots_out, slots_in, right, middle, left, after):
    width = middle.shape[-1]
    groups = node_order.shape[0]
    block = width // groups

    def kernel(node_order, right, middle, left, right0, right1, middle0, left0, left1):
        place, group = lax.axis_index("sub"), lax.axis_index("mid")
        bit0, bit1 = place & 1, place >> 1 & 1
        right0[...] = swapped(swapped(right[0, 0], 1, bit0), 0, bit1)
        place = lax.broadcasted_iota(jnp.int32, (width, 1), 0)
        source = place % block
        for i, slot in enumerate(slots_out):
            piece = node_order[slot ^ group] * block
            source += jnp.where(place // block == i, piece, 0)
        across = lax.broadcasted_iota(jnp.int32, (width, width), 1)
        pick = jnp.where(across == source, 1.0, 0.0).astype(BF16)
        right1[...] = matmul(pick, swapped(right[0, 1], 1, bit1)).astype(BF16)
        place = lax.broadcasted_iota(jnp.int32, (1, width), 1)
        source = place % block
        for i, slot in enumerate(slots_in):
            source += jnp.where(place // block == i, (slot ^ group) * block, 0)
        down = lax.broadcasted_iota(jnp.int32, (width, width), 0)
        pick = jnp.where(down == source, 1.0, 0.0).astype(BF16)
        middle0[...] = swapped(matmul(middle[0], pick).astype(BF16), 0, bit1)
        left0[...] = swapped(swapped(left[0, 0], 1, bit1), 0, bit0)
        left1[...] = swapped(left[0, 1], 1, bit0)

    return call(
        kernel,
        name,
        [jax.ShapeDtypeStruct((width, width), BF16)] * 5,
        [SCALARS] + [WHOLE] * 3,
        [node_order, right, middle, left],
        after,
        out_specs=[WHOLE] * 5,
        cost_estimate=cost(4 * width**3, 20 * width**2),
    )


def row_pieces(rows, pieces):
    return pieces if rows % (pieces * ROWS) == 0 else 1


def opening(name, basis, signal, widths):
    rows, width = basis.shape
    half = width // 2
    pieces = row_pieces(rows, 6)
    depth = rows // pieces
    lows = [sum(widths[:i]) for i in range(len(widths))]

    def kernel(basis, signal, *refs):
        outs, (basis_here, signal_here, arrived, basis_arrived) = refs[:-4], refs[-4:]
        fetch_basis = pltpu.make_async_copy(basis, basis_here, basis_arrived)
        fetch_basis.start()
        copies = []
        for i in range(pieces):
            part = pl.ds(i * depth, depth)
            copies.append(
                pltpu.make_async_copy(signal.at[part], signal_here.at[part], arrived.at[i])
            )
            copies[-1].start()
        fetch_basis.wait()
        flipped = swapped(basis_here[...].T, 0, lax.axis_index("sub") & 1)
        for copy in copies:
            copy.wait()
        for i, (low, wide) in enumerate(zip(lows, widths)):
            total = matmul(flipped, signal_here[:, low : low + wide])
            outs[2 * i][...] = total[:half].astype(BF16)
            outs[2 * i + 1][...] = total[half:].astype(BF16)

    outs = call(
        kernel,
        name,
        [jax.ShapeDtypeStruct((half, wide), BF16) for wide in widths for _ in range(2)],
        [HBM, HBM],
        [basis, signal],
        None,
        limit=MOST,
        out_specs=[WHOLE] * (2 * len(widths)),
        scratch_shapes=[
            pltpu.VMEM((rows, width), BF16),
            pltpu.VMEM(signal.shape, BF16),
            pltpu.SemaphoreType.DMA((pieces,)),
            pltpu.SemaphoreType.DMA,
        ],
        cost_estimate=cost(2 * rows * width * sum(widths), 2 * rows * (sum(widths) + width)),
    )
    return list(zip(outs[0::2], outs[1::2]))


def level(name, weight, chunks, widths, count, after):
    width = weight.shape[0]
    depth = width // count
    columns = sum(widths)
    blocks = len(chunks[0])

    def kernel(weight, *refs):
        ins, outs = refs[: blocks * len(chunks)], refs[blocks * len(chunks) :]
        stacked = [
            jnp.concatenate([ref[...] for ref in ins[i * blocks : (i + 1) * blocks]], axis=0)
            for i in range(len(chunks))
        ]
        total = matmul(weight[...], jnp.concatenate(stacked, axis=1))
        low = 0
        for i, wide in enumerate(widths):
            for j in range(count):
                part = total[j * depth : (j + 1) * depth, low : low + wide]
                outs[i * count + j][...] = part.astype(BF16)
            low += wide

    flat = [block for chunk in chunks for block in chunk]
    outs = call(
        kernel,
        name,
        [jax.ShapeDtypeStruct((depth, wide), BF16) for wide in widths for _ in range(count)],
        [WHOLE] * (1 + len(flat)),
        [weight] + flat,
        after,
        out_specs=[WHOLE] * (count * len(widths)),
        cost_estimate=cost(2 * width * width * columns, 4 * width * columns),
    )
    return [list(outs[i * count : (i + 1) * count]) for i in range(len(widths))]


def digits(groups):
    bits = groups.bit_length() - 1
    found = [(0, 2)]
    while found[-1][0] + (found[-1][1].bit_length() - 1) < bits:
        shift = found[-1][0] + found[-1][1].bit_length() - 1
        found.append((shift, 4 if shift + 2 <= bits else 2))
    return found


def by_digit(slots, digit):
    shift, radix = digit
    return [[r for r in slots if r >> shift & radix - 1 == value] for value in range(radix)]


def regroup(name, blocks, layout, digit, block, after):
    columns = blocks[0].shape[1]
    place = {r: (i, j) for i, held in enumerate(layout) for j, r in enumerate(held)}
    wanted = by_digit(sum(layout, []), digit)

    def sort(values):
        parts = [[values[place[r][0]][place[r][1] * block :][:block] for r in held] for held in wanted]
        return [jnp.concatenate(part, axis=0) for part in parts]

    if block % ROWS:
        return sort(blocks), wanted

    def kernel(*refs):
        for ref, value in zip(refs[len(blocks) :], sort([ref[...] for ref in refs[: len(blocks)]])):
            ref[...] = value

    outs = call(
        kernel,
        name,
        [jax.ShapeDtypeStruct((len(held) * block, columns), BF16) for held in wanted],
        [WHOLE] * len(blocks),
        blocks,
        after,
        out_specs=[WHOLE] * len(wanted),
        cost_estimate=cost(0, 4 * block * len(place) * columns),
    )
    return list(outs), wanted


def last(name, weight, basis, keep, got, before, low, columns, after):
    rows, width = basis.shape
    wide = keep.shape[1]
    pieces = row_pieces(rows, 6)
    depth = rows // pieces
    given = [] if before is None else [before]

    def kernel(weight, basis, keep, got, *refs):
        out, here, left = refs[len(given) :]
        stacked = jnp.concatenate([keep[...], got[...]], axis=0)
        coeffs = matmul(weight[...], stacked).astype(BF16)
        copies = []
        for i in range(pieces):
            part = pl.ds(i * depth, depth)
            here[part, :] = matmul(basis[part, :], coeffs).astype(BF16)
            copy = pltpu.make_async_copy(here.at[part], out.at[part, pl.ds(low, wide)], left.at[i])
            copy.start()
            copies.append(copy)
        for copy in copies:
            copy.wait()

    return call(
        kernel,
        name,
        jax.ShapeDtypeStruct((rows, columns), BF16),
        [WHOLE] * 4 + [HBM] * len(given),
        [weight, basis, keep, got] + given,
        after,
        out_specs=HBM,
        scratch_shapes=[pltpu.VMEM((rows, wide), BF16), pltpu.SemaphoreType.DMA((pieces,))],
        input_output_aliases={4: 0} if given else {},
        cost_estimate=cost(2 * rows * width * wide, 2 * rows * wide),
    )


def local(signal, col_basis, right_coupling, middle_coupling, left_coupling, row_basis, node_order):
    groups = lax.axis_size("mid")
    width = col_basis.shape[1]
    block = width // groups
    columns = signal.shape[1]
    chunks = shares(columns, ENTRY_SHARES)
    starts = [sum(chunks[:i]) for i in range(len(chunks))]
    merged = {i: group for group in MERGED for i in group}
    if len(chunks) < len(ENTRY_SHARES):
        merged = {i: (i,) for i in range(len(chunks))}
    steps = digits(groups)
    layouts = [by_digit(range(groups), steps[0])]
    for step in steps[1:]:
        layouts.append(by_digit(sum(layouts[-1], []), step))

    opened = opening("opening", col_basis, signal, chunks)
    couplings, out, after = None, None, None
    waiting, pops, entered = [], 0, 0
    parked = {}
    while waiting or entered < len(chunks):
        if entered < len(chunks) and (pops >= ENTRY[entered] or not waiting):
            i, entered = entered, entered + 1
            keep, send = opened[i]
            waiting.append((1, (i,), starts[i], [keep, swap(send, "sub", 1)]))
            continue
        stage, ids, low, blocks = waiting.pop(0)
        pops += 1
        wide = blocks[0].shape[1]
        name = "".join(str(i) for i in ids)
        if couplings is None:
            couplings = prepare(
                "prepare",
                node_order,
                sum(layouts[0], []),
                sum(layouts[-1], []),
                right_coupling,
                middle_coupling,
                left_coupling,
                after,
            )
            right0, right1, middle, left0, left1 = couplings
            after = right0
        if stage == 1:
            results = level(f"right0_{name}", right0, [blocks], [wide], 2, after)
            axis, shift = "sub", 1
        elif stage == 2:
            parked[ids[0]] = blocks
            ids = merged[ids[0]]
            if any(i not in parked for i in ids):
                continue
            wide = sum(chunks[i] for i in ids)
            low = starts[ids[0]]
            blocks = [parked[i] for i in ids]
            results = level(f"right1_{name}", right1, blocks, [wide], steps[0][1], after)
            axis, shift = "mid", steps[0][0]
        elif stage < 2 + len(steps):
            step = steps[stage - 2]
            held_as = layouts[stage - 3]
            results = [regroup(f"regroup{stage}_{name}", blocks, held_as, step, block, after)[0]]
            axis, shift = "mid", step[0]
        elif stage == 2 + len(steps):
            widths = shares(wide, SPLIT.get(ids, (1,)))
            results = level(f"middle_{name}", middle, [blocks], widths, 2, after)
            axis, shift = "sub", 1
        elif stage == 3 + len(steps):
            results = level(f"left0_{name}", left0, [blocks], [wide], 2, after)
            axis, shift = "sub", 0
        else:
            out = last(f"last{low}", left1, row_basis, *blocks, out, low, columns, after)
            continue
        after = results[0][0]
        for result in results:
            moved = [swap(send, axis, i + 1 << shift) for i, send in enumerate(result[1:])]
            waiting.append((stage + 1, ids, low, result[:1] + moved))
            low += result[0].shape[1]
    return out


def solution(mesh):
    return jax.shard_map(
        local,
        mesh=mesh,
        in_specs=(
            P(("mid", "sub"), None),
            P(("mid", "sub"), None),
            P(("mid", "sub"), None, None, None),
            P(("mid", "sub"), None, None),
            P(("mid", "sub"), None, None, None),
            P(("mid", "sub"), None),
            P(),
        ),
        out_specs=P(("mid", "sub"), None),
        check_vma=False,
    )
```

```python
import jax
import jax.numpy as jnp
from jax import lax
from jax.experimental import pallas as pl
from jax.experimental.pallas import tpu as pltpu
from jax.sharding import PartitionSpec as P

LANES = 128
ENTRY_SHARES = (1, 2, 3, 3)
ENTRY = (0, 0, 0, 2)
MERGED = ((0, 1), (2,), (3,))
SPLIT = {}
ROWS = 16
SCOPED = 8 * 2**20
MOST = 213 * 2**18
F32 = jnp.float32
BF16 = jnp.bfloat16
WHOLE = pl.BlockSpec(memory_space=pltpu.VMEM)
SCALARS = pl.BlockSpec(memory_space=pltpu.SMEM)
PLACE = pl.BlockSpec(memory_space=pl.ANY)
HBM = pl.BlockSpec(memory_space=pltpu.HBM)


def shares(columns, weights):
    tiles = columns // LANES
    if tiles < len(weights):
        return [columns]
    edges = [round(tiles * sum(weights[:i]) / sum(weights)) * LANES for i in range(len(weights))]
    edges.append(columns)
    return [high - low for low, high in zip(edges[:-1], edges[1:])]


def swap(block, axis, distance):
    count = lax.axis_size(axis)
    return lax.ppermute(block, axis, [(i, i ^ distance) for i in range(count)])


def swapped(matrix, axis, flag):
    half = matrix.shape[axis] // 2
    low = lax.slice_in_dim(matrix, 0, half, axis=axis)
    high = lax.slice_in_dim(matrix, half, 2 * half, axis=axis)
    return jnp.where(flag == 1, jnp.concatenate([high, low], axis=axis), matrix)


def matmul(left, right):
    return lax.dot_general(left, right, (((1,), (0,)), ((), ())), preferred_element_type=F32)


def cost(flops, moved):
    return pl.CostEstimate(flops=flops, bytes_accessed=moved, transcendentals=0)


def call(kernel, name, outs, specs, operands, after, limit=SCOPED, **more):
    extra = [] if after is None else [after]

    def body(*refs):
        kernel(*refs[: len(operands)], *refs[len(operands) + len(extra) :])

    return pl.pallas_call(
        body,
        name=name,
        in_specs=specs + [PLACE] * len(extra),
        out_shape=outs,
        compiler_params=pltpu.CompilerParams(vmem_limit_bytes=limit),
        **more,
    )(*operands, *extra)


def prepare(name, node_order, slots_out, slots_in, right, middle, left, after):
    width = middle.shape[-1]
    groups = node_order.shape[0]
    block = width // groups

    def kernel(node_order, right, middle, left, right0, right1, middle0, left0, left1):
        place, group = lax.axis_index("sub"), lax.axis_index("mid")
        bit0, bit1 = place & 1, place >> 1 & 1
        right0[...] = swapped(swapped(right[0, 0], 1, bit0), 0, bit1)
        place = lax.broadcasted_iota(jnp.int32, (width, 1), 0)
        source = place % block
        for i, slot in enumerate(slots_out):
            piece = node_order[slot ^ group] * block
            source += jnp.where(place // block == i, piece, 0)
        across = lax.broadcasted_iota(jnp.int32, (width, width), 1)
        pick = jnp.where(across == source, 1.0, 0.0).astype(BF16)
        right1[...] = matmul(pick, swapped(right[0, 1], 1, bit1)).astype(BF16)
        place = lax.broadcasted_iota(jnp.int32, (1, width), 1)
        source = place % block
        for i, slot in enumerate(slots_in):
            source += jnp.where(place // block == i, (slot ^ group) * block, 0)
        down = lax.broadcasted_iota(jnp.int32, (width, width), 0)
        pick = jnp.where(down == source, 1.0, 0.0).astype(BF16)
        middle0[...] = swapped(matmul(middle[0], pick).astype(BF16), 0, bit1)
        left0[...] = swapped(swapped(left[0, 0], 1, bit1), 0, bit0)
        left1[...] = swapped(left[0, 1], 1, bit0)

    return call(
        kernel,
        name,
        [jax.ShapeDtypeStruct((width, width), BF16)] * 5,
        [SCALARS] + [WHOLE] * 3,
        [node_order, right, middle, left],
        after,
        out_specs=[WHOLE] * 5,
        cost_estimate=cost(4 * width**3, 20 * width**2),
    )


def row_pieces(rows, pieces):
    return pieces if rows % (pieces * ROWS) == 0 else 1


def opening(name, basis, signal, widths):
    rows, width = basis.shape
    half = width // 2
    pieces = row_pieces(rows, 6)
    depth = rows // pieces
    lows = [sum(widths[:i]) for i in range(len(widths))]

    def kernel(basis, signal, *refs):
        outs, (basis_here, signal_here, arrived, basis_arrived) = refs[:-4], refs[-4:]
        fetch_basis = pltpu.make_async_copy(basis, basis_here, basis_arrived)
        fetch_basis.start()
        copies = []
        for i in range(pieces):
            part = pl.ds(i * depth, depth)
            copies.append(
                pltpu.make_async_copy(signal.at[part], signal_here.at[part], arrived.at[i])
            )
            copies[-1].start()
        fetch_basis.wait()
        flipped = swapped(basis_here[...].T, 0, lax.axis_index("sub") & 1)
        for copy in copies:
            copy.wait()
        for i, (low, wide) in enumerate(zip(lows, widths)):
            total = matmul(flipped, signal_here[:, low : low + wide])
            outs[2 * i][...] = total[:half].astype(BF16)
            outs[2 * i + 1][...] = total[half:].astype(BF16)

    outs = call(
        kernel,
        name,
        [jax.ShapeDtypeStruct((half, wide), BF16) for wide in widths for _ in range(2)],
        [HBM, HBM],
        [basis, signal],
        None,
        limit=MOST,
        out_specs=[WHOLE] * (2 * len(widths)),
        scratch_shapes=[
            pltpu.VMEM((rows, width), BF16),
            pltpu.VMEM(signal.shape, BF16),
            pltpu.SemaphoreType.DMA((pieces,)),
            pltpu.SemaphoreType.DMA,
        ],
        cost_estimate=cost(2 * rows * width * sum(widths), 2 * rows * (sum(widths) + width)),
    )
    return list(zip(outs[0::2], outs[1::2]))


def level(name, weight, chunks, widths, count, after):
    width = weight.shape[0]
    depth = width // count
    columns = sum(widths)
    blocks = len(chunks[0])

    def kernel(weight, *refs):
        ins, outs = refs[: blocks * len(chunks)], refs[blocks * len(chunks) :]
        stacked = [
            jnp.concatenate([ref[...] for ref in ins[i * blocks : (i + 1) * blocks]], axis=0)
            for i in range(len(chunks))
        ]
        total = matmul(weight[...], jnp.concatenate(stacked, axis=1))
        low = 0
        for i, wide in enumerate(widths):
            for j in range(count):
                part = total[j * depth : (j + 1) * depth, low : low + wide]
                outs[i * count + j][...] = part.astype(BF16)
            low += wide

    flat = [block for chunk in chunks for block in chunk]
    outs = call(
        kernel,
        name,
        [jax.ShapeDtypeStruct((depth, wide), BF16) for wide in widths for _ in range(count)],
        [WHOLE] * (1 + len(flat)),
        [weight] + flat,
        after,
        out_specs=[WHOLE] * (count * len(widths)),
        cost_estimate=cost(2 * width * width * columns, 4 * width * columns),
    )
    return [list(outs[i * count : (i + 1) * count]) for i in range(len(widths))]


def digits(groups):
    bits = groups.bit_length() - 1
    found = [(0, 2)]
    while found[-1][0] + (found[-1][1].bit_length() - 1) < bits:
        shift = found[-1][0] + found[-1][1].bit_length() - 1
        found.append((shift, 4 if shift + 2 <= bits else 2))
    return found


def by_digit(slots, digit):
    shift, radix = digit
    return [[r for r in slots if r >> shift & radix - 1 == value] for value in range(radix)]


def regroup(name, blocks, layout, digit, block, after):
    columns = blocks[0].shape[1]
    place = {r: (i, j) for i, held in enumerate(layout) for j, r in enumerate(held)}
    wanted = by_digit(sum(layout, []), digit)

    def sort(values):
        parts = [[values[place[r][0]][place[r][1] * block :][:block] for r in held] for held in wanted]
        return [jnp.concatenate(part, axis=0) for part in parts]

    if block % ROWS:
        return sort(blocks), wanted

    def kernel(*refs):
        for ref, value in zip(refs[len(blocks) :], sort([ref[...] for ref in refs[: len(blocks)]])):
            ref[...] = value

    outs = call(
        kernel,
        name,
        [jax.ShapeDtypeStruct((len(held) * block, columns), BF16) for held in wanted],
        [WHOLE] * len(blocks),
        blocks,
        after,
        out_specs=[WHOLE] * len(wanted),
        cost_estimate=cost(0, 4 * block * len(place) * columns),
    )
    return list(outs), wanted


def last(name, weight, basis, keep, got, before, low, columns, after):
    rows, width = basis.shape
    wide = keep.shape[1]
    pieces = row_pieces(rows, 6)
    depth = rows // pieces
    given = [] if before is None else [before]

    def kernel(weight, basis, keep, got, *refs):
        out, here, left = refs[len(given) :]
        stacked = jnp.concatenate([keep[...], got[...]], axis=0)
        coeffs = matmul(weight[...], stacked).astype(BF16)
        copies = []
        for i in range(pieces):
            part = pl.ds(i * depth, depth)
            here[part, :] = matmul(basis[part, :], coeffs).astype(BF16)
            copy = pltpu.make_async_copy(here.at[part], out.at[part, pl.ds(low, wide)], left.at[i])
            copy.start()
            copies.append(copy)
        for copy in copies:
            copy.wait()

    return call(
        kernel,
        name,
        jax.ShapeDtypeStruct((rows, columns), BF16),
        [WHOLE] * 4 + [HBM] * len(given),
        [weight, basis, keep, got] + given,
        after,
        out_specs=HBM,
        scratch_shapes=[pltpu.VMEM((rows, wide), BF16), pltpu.SemaphoreType.DMA((pieces,))],
        input_output_aliases={4: 0} if given else {},
        cost_estimate=cost(2 * rows * width * wide, 2 * rows * wide),
    )


def local(signal, col_basis, right_coupling, middle_coupling, left_coupling, row_basis, node_order):
    groups = lax.axis_size("mid")
    width = col_basis.shape[1]
    block = width // groups
    columns = signal.shape[1]
    chunks = shares(columns, ENTRY_SHARES)
    starts = [sum(chunks[:i]) for i in range(len(chunks))]
    merged = {i: group for group in MERGED for i in group}
    if len(chunks) < len(ENTRY_SHARES):
        merged = {i: (i,) for i in range(len(chunks))}
    steps = digits(groups)
    layouts = [by_digit(range(groups), steps[0])]
    for step in steps[1:]:
        layouts.append(by_digit(sum(layouts[-1], []), step))

    opened = opening("opening", col_basis, signal, chunks)
    couplings, out, after = None, None, None
    waiting, pops, entered = [], 0, 0
    parked = {}
    while waiting or entered < len(chunks):
        if entered < len(chunks) and (pops >= ENTRY[entered] or not waiting):
            i, entered = entered, entered + 1
            keep, send = opened[i]
            waiting.append((1, (i,), starts[i], [keep, swap(send, "sub", 1)]))
            continue
        stage, ids, low, blocks = waiting.pop(0)
        pops += 1
        wide = blocks[0].shape[1]
        name = "".join(str(i) for i in ids)
        if couplings is None:
            couplings = prepare(
                "prepare",
                node_order,
                sum(layouts[0], []),
                sum(layouts[-1], []),
                right_coupling,
                middle_coupling,
                left_coupling,
                after,
            )
            right0, right1, middle, left0, left1 = couplings
            after = right0
        if stage == 1:
            results = level(f"right0_{name}", right0, [blocks], [wide], 2, after)
            axis, shift = "sub", 1
        elif stage == 2:
            parked[ids[0]] = blocks
            ids = merged[ids[0]]
            if any(i not in parked for i in ids):
                continue
            wide = sum(chunks[i] for i in ids)
            low = starts[ids[0]]
            blocks = [parked[i] for i in ids]
            results = level(f"right1_{name}", right1, blocks, [wide], steps[0][1], after)
            axis, shift = "mid", steps[0][0]
        elif stage < 2 + len(steps):
            step = steps[stage - 2]
            held_as = layouts[stage - 3]
            results = [regroup(f"regroup{stage}_{name}", blocks, held_as, step, block, after)[0]]
            axis, shift = "mid", step[0]
        elif stage == 2 + len(steps):
            widths = shares(wide, SPLIT.get(ids, (1,)))
            results = level(f"middle_{name}", middle, [blocks], widths, 2, after)
            axis, shift = "sub", 1
        elif stage == 3 + len(steps):
            results = level(f"left0_{name}", left0, [blocks], [wide], 2, after)
            axis, shift = "sub", 0
        else:
            out = last(f"last{low}", left1, row_basis, *blocks, out, low, columns, after)
            continue
        after = results[0][0]
        for result in results:
            moved = [swap(send, axis, i + 1 << shift) for i, send in enumerate(result[1:])]
            waiting.append((stage + 1, ids, low, result[:1] + moved))
            low += result[0].shape[1]
    return out


def solution(mesh):
    return jax.shard_map(
        local,
        mesh=mesh,
        in_specs=(
            P(("mid", "sub"), None),
            P(("mid", "sub"), None),
            P(("mid", "sub"), None, None, None),
            P(("mid", "sub"), None, None),
            P(("mid", "sub"), None, None, None),
            P(("mid", "sub"), None),
            P(),
        ),
        out_specs=P(("mid", "sub"), None),
        check_vma=False,
    )
```

```python
import jax
import jax.numpy as jnp
from jax import lax
from jax.experimental import pallas as pl
from jax.experimental.pallas import tpu as pltpu
from jax.sharding import PartitionSpec as P

LANES = 128
ENTRY_SHARES = (3, 3, 3)
ENTRY = (0, 0, 1)
MERGED = ((0,), (1,), (2,))
SPLIT = {}
ROWS = 16
SCOPED = 8 * 2**20
MOST = 213 * 2**18
F32 = jnp.float32
BF16 = jnp.bfloat16
WHOLE = pl.BlockSpec(memory_space=pltpu.VMEM)
SCALARS = pl.BlockSpec(memory_space=pltpu.SMEM)
PLACE = pl.BlockSpec(memory_space=pl.ANY)
HBM = pl.BlockSpec(memory_space=pltpu.HBM)


def shares(columns, weights):
    tiles = columns // LANES
    if tiles < len(weights):
        return [columns]
    edges = [round(tiles * sum(weights[:i]) / sum(weights)) * LANES for i in range(len(weights))]
    edges.append(columns)
    return [high - low for low, high in zip(edges[:-1], edges[1:])]


def swap(block, axis, distance):
    count = lax.axis_size(axis)
    return lax.ppermute(block, axis, [(i, i ^ distance) for i in range(count)])


def swapped(matrix, axis, flag):
    half = matrix.shape[axis] // 2
    low = lax.slice_in_dim(matrix, 0, half, axis=axis)
    high = lax.slice_in_dim(matrix, half, 2 * half, axis=axis)
    return jnp.where(flag == 1, jnp.concatenate([high, low], axis=axis), matrix)


def matmul(left, right):
    return lax.dot_general(left, right, (((1,), (0,)), ((), ())), preferred_element_type=F32)


def cost(flops, moved):
    return pl.CostEstimate(flops=flops, bytes_accessed=moved, transcendentals=0)


def call(kernel, name, outs, specs, operands, after, limit=SCOPED, **more):
    extra = [] if after is None else [after]

    def body(*refs):
        kernel(*refs[: len(operands)], *refs[len(operands) + len(extra) :])

    return pl.pallas_call(
        body,
        name=name,
        in_specs=specs + [PLACE] * len(extra),
        out_shape=outs,
        compiler_params=pltpu.CompilerParams(vmem_limit_bytes=limit),
        **more,
    )(*operands, *extra)


def prepare(name, node_order, right, middle, left, held):
    width = middle.shape[-1]
    groups = node_order.shape[0]
    block = width // groups

    def kernel(node_order, right, middle, left, *refs):
        right0, right1, middle0, left0, left1 = refs[len(held) : len(held) + 5]
        for block_in, block_out in zip(refs[: len(held)], refs[len(held) + 5 :]):
            block_out[...] = block_in[...]
        place, group = lax.axis_index("sub"), lax.axis_index("mid")
        bit0, bit1 = place & 1, place >> 1 & 1
        right0[...] = swapped(swapped(right[0, 0], 1, bit0), 0, bit1)
        place = lax.broadcasted_iota(jnp.int32, (width, 1), 0)
        source = place % block
        for i in range(groups):
            chip, other = i % (groups // 2), i // (groups // 2)
            piece = node_order[2 * chip + (group & 1 ^ other)] * block
            source += jnp.where(place // block == i, piece, 0)
        across = lax.broadcasted_iota(jnp.int32, (width, width), 1)
        pick = jnp.where(across == source, 1.0, 0.0).astype(BF16)
        right1[...] = matmul(pick, swapped(right[0, 1], 1, bit1)).astype(BF16)
        place = lax.broadcasted_iota(jnp.int32, (1, width), 1)
        source = place % block
        for i in range(groups):
            source += jnp.where(place // block == i, (i ^ group & 1) * block, 0)
        down = lax.broadcasted_iota(jnp.int32, (width, width), 0)
        pick = jnp.where(down == source, 1.0, 0.0).astype(BF16)
        middle0[...] = swapped(matmul(middle[0], pick).astype(BF16), 0, bit1)
        left0[...] = swapped(swapped(left[0, 0], 1, bit1), 0, bit0)
        left1[...] = swapped(left[0, 1], 1, bit0)

    return call(
        kernel,
        name,
        [jax.ShapeDtypeStruct((width, width), BF16)] * 5
        + [jax.ShapeDtypeStruct(block.shape, BF16) for block in held],
        [SCALARS] + [WHOLE] * (3 + len(held)),
        [node_order, right, middle, left] + held,
        None,
        out_specs=[WHOLE] * (5 + len(held)),
        cost_estimate=cost(4 * width**3, 20 * width**2),
    )


def row_pieces(rows, pieces):
    return pieces if rows % (pieces * ROWS) == 0 else 1


def opening(name, basis, signal, widths):
    rows, width = basis.shape
    half = width // 2
    pieces = row_pieces(rows, 6)
    depth = rows // pieces
    lows = [sum(widths[:i]) for i in range(len(widths))]

    def kernel(basis, signal, *refs):
        outs, (basis_here, signal_here, arrived, basis_arrived) = refs[:-4], refs[-4:]
        fetch_basis = pltpu.make_async_copy(basis, basis_here, basis_arrived)
        fetch_basis.start()
        copies = []
        for i in range(pieces):
            part = pl.ds(i * depth, depth)
            copies.append(
                pltpu.make_async_copy(signal.at[part], signal_here.at[part], arrived.at[i])
            )
            copies[-1].start()
        fetch_basis.wait()
        flipped = swapped(basis_here[...].T, 0, lax.axis_index("sub") & 1)
        for copy in copies:
            copy.wait()
        for i, (low, wide) in enumerate(zip(lows, widths)):
            total = matmul(flipped, signal_here[:, low : low + wide])
            outs[2 * i][...] = total[:half].astype(BF16)
            outs[2 * i + 1][...] = total[half:].astype(BF16)

    outs = call(
        kernel,
        name,
        [jax.ShapeDtypeStruct((half, wide), BF16) for wide in widths for _ in range(2)],
        [HBM, HBM],
        [basis, signal],
        None,
        limit=MOST,
        out_specs=[WHOLE] * (2 * len(widths)),
        scratch_shapes=[
            pltpu.VMEM((rows, width), BF16),
            pltpu.VMEM(signal.shape, BF16),
            pltpu.SemaphoreType.DMA((pieces,)),
            pltpu.SemaphoreType.DMA,
        ],
        cost_estimate=cost(2 * rows * width * sum(widths), 2 * rows * (sum(widths) + width)),
    )
    return list(zip(outs[0::2], outs[1::2]))


def level(name, weight, chunks, widths, count, after):
    width = weight.shape[0]
    depth = width // count
    columns = sum(widths)
    blocks = len(chunks[0])

    def kernel(weight, *refs):
        ins, outs = refs[: blocks * len(chunks)], refs[blocks * len(chunks) :]
        stacked = [
            jnp.concatenate([ref[...] for ref in ins[i * blocks : (i + 1) * blocks]], axis=0)
            for i in range(len(chunks))
        ]
        total = matmul(weight[...], jnp.concatenate(stacked, axis=1))
        low = 0
        for i, wide in enumerate(widths):
            for j in range(count):
                part = total[j * depth : (j + 1) * depth, low : low + wide]
                outs[i * count + j][...] = part.astype(BF16)
            low += wide

    flat = [block for chunk in chunks for block in chunk]
    outs = call(
        kernel,
        name,
        [jax.ShapeDtypeStruct((depth, wide), BF16) for wide in widths for _ in range(count)],
        [WHOLE] * (1 + len(flat)),
        [weight] + flat,
        after,
        out_specs=[WHOLE] * (count * len(widths)),
        cost_estimate=cost(2 * width * width * columns, 4 * width * columns),
    )
    return [list(outs[i * count : (i + 1) * count]) for i in range(len(widths))]


def interleave(name, keep, got, block, after):
    half, columns = keep.shape

    def turns(one, other):
        parts = [x[i : i + block] for i in range(0, half, block) for x in (one, other)]
        return jnp.concatenate(parts, axis=0)

    if block % ROWS:
        return turns(keep, got)

    def kernel(keep, got, out):
        out[...] = turns(keep[...], got[...])

    return call(
        kernel,
        name,
        jax.ShapeDtypeStruct((2 * half, columns), BF16),
        [WHOLE] * 2,
        [keep, got],
        after,
        out_specs=WHOLE,
        cost_estimate=cost(0, 8 * half * columns),
    )


def among_chips(block):
    groups = lax.axis_size("mid")
    chips = groups // 2
    members = [[2 * chip + core for chip in range(chips)] for core in range(2)]
    pieces = block.reshape(chips, -1, block.shape[1])
    moved = lax.all_to_all(pieces, "mid", 0, 0, axis_index_groups=members, tiled=True)
    return moved.reshape(block.shape)


def last(name, weight, basis, keep, got, before, low, columns, after):
    rows, width = basis.shape
    wide = keep.shape[1]
    pieces = row_pieces(rows, 6)
    depth = rows // pieces
    given = [] if before is None else [before]

    def kernel(weight, basis, keep, got, *refs):
        out, here, left = refs[len(given) :]
        stacked = jnp.concatenate([keep[...], got[...]], axis=0)
        coeffs = matmul(weight[...], stacked).astype(BF16)
        copies = []
        for i in range(pieces):
            part = pl.ds(i * depth, depth)
            here[part, :] = matmul(basis[part, :], coeffs).astype(BF16)
            copy = pltpu.make_async_copy(here.at[part], out.at[part, pl.ds(low, wide)], left.at[i])
            copy.start()
            copies.append(copy)
        for copy in copies:
            copy.wait()

    return call(
        kernel,
        name,
        jax.ShapeDtypeStruct((rows, columns), BF16),
        [WHOLE] * 4 + [HBM] * len(given),
        [weight, basis, keep, got] + given,
        after,
        out_specs=HBM,
        scratch_shapes=[pltpu.VMEM((rows, wide), BF16), pltpu.SemaphoreType.DMA((pieces,))],
        input_output_aliases={4: 0} if given else {},
        cost_estimate=cost(2 * rows * width * wide, 2 * rows * wide),
    )


def local(signal, col_basis, right_coupling, middle_coupling, left_coupling, row_basis, node_order):
    groups = lax.axis_size("mid")
    width = col_basis.shape[1]
    block = width // groups
    columns = signal.shape[1]
    chunks = shares(columns, ENTRY_SHARES)
    starts = [sum(chunks[:i]) for i in range(len(chunks))]
    merged = {i: group for group in MERGED for i in group}
    if len(chunks) < len(ENTRY_SHARES):
        merged = {i: (i,) for i in range(len(chunks))}

    opened = opening("opening", col_basis, signal, chunks)
    right0, right1, middle, left0, left1, *sends = prepare(
        "prepare",
        node_order,
        right_coupling,
        middle_coupling,
        left_coupling,
        [send for _, send in opened[1:]],
    )
    opened = opened[:1] + [(keep, send) for (keep, _), send in zip(opened[1:], sends)]
    out, after = None, right0
    waiting, pops, entered = [], 0, 0
    parked = {}
    while waiting or entered < len(chunks):
        if entered < len(chunks) and (pops >= ENTRY[entered] or not waiting):
            i, entered = entered, entered + 1
            keep, send = opened[i]
            waiting.append((1, (i,), starts[i], [keep, swap(send, "sub", 1)]))
            continue
        stage, ids, low, blocks = waiting.pop(0)
        pops += 1
        wide = blocks[0].shape[1]
        name = "".join(str(i) for i in ids)
        if stage == 1:
            results = level(f"right0_{name}", right0, [blocks], [wide], 2, after)
            axis, shift = "sub", 1
        elif stage == 2:
            parked[ids[0]] = blocks
            ids = merged[ids[0]]
            if any(i not in parked for i in ids):
                continue
            wide = sum(chunks[i] for i in ids)
            low = starts[ids[0]]
            blocks = [parked[i] for i in ids]
            results = level(f"right1_{name}", right1, blocks, [wide], 2, after)
            axis, shift = "mid", 0
        elif stage == 3:
            mixed = interleave(f"interleave_{name}", *blocks, block, after)
            waiting.append((stage + 1, ids, low, [among_chips(mixed)]))
            after = mixed
            continue
        elif stage == 4:
            widths = shares(wide, SPLIT.get(ids, (1,)))
            results = level(f"middle_{name}", middle, [blocks], widths, 2, after)
            axis, shift = "sub", 1
        elif stage == 5:
            results = level(f"left0_{name}", left0, [blocks], [wide], 2, after)
            axis, shift = "sub", 0
        else:
            out = last(f"last{low}", left1, row_basis, *blocks, out, low, columns, after)
            continue
        after = results[0][0]
        for result in results:
            moved = [swap(send, axis, i + 1 << shift) for i, send in enumerate(result[1:])]
            waiting.append((stage + 1, ids, low, result[:1] + moved))
            low += result[0].shape[1]
    return out


def solution(mesh):
    return jax.shard_map(
        local,
        mesh=mesh,
        in_specs=(
            P(("mid", "sub"), None),
            P(("mid", "sub"), None),
            P(("mid", "sub"), None, None, None),
            P(("mid", "sub"), None, None),
            P(("mid", "sub"), None, None, None),
            P(("mid", "sub"), None),
            P(),
        ),
        out_specs=P(("mid", "sub"), None),
        check_vma=False,
    )
```

```python
import jax
import jax.numpy as jnp
from jax import lax
from jax.experimental import pallas as pl
from jax.experimental.pallas import tpu as pltpu
from jax.sharding import PartitionSpec as P

LANES = 128
ENTRY_SHARES = (3, 3, 3)
ENTRY = (0, 0, 1)
MERGED = ((0,), (1,), (2,))
SPLIT = {}
ROWS = 16
SCOPED = 8 * 2**20
MOST = 213 * 2**18
F32 = jnp.float32
BF16 = jnp.bfloat16
WHOLE = pl.BlockSpec(memory_space=pltpu.VMEM)
SCALARS = pl.BlockSpec(memory_space=pltpu.SMEM)
SPAN = pl.CostEstimate(flops=2 * 10**9, bytes_accessed=0, transcendentals=0)
PLACE = pl.BlockSpec(memory_space=pl.ANY)
HBM = pl.BlockSpec(memory_space=pltpu.HBM)


def shares(columns, weights):
    tiles = columns // LANES
    if tiles < len(weights):
        return [columns]
    edges = [round(tiles * sum(weights[:i]) / sum(weights)) * LANES for i in range(len(weights))]
    edges.append(columns)
    return [high - low for low, high in zip(edges[:-1], edges[1:])]


def swap(block, axis, distance):
    count = lax.axis_size(axis)
    return lax.ppermute(block, axis, [(i, i ^ distance) for i in range(count)])


def swapped(matrix, axis, flag):
    half = matrix.shape[axis] // 2
    low = lax.slice_in_dim(matrix, 0, half, axis=axis)
    high = lax.slice_in_dim(matrix, half, 2 * half, axis=axis)
    return jnp.where(flag == 1, jnp.concatenate([high, low], axis=axis), matrix)


def matmul(left, right):
    return lax.dot_general(left, right, (((1,), (0,)), ((), ())), preferred_element_type=F32)


def call(kernel, name, outs, specs, operands, after, limit=SCOPED, **more):
    extra = [] if after is None else [after]

    def body(*refs):
        kernel(*refs[: len(operands)], *refs[len(operands) + len(extra) :])

    return pl.pallas_call(
        body,
        name=name,
        in_specs=specs + [PLACE] * len(extra),
        out_shape=outs,
        compiler_params=pltpu.CompilerParams(vmem_limit_bytes=limit),
        **more,
    )(*operands, *extra)


def prepare(name, node_order, slots_out, slots_in, right, middle, left, held):
    width = middle.shape[-1]
    groups = node_order.shape[0]
    block = width // groups

    def kernel(node_order, right, middle, left, *refs):
        right0, right1, middle0, left0, left1 = refs[len(held) : len(held) + 5]
        for block_in, block_out in zip(refs[: len(held)], refs[len(held) + 5 :]):
            block_out[...] = block_in[...]
        place, group = lax.axis_index("sub"), lax.axis_index("mid")
        bit0, bit1 = place & 1, place >> 1 & 1
        right0[...] = swapped(swapped(right[0, 0], 1, bit0), 0, bit1)
        place = lax.broadcasted_iota(jnp.int32, (width, 1), 0)
        source = place % block
        for i, slot in enumerate(slots_out):
            piece = node_order[slot ^ group] * block
            source += jnp.where(place // block == i, piece, 0)
        across = lax.broadcasted_iota(jnp.int32, (width, width), 1)
        pick = jnp.where(across == source, 1.0, 0.0).astype(BF16)
        right1[...] = matmul(pick, swapped(right[0, 1], 1, bit1)).astype(BF16)
        place = lax.broadcasted_iota(jnp.int32, (1, width), 1)
        source = place % block
        for i, slot in enumerate(slots_in):
            source += jnp.where(place // block == i, (slot ^ group) * block, 0)
        down = lax.broadcasted_iota(jnp.int32, (width, width), 0)
        pick = jnp.where(down == source, 1.0, 0.0).astype(BF16)
        middle0[...] = swapped(matmul(middle[0], pick).astype(BF16), 0, bit1)
        left0[...] = swapped(swapped(left[0, 0], 1, bit1), 0, bit0)
        left1[...] = swapped(left[0, 1], 1, bit0)

    return call(
        kernel,
        name,
        [jax.ShapeDtypeStruct((width, width), BF16)] * 5
        + [jax.ShapeDtypeStruct(block.shape, BF16) for block in held],
        [SCALARS] + [WHOLE] * (3 + len(held)),
        [node_order, right, middle, left] + held,
        None,
        out_specs=[WHOLE] * (5 + len(held)),
        cost_estimate=SPAN,
    )


def row_pieces(rows, pieces):
    return pieces if rows % (pieces * ROWS) == 0 else 1


def opening(name, basis, signal, widths):
    rows, width = basis.shape
    half = width // 2
    pieces = row_pieces(rows, 3)
    depth = rows // pieces
    lows = [sum(widths[:i]) for i in range(len(widths))]

    def kernel(basis, signal, *refs):
        outs, (basis_here, signal_here, sums, arrived, basis_arrived) = refs[:-5], refs[-5:]
        fetch_basis = pltpu.make_async_copy(basis, basis_here, basis_arrived)
        fetch_basis.start()
        copies = []
        for i in range(pieces):
            part = pl.ds(i * depth, depth)
            copies.append(
                pltpu.make_async_copy(signal.at[part], signal_here.at[part], arrived.at[i])
            )
            copies[-1].start()
        fetch_basis.wait()
        flipped = swapped(basis_here[...].T, 0, lax.axis_index("sub") & 1)
        for i, copy in enumerate(copies):
            copy.wait()
            rows_here = slice(i * depth, (i + 1) * depth)
            if i < pieces - 1:
                part = matmul(flipped[:, rows_here], signal_here[rows_here, :])
                sums[...] = part if i == 0 else sums[...] + part
        for i, (low, wide) in enumerate(zip(lows, widths)):
            here = slice(low, low + wide)
            total = matmul(flipped[:, rows_here], signal_here[rows_here, here])
            if pieces > 1:
                total += sums[:, here]
            outs[2 * i][...] = total[:half].astype(BF16)
            outs[2 * i + 1][...] = total[half:].astype(BF16)

    outs = call(
        kernel,
        name,
        [jax.ShapeDtypeStruct((half, wide), BF16) for wide in widths for _ in range(2)],
        [HBM, HBM],
        [basis, signal],
        None,
        limit=MOST,
        out_specs=[WHOLE] * (2 * len(widths)),
        scratch_shapes=[
            pltpu.VMEM((rows, width), BF16),
            pltpu.VMEM(signal.shape, BF16),
            pltpu.VMEM((width, signal.shape[1]), F32),
            pltpu.SemaphoreType.DMA((pieces,)),
            pltpu.SemaphoreType.DMA,
        ],
        cost_estimate=SPAN,
    )
    return list(zip(outs[0::2], outs[1::2]))


def level(name, weight, chunks, widths, count, after):
    width = weight.shape[0]
    depth = width // count
    columns = sum(widths)
    blocks = len(chunks[0])

    def kernel(weight, *refs):
        ins, outs = refs[: blocks * len(chunks)], refs[blocks * len(chunks) :]
        stacked = [
            jnp.concatenate([ref[...] for ref in ins[i * blocks : (i + 1) * blocks]], axis=0)
            for i in range(len(chunks))
        ]
        total = matmul(weight[...], jnp.concatenate(stacked, axis=1))
        low = 0
        for i, wide in enumerate(widths):
            for j in range(count):
                part = total[j * depth : (j + 1) * depth, low : low + wide]
                outs[i * count + j][...] = part.astype(BF16)
            low += wide

    flat = [block for chunk in chunks for block in chunk]
    outs = call(
        kernel,
        name,
        [jax.ShapeDtypeStruct((depth, wide), BF16) for wide in widths for _ in range(count)],
        [WHOLE] * (1 + len(flat)),
        [weight] + flat,
        after,
        out_specs=[WHOLE] * (count * len(widths)),
        cost_estimate=SPAN,
    )
    return [list(outs[i * count : (i + 1) * count]) for i in range(len(widths))]


def digits(groups):
    bits = groups.bit_length() - 1
    found = [(0, 2)]
    while found[-1][0] + (found[-1][1].bit_length() - 1) < bits:
        shift = found[-1][0] + found[-1][1].bit_length() - 1
        found.append((shift, 4 if shift + 2 <= bits else 2))
    return found


def by_digit(slots, digit):
    shift, radix = digit
    return [[r for r in slots if r >> shift & radix - 1 == value] for value in range(radix)]


def regroup(name, blocks, layout, digit, block, after):
    columns = blocks[0].shape[1]
    place = {r: (i, j) for i, held in enumerate(layout) for j, r in enumerate(held)}
    wanted = by_digit(sum(layout, []), digit)

    def sort(values):
        parts = [[values[place[r][0]][place[r][1] * block :][:block] for r in held] for held in wanted]
        return [jnp.concatenate(part, axis=0) for part in parts]

    if block % ROWS:
        return sort(blocks), wanted

    def kernel(*refs):
        for ref, value in zip(refs[len(blocks) :], sort([ref[...] for ref in refs[: len(blocks)]])):
            ref[...] = value

    outs = call(
        kernel,
        name,
        [jax.ShapeDtypeStruct((len(held) * block, columns), BF16) for held in wanted],
        [WHOLE] * len(blocks),
        blocks,
        after,
        out_specs=[WHOLE] * len(wanted),
        cost_estimate=SPAN,
    )
    return list(outs), wanted


def last(name, weight, basis, keep, got, before, low, columns, after):
    rows, width = basis.shape
    wide = keep.shape[1]
    pieces = row_pieces(rows, 6)
    depth = rows // pieces
    given = [] if before is None else [before]

    def kernel(weight, basis, keep, got, *refs):
        out, here, left = refs[len(given) :]
        stacked = jnp.concatenate([keep[...], got[...]], axis=0)
        coeffs = matmul(weight[...], stacked).astype(BF16)
        copies = []
        for i in range(pieces):
            part = pl.ds(i * depth, depth)
            here[part, :] = matmul(basis[part, :], coeffs).astype(BF16)
            copy = pltpu.make_async_copy(here.at[part], out.at[part, pl.ds(low, wide)], left.at[i])
            copy.start()
            copies.append(copy)
        for copy in copies:
            copy.wait()

    return call(
        kernel,
        name,
        jax.ShapeDtypeStruct((rows, columns), BF16),
        [WHOLE] * 4 + [HBM] * len(given),
        [weight, basis, keep, got] + given,
        after,
        out_specs=HBM,
        scratch_shapes=[pltpu.VMEM((rows, wide), BF16), pltpu.SemaphoreType.DMA((pieces,))],
        input_output_aliases={4: 0} if given else {},
        cost_estimate=SPAN,
    )


def local(signal, col_basis, right_coupling, middle_coupling, left_coupling, row_basis, node_order):
    groups = lax.axis_size("mid")
    width = col_basis.shape[1]
    block = width // groups
    columns = signal.shape[1]
    chunks = shares(columns, ENTRY_SHARES)
    starts = [sum(chunks[:i]) for i in range(len(chunks))]
    merged = {i: group for group in MERGED for i in group}
    if len(chunks) < len(ENTRY_SHARES):
        merged = {i: (i,) for i in range(len(chunks))}
    steps = digits(groups)
    layouts = [by_digit(range(groups), steps[0])]
    for step in steps[1:]:
        layouts.append(by_digit(sum(layouts[-1], []), step))

    opened = opening("opening", col_basis, signal, chunks)
    right0, right1, middle, left0, left1, *sends = prepare(
        "prepare",
        node_order,
        sum(layouts[0], []),
        sum(layouts[-1], []),
        right_coupling,
        middle_coupling,
        left_coupling,
        [send for _, send in opened[1:]],
    )
    opened = opened[:1] + [(keep, send) for (keep, _), send in zip(opened[1:], sends)]
    out, after = None, right0
    waiting, pops, entered = [], 0, 0
    parked = {}
    while waiting or entered < len(chunks):
        if entered < len(chunks) and (pops >= ENTRY[entered] or not waiting):
            i, entered = entered, entered + 1
            keep, send = opened[i]
            waiting.append((1, (i,), starts[i], [keep, swap(send, "sub", 1)]))
            continue
        stage, ids, low, blocks = waiting.pop(0)
        pops += 1
        wide = blocks[0].shape[1]
        name = "".join(str(i) for i in ids)
        if stage == 1:
            results = level(f"right0_{name}", right0, [blocks], [wide], 2, after)
            axis, shift = "sub", 1
        elif stage == 2:
            parked[ids[0]] = blocks
            ids = merged[ids[0]]
            if any(i not in parked for i in ids):
                continue
            wide = sum(chunks[i] for i in ids)
            low = starts[ids[0]]
            blocks = [parked[i] for i in ids]
            results = level(f"right1_{name}", right1, blocks, [wide], steps[0][1], after)
            axis, shift = "mid", steps[0][0]
        elif stage < 2 + len(steps):
            step = steps[stage - 2]
            held_as = layouts[stage - 3]
            results = [regroup(f"regroup{stage}_{name}", blocks, held_as, step, block, after)[0]]
            axis, shift = "mid", step[0]
        elif stage == 2 + len(steps):
            widths = shares(wide, SPLIT.get(ids, (1,)))
            results = level(f"middle_{name}", middle, [blocks], widths, 2, after)
            axis, shift = "sub", 1
        elif stage == 3 + len(steps):
            results = level(f"left0_{name}", left0, [blocks], [wide], 2, after)
            axis, shift = "sub", 0
        else:
            out = last(f"last{low}", left1, row_basis, *blocks, out, low, columns, after)
            continue
        after = results[0][0]
        for result in results:
            moved = [swap(send, axis, i + 1 << shift) for i, send in enumerate(result[1:])]
            waiting.append((stage + 1, ids, low, result[:1] + moved))
            low += result[0].shape[1]
    return out


def solution(mesh):
    return jax.shard_map(
        local,
        mesh=mesh,
        in_specs=(
            P(("mid", "sub"), None),
            P(("mid", "sub"), None),
            P(("mid", "sub"), None, None, None),
            P(("mid", "sub"), None, None),
            P(("mid", "sub"), None, None, None),
            P(("mid", "sub"), None),
            P(),
        ),
        out_specs=P(("mid", "sub"), None),
        check_vma=False,
    )
```

```python
import jax
import jax.numpy as jnp
from jax import lax
from jax.experimental import pallas as pl
from jax.experimental.pallas import tpu as pltpu
from jax.sharding import PartitionSpec as P

LANES = 128
ENTRY_SHARES = (3, 3, 3)
ENTRY = (0, 0, 1)
MERGED = ((0,), (1,), (2,))
SPLIT = {}
DIRECT = (True, True, True)
TURNS = {}
SPANS = {"right0": 2 * 10**9}
ROWS = 16
SCOPED = 8 * 2**20
MOST = 213 * 2**18
F32 = jnp.float32
BF16 = jnp.bfloat16
WHOLE = pl.BlockSpec(memory_space=pltpu.VMEM)
SCALARS = pl.BlockSpec(memory_space=pltpu.SMEM)
PLACE = pl.BlockSpec(memory_space=pl.ANY)
HBM = pl.BlockSpec(memory_space=pltpu.HBM)


def shares(columns, weights):
    tiles = columns // LANES
    if tiles < len(weights):
        return [columns]
    edges = [round(tiles * sum(weights[:i]) / sum(weights)) * LANES for i in range(len(weights))]
    edges.append(columns)
    return [high - low for low, high in zip(edges[:-1], edges[1:])]


def swap(block, axis, distance):
    count = lax.axis_size(axis)
    return lax.ppermute(block, axis, [(i, i ^ distance) for i in range(count)])


def swapped(matrix, axis, flag):
    half = matrix.shape[axis] // 2
    low = lax.slice_in_dim(matrix, 0, half, axis=axis)
    high = lax.slice_in_dim(matrix, half, 2 * half, axis=axis)
    return jnp.where(flag == 1, jnp.concatenate([high, low], axis=axis), matrix)


def matmul(left, right):
    return lax.dot_general(left, right, (((1,), (0,)), ((), ())), preferred_element_type=F32)


def span(name):
    flops = SPANS.get(name.split("_")[0], 6 * 10**8)
    return pl.CostEstimate(flops=flops, bytes_accessed=0, transcendentals=0)


def call(kernel, name, outs, specs, operands, after, limit=SCOPED, **more):
    extra = [] if after is None else [after]

    def body(*refs):
        kernel(*refs[: len(operands)], *refs[len(operands) + len(extra) :])

    return pl.pallas_call(
        body,
        name=name,
        in_specs=specs + [PLACE] * len(extra),
        out_shape=outs,
        compiler_params=pltpu.CompilerParams(vmem_limit_bytes=limit),
        **more,
    )(*operands, *extra)


def prepare(name, node_order, slots_out, slots_in, right, middle, left, held):
    width = middle.shape[-1]
    groups = node_order.shape[0]
    block = width // groups

    def kernel(node_order, right, middle, left, *refs):
        right0, right1, left0, left1, *rest = refs[len(held) :]
        middles, passed = rest[: len(slots_in)], rest[len(slots_in) :]
        for block_in, block_out in zip(refs[: len(held)], passed):
            block_out[...] = block_in[...]
        place, group = lax.axis_index("sub"), lax.axis_index("mid")
        bit0, bit1 = place & 1, place >> 1 & 1
        right0[...] = swapped(swapped(right[0, 0], 1, bit0), 0, bit1)
        place = lax.broadcasted_iota(jnp.int32, (width, 1), 0)
        source = place % block
        for i, slot in enumerate(slots_out):
            piece = node_order[slot ^ group] * block
            source += jnp.where(place // block == i, piece, 0)
        across = lax.broadcasted_iota(jnp.int32, (width, width), 1)
        pick = jnp.where(across == source, 1.0, 0.0).astype(BF16)
        right1[...] = matmul(pick, swapped(right[0, 1], 1, bit1)).astype(BF16)
        down = lax.broadcasted_iota(jnp.int32, (width, width), 0)
        for slots, out in zip(slots_in, middles):
            place = lax.broadcasted_iota(jnp.int32, (1, width), 1)
            source = place % block
            for i, slot in enumerate(slots):
                source += jnp.where(place // block == i, (slot ^ group) * block, 0)
            pick = jnp.where(down == source, 1.0, 0.0).astype(BF16)
            out[...] = swapped(matmul(middle[0], pick).astype(BF16), 0, bit1)
        left0[...] = swapped(swapped(left[0, 0], 1, bit1), 0, bit0)
        left1[...] = swapped(left[0, 1], 1, bit0)

    return call(
        kernel,
        name,
        [jax.ShapeDtypeStruct((width, width), BF16)] * (4 + len(slots_in))
        + [jax.ShapeDtypeStruct(block.shape, BF16) for block in held],
        [SCALARS] + [WHOLE] * (3 + len(held)),
        [node_order, right, middle, left] + held,
        None,
        out_specs=[WHOLE] * (4 + len(slots_in) + len(held)),
        cost_estimate=span(name),
    )


def row_pieces(rows, pieces):
    return pieces if rows % (pieces * ROWS) == 0 else 1


def opening(name, basis, signal, widths):
    rows, width = basis.shape
    half = width // 2
    pieces = row_pieces(rows, 6)
    depth = rows // pieces
    lows = [sum(widths[:i]) for i in range(len(widths))]

    def kernel(basis, signal, *refs):
        outs, (basis_here, signal_here, arrived, basis_arrived) = refs[:-4], refs[-4:]
        fetch_basis = pltpu.make_async_copy(basis, basis_here, basis_arrived)
        fetch_basis.start()
        copies = []
        for i in range(pieces):
            part = pl.ds(i * depth, depth)
            copies.append(
                pltpu.make_async_copy(signal.at[part], signal_here.at[part], arrived.at[i])
            )
            copies[-1].start()
        fetch_basis.wait()
        flipped = swapped(basis_here[...].T, 0, lax.axis_index("sub") & 1)
        for copy in copies:
            copy.wait()
        for i, (low, wide) in enumerate(zip(lows, widths)):
            total = matmul(flipped, signal_here[:, low : low + wide])
            outs[2 * i][...] = total[:half].astype(BF16)
            outs[2 * i + 1][...] = total[half:].astype(BF16)

    outs = call(
        kernel,
        name,
        [jax.ShapeDtypeStruct((half, wide), BF16) for wide in widths for _ in range(2)],
        [HBM, HBM],
        [basis, signal],
        None,
        limit=MOST,
        out_specs=[WHOLE] * (2 * len(widths)),
        scratch_shapes=[
            pltpu.VMEM((rows, width), BF16),
            pltpu.VMEM(signal.shape, BF16),
            pltpu.SemaphoreType.DMA((pieces,)),
            pltpu.SemaphoreType.DMA,
        ],
        cost_estimate=span(name),
    )
    return list(zip(outs[0::2], outs[1::2]))


def level(name, weight, chunks, widths, count, after):
    width = weight.shape[0]
    depth = width // count
    columns = sum(widths)
    blocks = len(chunks[0])

    def kernel(weight, *refs):
        ins, outs = refs[: blocks * len(chunks)], refs[blocks * len(chunks) :]
        stacked = [
            jnp.concatenate([ref[...] for ref in ins[i * blocks : (i + 1) * blocks]], axis=0)
            for i in range(len(chunks))
        ]
        total = matmul(weight[...], jnp.concatenate(stacked, axis=1))
        low = 0
        for i, wide in enumerate(widths):
            for j in range(count):
                part = total[j * depth : (j + 1) * depth, low : low + wide]
                outs[i * count + j][...] = part.astype(BF16)
            low += wide

    flat = [block for chunk in chunks for block in chunk]
    outs = call(
        kernel,
        name,
        [jax.ShapeDtypeStruct((depth, wide), BF16) for wide in widths for _ in range(count)],
        [WHOLE] * (1 + len(flat)),
        [weight] + flat,
        after,
        out_specs=[WHOLE] * (count * len(widths)),
        cost_estimate=span(name),
    )
    return [list(outs[i * count : (i + 1) * count]) for i in range(len(widths))]


def digits(groups, direct):
    bits = groups.bit_length() - 1
    found, shift = [(0, 2)], 1
    while shift < bits:
        count = 2 if direct and shift + 2 <= bits else 1
        found.append((shift, 1 << count))
        shift += count
    return found


def layouts_of(groups, steps):
    layouts = [by_digit(range(groups), steps[0])]
    for step in steps[1:]:
        layouts.append(by_digit(sum(layouts[-1], []), step))
    return layouts


def values_of(radix):
    return [0] + sorted(range(1, radix), key=lambda value: -value.bit_count())


def by_digit(slots, digit):
    shift, radix = digit
    return [[r for r in slots if r >> shift & radix - 1 == value] for value in values_of(radix)]


def regroup(name, blocks, layout, digit, block, after):
    columns = blocks[0].shape[1]
    place = {r: (i, j) for i, held in enumerate(layout) for j, r in enumerate(held)}
    wanted = by_digit(sum(layout, []), digit)

    def sort(values):
        parts = [[values[place[r][0]][place[r][1] * block :][:block] for r in held] for held in wanted]
        return [jnp.concatenate(part, axis=0) for part in parts]

    if block % ROWS:
        return sort(blocks), wanted

    def kernel(*refs):
        for ref, value in zip(refs[len(blocks) :], sort([ref[...] for ref in refs[: len(blocks)]])):
            ref[...] = value

    outs = call(
        kernel,
        name,
        [jax.ShapeDtypeStruct((len(held) * block, columns), BF16) for held in wanted],
        [WHOLE] * len(blocks),
        blocks,
        after,
        out_specs=[WHOLE] * len(wanted),
        cost_estimate=span(name),
    )
    return list(outs), wanted


def last(name, weight, basis, keep, got, before, low, columns, after):
    rows, width = basis.shape
    wide = keep.shape[1]
    pieces = row_pieces(rows, 6)
    depth = rows // pieces
    given = [] if before is None else [before]

    def kernel(weight, basis, keep, got, *refs):
        out, here, left = refs[len(given) :]
        stacked = jnp.concatenate([keep[...], got[...]], axis=0)
        coeffs = matmul(weight[...], stacked).astype(BF16)
        copies = []
        for i in range(pieces):
            part = pl.ds(i * depth, depth)
            here[part, :] = matmul(basis[part, :], coeffs).astype(BF16)
            copy = pltpu.make_async_copy(here.at[part], out.at[part, pl.ds(low, wide)], left.at[i])
            copy.start()
            copies.append(copy)
        for copy in copies:
            copy.wait()

    return call(
        kernel,
        name,
        jax.ShapeDtypeStruct((rows, columns), BF16),
        [WHOLE] * 4 + [HBM] * len(given),
        [weight, basis, keep, got] + given,
        after,
        out_specs=HBM,
        scratch_shapes=[pltpu.VMEM((rows, wide), BF16), pltpu.SemaphoreType.DMA((pieces,))],
        input_output_aliases={4: 0} if given else {},
        cost_estimate=span(name),
    )


def local(signal, col_basis, right_coupling, middle_coupling, left_coupling, row_basis, node_order):
    groups = lax.axis_size("mid")
    width = col_basis.shape[1]
    block = width // groups
    columns = signal.shape[1]
    chunks = shares(columns, ENTRY_SHARES)
    starts = [sum(chunks[:i]) for i in range(len(chunks))]
    merged = {i: group for group in MERGED for i in group}
    if len(chunks) < len(ENTRY_SHARES):
        merged = {i: (i,) for i in range(len(chunks))}
    plans = {flag: digits(groups, flag) for flag in sorted(set(DIRECT))}
    layouts_by = {flag: layouts_of(groups, plan) for flag, plan in plans.items()}

    opened = opening("opening", col_basis, signal, chunks)
    right0, right1, left0, left1, *rest = prepare(
        "prepare",
        node_order,
        sum(by_digit(range(groups), (0, 2)), []),
        [sum(layouts[-1], []) for layouts in layouts_by.values()],
        right_coupling,
        middle_coupling,
        left_coupling,
        [send for _, send in opened[1:]],
    )
    middles = dict(zip(layouts_by, rest))
    sends = rest[len(middles) :]
    opened = opened[:1] + [(keep, send) for (keep, _), send in zip(opened[1:], sends)]
    out, after = None, right0
    waiting, pops, entered = [], 0, 0
    parked = {}
    while waiting or entered < len(chunks):
        if entered < len(chunks) and (pops >= ENTRY[entered] or not waiting):
            i, entered = entered, entered + 1
            keep, send = opened[i]
            waiting.append((1, (i,), starts[i], [keep, swap(send, "sub", 1)]))
            continue
        turn = TURNS.get(pops, 0)
        stage, ids, low, blocks = waiting.pop(turn if turn < len(waiting) else 0)
        pops += 1
        flag = DIRECT[ids[0]]
        steps, layouts, middle = plans[flag], layouts_by[flag], middles[flag]
        wide = blocks[0].shape[1]
        name = "".join(str(i) for i in ids)
        if stage == 1:
            results = level(f"right0_{name}", right0, [blocks], [wide], 2, after)
            axis, shift, radix = "sub", 1, 2
        elif stage == 2:
            parked[ids[0]] = blocks
            ids = merged[ids[0]]
            if any(i not in parked for i in ids):
                continue
            wide = sum(chunks[i] for i in ids)
            low = starts[ids[0]]
            blocks = [parked[i] for i in ids]
            results = level(f"right1_{name}", right1, blocks, [wide], steps[0][1], after)
            axis, shift, radix = "mid", *steps[0]
        elif stage < 2 + len(steps):
            step = steps[stage - 2]
            held_as = layouts[stage - 3]
            results = [regroup(f"regroup{stage}_{name}", blocks, held_as, step, block, after)[0]]
            axis, shift, radix = "mid", *step
        elif stage == 2 + len(steps):
            widths = shares(wide, SPLIT.get(ids, (1,)))
            results = level(f"middle_{name}", middle, [blocks], widths, 2, after)
            axis, shift, radix = "sub", 1, 2
        elif stage == 3 + len(steps):
            results = level(f"left0_{name}", left0, [blocks], [wide], 2, after)
            axis, shift, radix = "sub", 0, 2
        else:
            out = last(f"last{low}", left1, row_basis, *blocks, out, low, columns, after)
            continue
        after = results[0][0]
        for result in results:
            routes = [value << shift for value in values_of(radix)[1:]]
            moved = [swap(send, axis, route) for send, route in zip(result[1:], routes)]
            waiting.append((stage + 1, ids, low, result[:1] + moved))
            low += result[0].shape[1]
    return out


def solution(mesh):
    return jax.shard_map(
        local,
        mesh=mesh,
        in_specs=(
            P(("mid", "sub"), None),
            P(("mid", "sub"), None),
            P(("mid", "sub"), None, None, None),
            P(("mid", "sub"), None, None),
            P(("mid", "sub"), None, None, None),
            P(("mid", "sub"), None),
            P(),
        ),
        out_specs=P(("mid", "sub"), None),
        check_vma=False,
    )
```

```python
import jax
import jax.numpy as jnp
from jax import lax
from jax.experimental import pallas as pl
from jax.experimental.pallas import tpu as pltpu
from jax.sharding import PartitionSpec as P

LANES = 128
SHARES = (3, 3, 3)
HEADS = ((0,), (1,), (2,))
TAILS = ((0,), (1,), (2,))
ENTRY = (0, 0, 1)
TURNS = {}
SPANS = {}
ROWS = 16
SCOPED = 8 * 2**20
MOST = 213 * 2**18
F32 = jnp.float32
BF16 = jnp.bfloat16
WHOLE = pl.BlockSpec(memory_space=pltpu.VMEM)
SCALARS = pl.BlockSpec(memory_space=pltpu.SMEM)
PLACE = pl.BlockSpec(memory_space=pl.ANY)
HBM = pl.BlockSpec(memory_space=pltpu.HBM)


def shares(columns, weights):
    tiles = columns // LANES
    if tiles < len(weights):
        return [columns]
    edges = [round(tiles * sum(weights[:i]) / sum(weights)) * LANES for i in range(len(weights))]
    edges.append(columns)
    return [high - low for low, high in zip(edges[:-1], edges[1:])]


def swap(block, axis, distances):
    count = lax.axis_size(axis)
    return lax.ppermute(block, axis, [(i, i ^ distances[i & 1]) for i in range(count)])


def swapped(matrix, axis, flag):
    half = matrix.shape[axis] // 2
    low = lax.slice_in_dim(matrix, 0, half, axis=axis)
    high = lax.slice_in_dim(matrix, half, 2 * half, axis=axis)
    return jnp.where(flag == 1, jnp.concatenate([high, low], axis=axis), matrix)


def matmul(left, right):
    return lax.dot_general(left, right, (((1,), (0,)), ((), ())), preferred_element_type=F32)


def span(name):
    flops = SPANS.get(name.split("_")[0], 0)
    return pl.CostEstimate(flops=flops, bytes_accessed=0, transcendentals=0)


def call(kernel, name, outs, specs, operands, after, limit=SCOPED, **more):
    extra = [] if after is None else [after]

    def body(*refs):
        kernel(*refs[: len(operands)], *refs[len(operands) + len(extra) :])

    return pl.pallas_call(
        body,
        name=name,
        in_specs=specs + [PLACE] * len(extra),
        out_shape=outs,
        compiler_params=pltpu.CompilerParams(vmem_limit_bytes=limit),
        **more,
    )(*operands, *extra)


def prepare(name, node_order, places_out, places_in, right, middle, left, held):
    width = middle.shape[-1]
    groups = node_order.shape[0]
    block = width // groups

    orders = bit_orders(groups)

    def slot(place, core):
        return jnp.where(core == 1, slot_number(place, orders[1]), slot_number(place, orders[0]))

    def kernel(node_order, right, middle, left, *refs):
        right0, right1, middle0, left0, left1, *passed = refs[len(held) :]
        for block_in, block_out in zip(refs[: len(held)], passed):
            block_out[...] = block_in[...]
        place, group = lax.axis_index("sub"), lax.axis_index("mid")
        bit0, bit1 = place & 1, place >> 1 & 1
        right0[...] = swapped(swapped(right[0, 0], 1, bit0), 0, bit1)
        place = lax.broadcasted_iota(jnp.int32, (width, 1), 0)
        source = place % block
        for i, p in enumerate(places_out):
            piece = node_order[slot(p, group & 1 ^ p & 1) ^ group] * block
            source += jnp.where(place // block == i, piece, 0)
        across = lax.broadcasted_iota(jnp.int32, (width, width), 1)
        pick = jnp.where(across == source, 1.0, 0.0).astype(BF16)
        right1[...] = matmul(pick, swapped(right[0, 1], 1, bit1)).astype(BF16)
        place = lax.broadcasted_iota(jnp.int32, (1, width), 1)
        source = place % block
        for i, p in enumerate(places_in):
            piece = (slot(p, group & 1) ^ group) * block
            source += jnp.where(place // block == i, piece, 0)
        down = lax.broadcasted_iota(jnp.int32, (width, width), 0)
        pick = jnp.where(down == source, 1.0, 0.0).astype(BF16)
        middle0[...] = swapped(matmul(middle[0], pick).astype(BF16), 0, bit1)
        left0[...] = swapped(swapped(left[0, 0], 1, bit1), 0, bit0)
        left1[...] = swapped(left[0, 1], 1, bit0)

    return call(
        kernel,
        name,
        [jax.ShapeDtypeStruct((width, width), BF16)] * 5
        + [jax.ShapeDtypeStruct(block.shape, BF16) for block in held],
        [SCALARS] + [WHOLE] * (3 + len(held)),
        [node_order, right, middle, left] + held,
        None,
        out_specs=[WHOLE] * (5 + len(held)),
        cost_estimate=span(name),
    )


def row_pieces(rows, pieces):
    return pieces if rows % (pieces * ROWS) == 0 else 1


def opening(name, basis, signal, widths, groups):
    rows, width = basis.shape
    half = width // 2
    pieces = row_pieces(rows, 6)
    depth = rows // pieces
    lows = [sum(widths[:i]) for i in range(len(widths))]
    all_widths = widths + [sum(widths[i] for i in group) for group in groups]

    def kernel(basis, signal, *refs):
        outs, (basis_here, signal_here, arrived, basis_arrived) = refs[:-4], refs[-4:]
        fetch_basis = pltpu.make_async_copy(basis, basis_here, basis_arrived)
        fetch_basis.start()
        copies = []
        for i in range(pieces):
            part = pl.ds(i * depth, depth)
            copies.append(
                pltpu.make_async_copy(signal.at[part], signal_here.at[part], arrived.at[i])
            )
            copies[-1].start()
        fetch_basis.wait()
        flipped = swapped(basis_here[...].T, 0, lax.axis_index("sub") & 1)
        for copy in copies:
            copy.wait()
        for group, send in zip(groups, outs[len(widths) :]):
            for i in group:
                low, wide = lows[i], widths[i]
                total = matmul(flipped, signal_here[:, low : low + wide])
                outs[i][...] = total[:half].astype(BF16)
                place = low - lows[group[0]]
                send[:, place : place + wide] = total[half:].astype(BF16)

    outs = call(
        kernel,
        name,
        [jax.ShapeDtypeStruct((half, wide), BF16) for wide in all_widths],
        [HBM, HBM],
        [basis, signal],
        None,
        limit=MOST,
        out_specs=[WHOLE] * len(all_widths),
        scratch_shapes=[
            pltpu.VMEM((rows, width), BF16),
            pltpu.VMEM(signal.shape, BF16),
            pltpu.SemaphoreType.DMA((pieces,)),
            pltpu.SemaphoreType.DMA,
        ],
        cost_estimate=span(name),
    )
    return outs[: len(widths)], outs[len(widths) :]


def level(name, weight, blocks, low, wide, count, before, after):
    width = weight.shape[0]
    depth = width // count
    ahead = sum(block.shape[1] for block in before)

    def kernel(weight, *refs):
        ins, outs = refs[: len(blocks)], refs[len(blocks) + len(before) :]
        here = [slice(low, low + wide) if ref.shape[1] > wide else slice(None) for ref in ins]
        stacked = jnp.concatenate([ref[:, part] for ref, part in zip(ins, here)], axis=0)
        total = matmul(weight[...], stacked)
        for i, out in enumerate(outs):
            value = total[i * depth : (i + 1) * depth].astype(BF16)
            if before and i == count - 1:
                out[:, :ahead] = refs[len(blocks)][...]
                out[:, ahead:] = value
            else:
                out[...] = value

    widths = [wide] * (count - 1) + [ahead + wide]
    return call(
        kernel,
        name,
        [jax.ShapeDtypeStruct((depth, columns), BF16) for columns in widths],
        [WHOLE] * (1 + len(blocks) + len(before)),
        [weight] + blocks + before,
        after,
        out_specs=[WHOLE] * count,
        cost_estimate=span(name),
    )


def bit_orders(groups):
    bits = list(range(1, groups.bit_length() - 1))
    return [bits[::-1], bits]


def slot_number(place, order):
    return place & 1 | sum((place >> 1 + t & 1) << bit for t, bit in enumerate(order))


def by_bit(places, bit):
    return [[p for p in places if p >> bit & 1 == value] for value in range(2)]


def layouts_of(groups):
    layouts = [by_bit(range(groups), 0)]
    for bit in range(1, groups.bit_length() - 1):
        layouts.append(by_bit(sum(layouts[-1], []), bit))
    return layouts


def regroup(name, blocks, layout, bit, block, after):
    columns = blocks[0].shape[1]
    place = {r: (i, j) for i, held in enumerate(layout) for j, r in enumerate(held)}
    wanted = by_bit(sum(layout, []), bit)

    def sort(values):
        parts = [[values[place[r][0]][place[r][1] * block :][:block] for r in held] for held in wanted]
        return [jnp.concatenate(part, axis=0) for part in parts]

    if block % ROWS:
        return sort(blocks), wanted

    def kernel(*refs):
        for ref, value in zip(refs[len(blocks) :], sort([ref[...] for ref in refs[: len(blocks)]])):
            ref[...] = value

    outs = call(
        kernel,
        name,
        [jax.ShapeDtypeStruct((len(held) * block, columns), BF16) for held in wanted],
        [WHOLE] * len(blocks),
        blocks,
        after,
        out_specs=[WHOLE] * len(wanted),
        cost_estimate=span(name),
    )
    return list(outs), wanted


def last(name, weight, basis, keeps, got, before, low, columns, after):
    rows, width = basis.shape
    wide = got.shape[1]
    pieces = row_pieces(rows, 6)
    depth = rows // pieces
    given = [] if before is None else [before]

    def kernel(weight, basis, got, *refs):
        out, here, left = refs[len(keeps) + len(given) :]
        keep = jnp.concatenate([ref[...] for ref in refs[: len(keeps)]], axis=1)
        stacked = jnp.concatenate([keep, got[...]], axis=0)
        coeffs = matmul(weight[...], stacked).astype(BF16)
        copies = []
        for i in range(pieces):
            part = pl.ds(i * depth, depth)
            here[part, :] = matmul(basis[part, :], coeffs).astype(BF16)
            copy = pltpu.make_async_copy(here.at[part], out.at[part, pl.ds(low, wide)], left.at[i])
            copy.start()
            copies.append(copy)
        for copy in copies:
            copy.wait()

    return call(
        kernel,
        name,
        jax.ShapeDtypeStruct((rows, columns), BF16),
        [WHOLE] * (3 + len(keeps)) + [HBM] * len(given),
        [weight, basis, got] + keeps + given,
        after,
        out_specs=HBM,
        scratch_shapes=[pltpu.VMEM((rows, wide), BF16), pltpu.SemaphoreType.DMA((pieces,))],
        input_output_aliases={3 + len(keeps): 0} if given else {},
        cost_estimate=span(name),
    )


def local(signal, col_basis, right_coupling, middle_coupling, left_coupling, row_basis, node_order):
    groups = lax.axis_size("mid")
    width = col_basis.shape[1]
    block = width // groups
    columns = signal.shape[1]
    chunks = shares(columns, SHARES)
    lows = [sum(chunks[:i]) for i in range(len(chunks))]
    whole = len(chunks) == len(SHARES)
    heads = HEADS if whole else ((0,),)
    tails = TAILS if whole else ((0,),)
    layouts = layouts_of(groups)
    routes = [(1, 1)] + [(1 << one, 1 << other) for one, other in zip(*bit_orders(groups))]

    keeps, sends = opening("opening", col_basis, signal, chunks, heads)
    right0, right1, middle, left0, left1, *later = prepare(
        "prepare",
        node_order,
        sum(layouts[0], []),
        sum(layouts[-1], []),
        right_coupling,
        middle_coupling,
        left_coupling,
        list(sends[1:]),
    )
    gots = {}
    for group, send in zip(heads, [sends[0]] + later):
        got = swap(send, "sub", (1, 1))
        for i in group:
            gots[i] = (got, lows[i] - lows[group[0]])

    out, after = None, right0
    waiting, pops, entered = [], 0, 0
    parked = {}
    while waiting or entered < len(chunks):
        if entered < len(chunks) and (pops >= ENTRY[entered] or not waiting):
            waiting.append((1, entered, [keeps[entered], gots[entered][0]]))
            entered += 1
            continue
        turn = TURNS.get(pops, 0)
        stage, i, blocks = waiting.pop(turn if turn < len(waiting) else 0)
        pops += 1
        wide = chunks[i]
        if stage == 1:
            results = level(f"right0_{i}", right0, blocks, gots[i][1], wide, 2, [], after)
            axis, route = "sub", (2, 2)
        elif stage == 2:
            results = level(f"right1_{i}", right1, blocks, 0, wide, 2, [], after)
            axis, route = "mid", routes[0]
        elif stage < 2 + len(routes):
            name = f"regroup{stage}_{i}"
            results, _ = regroup(name, blocks, layouts[stage - 3], stage - 2, block, after)
            axis, route = "mid", routes[stage - 2]
        elif stage == 2 + len(routes):
            results = level(f"middle_{i}", middle, blocks, 0, wide, 2, [], after)
            axis, route = "sub", (2, 2)
        elif stage == 3 + len(routes):
            group = next(group for group in tails if i in group)
            before = [parked[group[0]][-1]] if i != group[0] else []
            results = level(f"left0_{i}", left0, blocks, 0, wide, 2, before, after)
            parked[group[0]] = parked.get(group[0], [])[:-1] + list(results)
            if i != group[-1]:
                after = results[0]
                continue
            results = parked[group[0]]
            got = swap(results[-1], "sub", (1, 1))
            waiting.append((stage + 1, group[0], [results[:-1], got]))
            after = results[-2]
            continue
        else:
            name = f"last_{i}"
            out = last(name, left1, row_basis, *blocks, out, lows[i], columns, after)
            continue
        after = results[0]
        waiting.append((stage + 1, i, [results[0], swap(results[1], axis, route)]))
    return out


def solution(mesh):
    return jax.shard_map(
        local,
        mesh=mesh,
        in_specs=(
            P(("mid", "sub"), None),
            P(("mid", "sub"), None),
            P(("mid", "sub"), None, None, None),
            P(("mid", "sub"), None, None),
            P(("mid", "sub"), None, None, None),
            P(("mid", "sub"), None),
            P(),
        ),
        out_specs=P(("mid", "sub"), None),
        check_vma=False,
    )
```

```python
import jax
import jax.numpy as jnp
from jax import lax
from jax.experimental import pallas as pl
from jax.experimental.pallas import tpu as pltpu
from jax.sharding import PartitionSpec as P

LANES = 128
SHARES = (3, 3, 3)
HEADS = ((0,), (1,), (2,))
ENTRY = (0, 0, 1)
WAITS = {1: 0}
TURNS = {6: 1}
SPANS = {}
ROWS = 16
SCOPED = 8 * 2**20
MOST = 213 * 2**18
F32 = jnp.float32
BF16 = jnp.bfloat16
WHOLE = pl.BlockSpec(memory_space=pltpu.VMEM)
SCALARS = pl.BlockSpec(memory_space=pltpu.SMEM)
PLACE = pl.BlockSpec(memory_space=pl.ANY)
HBM = pl.BlockSpec(memory_space=pltpu.HBM)


def shares(columns, weights):
    tiles = columns // LANES
    if tiles < len(weights):
        return [columns]
    edges = [round(tiles * sum(weights[:i]) / sum(weights)) * LANES for i in range(len(weights))]
    edges.append(columns)
    return [high - low for low, high in zip(edges[:-1], edges[1:])]


def swap(block, axis, distance):
    count = lax.axis_size(axis)
    return lax.ppermute(block, axis, [(i, i ^ distance) for i in range(count)])


def swapped(matrix, axis, flag):
    half = matrix.shape[axis] // 2
    low = lax.slice_in_dim(matrix, 0, half, axis=axis)
    high = lax.slice_in_dim(matrix, half, 2 * half, axis=axis)
    return jnp.where(flag == 1, jnp.concatenate([high, low], axis=axis), matrix)


def matmul(left, right):
    return lax.dot_general(left, right, (((1,), (0,)), ((), ())), preferred_element_type=F32)


def span(name):
    flops = SPANS.get(name.split("_")[0], 0)
    return pl.CostEstimate(flops=flops, bytes_accessed=0, transcendentals=0)


def call(kernel, name, outs, specs, operands, after, limit=SCOPED, **more):
    extra = [] if after is None else [after]

    def body(*refs):
        kernel(*refs[: len(operands)], *refs[len(operands) + len(extra) :])

    return pl.pallas_call(
        body,
        name=name,
        in_specs=specs + [PLACE] * len(extra),
        out_shape=outs,
        compiler_params=pltpu.CompilerParams(vmem_limit_bytes=limit),
        **more,
    )(*operands, *extra)


def prepare(name, node_order, slots_out, slots_in, right, middle, left, held):
    width = middle.shape[-1]
    groups = node_order.shape[0]
    block = width // groups

    def kernel(node_order, right, middle, left, *refs):
        right0, right1, middle0, left0, left1, *passed = refs[len(held) :]
        for block_in, block_out in zip(refs[: len(held)], passed):
            block_out[...] = block_in[...]
        place, group = lax.axis_index("sub"), lax.axis_index("mid")
        bit0, bit1 = place & 1, place >> 1 & 1
        right0[...] = swapped(swapped(right[0, 0], 1, bit0), 0, bit1)
        place = lax.broadcasted_iota(jnp.int32, (width, 1), 0)
        source = place % block
        for i, slot in enumerate(slots_out):
            piece = node_order[slot ^ group] * block
            source += jnp.where(place // block == i, piece, 0)
        across = lax.broadcasted_iota(jnp.int32, (width, width), 1)
        pick = jnp.where(across == source, 1.0, 0.0).astype(BF16)
        right1[...] = matmul(pick, swapped(right[0, 1], 1, bit1)).astype(BF16)
        place = lax.broadcasted_iota(jnp.int32, (1, width), 1)
        source = place % block
        for i, slot in enumerate(slots_in):
            source += jnp.where(place // block == i, (slot ^ group) * block, 0)
        down = lax.broadcasted_iota(jnp.int32, (width, width), 0)
        pick = jnp.where(down == source, 1.0, 0.0).astype(BF16)
        middle0[...] = swapped(matmul(middle[0], pick).astype(BF16), 0, bit1)
        left0[...] = swapped(swapped(left[0, 0], 1, bit1), 0, bit0)
        left1[...] = swapped(left[0, 1], 1, bit0)

    return call(
        kernel,
        name,
        [jax.ShapeDtypeStruct((width, width), BF16)] * 5
        + [jax.ShapeDtypeStruct(block.shape, BF16) for block in held],
        [SCALARS] + [WHOLE] * (3 + len(held)),
        [node_order, right, middle, left] + held,
        None,
        out_specs=[WHOLE] * (5 + len(held)),
        cost_estimate=span(name),
    )


def row_pieces(rows, pieces):
    return pieces if rows % (pieces * ROWS) == 0 else 1


def opening(name, basis, signal, widths, groups):
    rows, width = basis.shape
    half = width // 2
    pieces = row_pieces(rows, 6)
    depth = rows // pieces
    lows = [sum(widths[:i]) for i in range(len(widths))]
    all_widths = widths + [sum(widths[i] for i in group) for group in groups]

    def kernel(basis, signal, *refs):
        outs, (basis_here, signal_here, arrived, basis_arrived) = refs[:-4], refs[-4:]
        fetch_basis = pltpu.make_async_copy(basis, basis_here, basis_arrived)
        fetch_basis.start()
        copies = []
        for i in range(pieces):
            part = pl.ds(i * depth, depth)
            copies.append(
                pltpu.make_async_copy(signal.at[part], signal_here.at[part], arrived.at[i])
            )
            copies[-1].start()
        fetch_basis.wait()
        flipped = swapped(basis_here[...].T, 0, lax.axis_index("sub") & 1)
        for copy in copies:
            copy.wait()
        for group, send in zip(groups, outs[len(widths) :]):
            for i in group:
                low, wide = lows[i], widths[i]
                total = matmul(flipped, signal_here[:, low : low + wide])
                outs[i][...] = total[:half].astype(BF16)
                place = low - lows[group[0]]
                send[:, place : place + wide] = total[half:].astype(BF16)

    outs = call(
        kernel,
        name,
        [jax.ShapeDtypeStruct((half, wide), BF16) for wide in all_widths],
        [HBM, HBM],
        [basis, signal],
        None,
        limit=MOST,
        out_specs=[WHOLE] * len(all_widths),
        scratch_shapes=[
            pltpu.VMEM((rows, width), BF16),
            pltpu.VMEM(signal.shape, BF16),
            pltpu.SemaphoreType.DMA((pieces,)),
            pltpu.SemaphoreType.DMA,
        ],
        cost_estimate=span(name),
    )
    return outs[: len(widths)], outs[len(widths) :]


def level(name, weight, blocks, low, wide, count, held, after):
    width = weight.shape[0]
    depth = width // count
    given = len(blocks) + len(held)

    def kernel(weight, *refs):
        ins, outs = refs[: len(blocks)], refs[given:]
        here = [slice(low, low + wide) if ref.shape[1] > wide else slice(None) for ref in ins]
        stacked = jnp.concatenate([ref[:, part] for ref, part in zip(ins, here)], axis=0)
        total = matmul(weight[...], stacked)
        for i, out in enumerate(outs[:count]):
            out[...] = total[i * depth : (i + 1) * depth].astype(BF16)
        for ref, out in zip(refs[len(blocks) : given], outs[count:]):
            out[...] = ref[...]

    shapes = [(depth, wide)] * count + [block.shape for block in held]
    return call(
        kernel,
        name,
        [jax.ShapeDtypeStruct(shape, BF16) for shape in shapes],
        [WHOLE] * (1 + given),
        [weight] + blocks + held,
        after,
        out_specs=[WHOLE] * len(shapes),
        cost_estimate=span(name),
    )


def digits(groups):
    bits = groups.bit_length() - 1
    found, shift = [(0, 2)], 1
    while shift < bits:
        count = 2 if shift + 2 <= bits else 1
        found.append((shift, 1 << count))
        shift += count
    return found


def layouts_of(groups, steps):
    layouts = [by_digit(range(groups), steps[0])]
    for step in steps[1:]:
        layouts.append(by_digit(sum(layouts[-1], []), step))
    return layouts


def values_of(radix):
    return [0] + sorted(range(1, radix), key=lambda value: -value.bit_count())


def by_digit(slots, digit):
    shift, radix = digit
    return [[r for r in slots if r >> shift & radix - 1 == value] for value in values_of(radix)]


def regroup(name, blocks, layout, digit, block, after):
    columns = blocks[0].shape[1]
    place = {r: (i, j) for i, held in enumerate(layout) for j, r in enumerate(held)}
    wanted = by_digit(sum(layout, []), digit)

    def sort(values):
        parts = [[values[place[r][0]][place[r][1] * block :][:block] for r in held] for held in wanted]
        return [jnp.concatenate(part, axis=0) for part in parts]

    if block % ROWS:
        return sort(blocks), wanted

    def kernel(*refs):
        for ref, value in zip(refs[len(blocks) :], sort([ref[...] for ref in refs[: len(blocks)]])):
            ref[...] = value

    outs = call(
        kernel,
        name,
        [jax.ShapeDtypeStruct((len(held) * block, columns), BF16) for held in wanted],
        [WHOLE] * len(blocks),
        blocks,
        after,
        out_specs=[WHOLE] * len(wanted),
        cost_estimate=span(name),
    )
    return list(outs), wanted


def last(name, weight, basis, keeps, got, before, low, columns, after):
    rows, width = basis.shape
    wide = got.shape[1]
    pieces = row_pieces(rows, 6)
    depth = rows // pieces
    given = [] if before is None else [before]

    def kernel(weight, basis, got, *refs):
        out, here, left = refs[len(keeps) + len(given) :]
        keep = jnp.concatenate([ref[...] for ref in refs[: len(keeps)]], axis=1)
        stacked = jnp.concatenate([keep, got[...]], axis=0)
        coeffs = matmul(weight[...], stacked).astype(BF16)
        copies = []
        for i in range(pieces):
            part = pl.ds(i * depth, depth)
            here[part, :] = matmul(basis[part, :], coeffs).astype(BF16)
            copy = pltpu.make_async_copy(here.at[part], out.at[part, pl.ds(low, wide)], left.at[i])
            copy.start()
            copies.append(copy)
        for copy in copies:
            copy.wait()

    return call(
        kernel,
        name,
        jax.ShapeDtypeStruct((rows, columns), BF16),
        [WHOLE] * (3 + len(keeps)) + [HBM] * len(given),
        [weight, basis, got] + keeps + given,
        after,
        out_specs=HBM,
        scratch_shapes=[pltpu.VMEM((rows, wide), BF16), pltpu.SemaphoreType.DMA((pieces,))],
        input_output_aliases={3 + len(keeps): 0} if given else {},
        cost_estimate=span(name),
    )


def local(signal, col_basis, right_coupling, middle_coupling, left_coupling, row_basis, node_order):
    groups = lax.axis_size("mid")
    width = col_basis.shape[1]
    block = width // groups
    columns = signal.shape[1]
    chunks = shares(columns, SHARES)
    lows = [sum(chunks[:i]) for i in range(len(chunks))]
    whole = len(chunks) == len(SHARES)
    heads = HEADS if whole else ((0,),)
    steps = digits(groups)
    layouts = layouts_of(groups, steps)

    keeps, sends = opening("opening", col_basis, signal, chunks, heads)
    right0, right1, middle, left0, left1, *later = prepare(
        "prepare",
        node_order,
        sum(layouts[0], []),
        sum(layouts[-1], []),
        right_coupling,
        middle_coupling,
        left_coupling,
        list(sends[1:]),
    )
    gots = {}
    for group, send in zip(heads, [sends[0]] + later):
        got = swap(send, "sub", 1)
        for i in group:
            gots[i] = (got, lows[i] - lows[group[0]])

    out, after = None, right0
    waiting, pops, entered = [], 0, 0
    held = []
    while waiting or entered < len(chunks):
        if entered < len(chunks) and (pops >= ENTRY[entered] or not waiting):
            waiting.append((1, entered, [keeps[entered], gots[entered][0]]))
            entered += 1
            continue
        turn = TURNS.get(pops, 0)
        stage, i, blocks = waiting.pop(turn if turn < len(waiting) else 0)
        pops += 1
        wide = chunks[i]
        released = []
        if stage == 1:
            results = level(f"right0_{i}", right0, blocks, gots[i][1], wide, 2, [], after)
            axis, shift, radix = "sub", 1, 2
            if i in WAITS and whole:
                held.append((i, results))
                after = results[0]
                continue
        elif stage == 2:
            count = steps[0][1]
            free = [(j, kept) for j, kept in held if WAITS[j] == i]
            sends = [kept[1] for _, kept in free]
            results = level(f"right1_{i}", right1, blocks, 0, wide, count, sends, after)
            axis, shift, radix = "mid", *steps[0]
            for (j, kept), send in zip(free, results[count:]):
                released.append((2, j, [kept[0], swap(send, "sub", 2)]))
            results = results[:count]
        elif stage < 2 + len(steps):
            step = steps[stage - 2]
            results, _ = regroup(
                f"regroup{stage}_{i}", blocks, layouts[stage - 3], step, block, after
            )
            axis, shift, radix = "mid", *step
        elif stage == 2 + len(steps):
            results = level(f"middle_{i}", middle, blocks, 0, wide, 2, [], after)
            axis, shift, radix = "sub", 1, 2
        elif stage == 3 + len(steps):
            results = level(f"left0_{i}", left0, blocks, 0, wide, 2, [], after)
            axis, shift, radix = "sub", 0, 2
        else:
            name = f"last_{i}"
            out = last(name, left1, row_basis, blocks[:1], blocks[1], out, lows[i], columns, after)
            continue
        after = results[0]
        routes = [value << shift for value in values_of(radix)[1:]]
        moved = [swap(send, axis, route) for send, route in zip(results[1:], routes)]
        waiting.append((stage + 1, i, [results[0]] + moved))
        waiting += released
    return out


def solution(mesh):
    return jax.shard_map(
        local,
        mesh=mesh,
        in_specs=(
            P(("mid", "sub"), None),
            P(("mid", "sub"), None),
            P(("mid", "sub"), None, None, None),
            P(("mid", "sub"), None, None),
            P(("mid", "sub"), None, None, None),
            P(("mid", "sub"), None),
            P(),
        ),
        out_specs=P(("mid", "sub"), None),
        check_vma=False,
    )
```

```python
import jax
import jax.numpy as jnp
from jax import lax
from jax.experimental import pallas as pl
from jax.experimental.pallas import tpu as pltpu
from jax.sharding import PartitionSpec as P

LANES = 128
SHARES = (3, 3, 3)
HEADS = ((0,), (1,), (2,))
ENTRY = (0, 0, 1)
WAITS = {1: 0}
TURNS = {6: 1, 7: 1, 9: 1}
SPANS = {}
ROWS = 16
SCOPED = 8 * 2**20
MOST = 213 * 2**18
F32 = jnp.float32
BF16 = jnp.bfloat16
WHOLE = pl.BlockSpec(memory_space=pltpu.VMEM)
SCALARS = pl.BlockSpec(memory_space=pltpu.SMEM)
PLACE = pl.BlockSpec(memory_space=pl.ANY)
HBM = pl.BlockSpec(memory_space=pltpu.HBM)


def shares(columns, weights):
    tiles = columns // LANES
    if tiles < len(weights):
        return [columns]
    edges = [round(tiles * sum(weights[:i]) / sum(weights)) * LANES for i in range(len(weights))]
    edges.append(columns)
    return [high - low for low, high in zip(edges[:-1], edges[1:])]


def swap(block, axis, distance):
    count = lax.axis_size(axis)
    return lax.ppermute(block, axis, [(i, i ^ distance) for i in range(count)])


def swapped(matrix, axis, flag):
    half = matrix.shape[axis] // 2
    low = lax.slice_in_dim(matrix, 0, half, axis=axis)
    high = lax.slice_in_dim(matrix, half, 2 * half, axis=axis)
    return jnp.where(flag == 1, jnp.concatenate([high, low], axis=axis), matrix)


def matmul(left, right):
    return lax.dot_general(left, right, (((1,), (0,)), ((), ())), preferred_element_type=F32)


def span(name):
    flops = SPANS.get(name.split("_")[0], 6 * 10**8)
    return pl.CostEstimate(flops=flops, bytes_accessed=0, transcendentals=0)


def call(kernel, name, outs, specs, operands, after, limit=SCOPED, **more):
    extra = [] if after is None else [after]

    def body(*refs):
        kernel(*refs[: len(operands)], *refs[len(operands) + len(extra) :])

    return pl.pallas_call(
        body,
        name=name,
        in_specs=specs + [PLACE] * len(extra),
        out_shape=outs,
        compiler_params=pltpu.CompilerParams(vmem_limit_bytes=limit),
        **more,
    )(*operands, *extra)


def prepare(name, node_order, slots_out, slots_in, right, middle, left, held):
    width = middle.shape[-1]
    groups = node_order.shape[0]
    block = width // groups

    def kernel(node_order, right, middle, left, *refs):
        right0, right1, middle0, left0, left1, *passed = refs[len(held) :]
        for block_in, block_out in zip(refs[: len(held)], passed):
            block_out[...] = block_in[...]
        place, group = lax.axis_index("sub"), lax.axis_index("mid")
        bit0, bit1 = place & 1, place >> 1 & 1
        right0[...] = swapped(swapped(right[0, 0], 1, bit0), 0, bit1)
        place = lax.broadcasted_iota(jnp.int32, (width, 1), 0)
        source = place % block
        for i, slot in enumerate(slots_out):
            piece = node_order[slot ^ group] * block
            source += jnp.where(place // block == i, piece, 0)
        across = lax.broadcasted_iota(jnp.int32, (width, width), 1)
        pick = jnp.where(across == source, 1.0, 0.0).astype(BF16)
        right1[...] = matmul(pick, swapped(right[0, 1], 1, bit1)).astype(BF16)
        place = lax.broadcasted_iota(jnp.int32, (1, width), 1)
        source = place % block
        for i, slot in enumerate(slots_in):
            source += jnp.where(place // block == i, (slot ^ group) * block, 0)
        down = lax.broadcasted_iota(jnp.int32, (width, width), 0)
        pick = jnp.where(down == source, 1.0, 0.0).astype(BF16)
        middle0[...] = swapped(matmul(middle[0], pick).astype(BF16), 0, bit1)
        left0[...] = swapped(swapped(left[0, 0], 1, bit1), 0, bit0)
        left1[...] = swapped(left[0, 1], 1, bit0)

    return call(
        kernel,
        name,
        [jax.ShapeDtypeStruct((width, width), BF16)] * 5
        + [jax.ShapeDtypeStruct(block.shape, BF16) for block in held],
        [SCALARS] + [WHOLE] * (3 + len(held)),
        [node_order, right, middle, left] + held,
        None,
        out_specs=[WHOLE] * (5 + len(held)),
        cost_estimate=span(name),
    )


def row_pieces(rows, pieces):
    return pieces if rows % (pieces * ROWS) == 0 else 1


def opening(name, basis, signal, widths, groups):
    rows, width = basis.shape
    half = width // 2
    pieces = row_pieces(rows, 6)
    depth = rows // pieces
    lows = [sum(widths[:i]) for i in range(len(widths))]
    all_widths = widths + [sum(widths[i] for i in group) for group in groups]

    def kernel(basis, signal, *refs):
        outs, (basis_here, signal_here, arrived, basis_arrived) = refs[:-4], refs[-4:]
        fetch_basis = pltpu.make_async_copy(basis, basis_here, basis_arrived)
        fetch_basis.start()
        copies = []
        for i in range(pieces):
            part = pl.ds(i * depth, depth)
            copies.append(
                pltpu.make_async_copy(signal.at[part], signal_here.at[part], arrived.at[i])
            )
            copies[-1].start()
        fetch_basis.wait()
        flipped = swapped(basis_here[...].T, 0, lax.axis_index("sub") & 1)
        for copy in copies:
            copy.wait()
        for group, send in zip(groups, outs[len(widths) :]):
            for i in group:
                low, wide = lows[i], widths[i]
                total = matmul(flipped, signal_here[:, low : low + wide])
                outs[i][...] = total[:half].astype(BF16)
                place = low - lows[group[0]]
                send[:, place : place + wide] = total[half:].astype(BF16)

    outs = call(
        kernel,
        name,
        [jax.ShapeDtypeStruct((half, wide), BF16) for wide in all_widths],
        [HBM, HBM],
        [basis, signal],
        None,
        limit=MOST,
        out_specs=[WHOLE] * len(all_widths),
        scratch_shapes=[
            pltpu.VMEM((rows, width), BF16),
            pltpu.VMEM(signal.shape, BF16),
            pltpu.SemaphoreType.DMA((pieces,)),
            pltpu.SemaphoreType.DMA,
        ],
        cost_estimate=span(name),
    )
    return outs[: len(widths)], outs[len(widths) :]


def level(name, weight, blocks, low, wide, count, held, after):
    width = weight.shape[0]
    depth = width // count
    given = len(blocks) + len(held)

    def kernel(weight, *refs):
        ins, outs = refs[: len(blocks)], refs[given:]
        here = [slice(low, low + wide) if ref.shape[1] > wide else slice(None) for ref in ins]
        stacked = jnp.concatenate([ref[:, part] for ref, part in zip(ins, here)], axis=0)
        total = matmul(weight[...], stacked)
        for i, out in enumerate(outs[:count]):
            out[...] = total[i * depth : (i + 1) * depth].astype(BF16)
        for ref, out in zip(refs[len(blocks) : given], outs[count:]):
            out[...] = ref[...]

    shapes = [(depth, wide)] * count + [block.shape for block in held]
    return call(
        kernel,
        name,
        [jax.ShapeDtypeStruct(shape, BF16) for shape in shapes],
        [WHOLE] * (1 + given),
        [weight] + blocks + held,
        after,
        out_specs=[WHOLE] * len(shapes),
        cost_estimate=span(name),
    )


def digits(groups):
    bits = groups.bit_length() - 1
    found, shift = [(0, 2)], 1
    while shift < bits:
        count = 2 if shift + 2 <= bits else 1
        found.append((shift, 1 << count))
        shift += count
    return found


def layouts_of(groups, steps):
    layouts = [by_digit(range(groups), steps[0])]
    for step in steps[1:]:
        layouts.append(by_digit(sum(layouts[-1], []), step))
    return layouts


def values_of(radix):
    return [0] + sorted(range(1, radix), key=lambda value: -value.bit_count())


def by_digit(slots, digit):
    shift, radix = digit
    return [[r for r in slots if r >> shift & radix - 1 == value] for value in values_of(radix)]


def regroup(name, blocks, layout, digit, block, after):
    columns = blocks[0].shape[1]
    place = {r: (i, j) for i, held in enumerate(layout) for j, r in enumerate(held)}
    wanted = by_digit(sum(layout, []), digit)

    def sort(values):
        parts = [[values[place[r][0]][place[r][1] * block :][:block] for r in held] for held in wanted]
        return [jnp.concatenate(part, axis=0) for part in parts]

    if block % ROWS:
        return sort(blocks), wanted

    def kernel(*refs):
        for ref, value in zip(refs[len(blocks) :], sort([ref[...] for ref in refs[: len(blocks)]])):
            ref[...] = value

    outs = call(
        kernel,
        name,
        [jax.ShapeDtypeStruct((len(held) * block, columns), BF16) for held in wanted],
        [WHOLE] * len(blocks),
        blocks,
        after,
        out_specs=[WHOLE] * len(wanted),
        cost_estimate=span(name),
    )
    return list(outs), wanted


def last(name, weight, basis, keeps, got, before, low, columns, after):
    rows, width = basis.shape
    wide = got.shape[1]
    pieces = row_pieces(rows, 6)
    depth = rows // pieces
    given = [] if before is None else [before]

    def kernel(weight, basis, got, *refs):
        out, here, left = refs[len(keeps) + len(given) :]
        keep = jnp.concatenate([ref[...] for ref in refs[: len(keeps)]], axis=1)
        stacked = jnp.concatenate([keep, got[...]], axis=0)
        coeffs = matmul(weight[...], stacked).astype(BF16)
        copies = []
        for i in range(pieces):
            part = pl.ds(i * depth, depth)
            here[part, :] = matmul(basis[part, :], coeffs).astype(BF16)
            copy = pltpu.make_async_copy(here.at[part], out.at[part, pl.ds(low, wide)], left.at[i])
            copy.start()
            copies.append(copy)
        for copy in copies:
            copy.wait()

    return call(
        kernel,
        name,
        jax.ShapeDtypeStruct((rows, columns), BF16),
        [WHOLE] * (3 + len(keeps)) + [HBM] * len(given),
        [weight, basis, got] + keeps + given,
        after,
        out_specs=HBM,
        scratch_shapes=[pltpu.VMEM((rows, wide), BF16), pltpu.SemaphoreType.DMA((pieces,))],
        input_output_aliases={3 + len(keeps): 0} if given else {},
        cost_estimate=span(name),
    )


def local(signal, col_basis, right_coupling, middle_coupling, left_coupling, row_basis, node_order):
    groups = lax.axis_size("mid")
    width = col_basis.shape[1]
    block = width // groups
    columns = signal.shape[1]
    chunks = shares(columns, SHARES)
    lows = [sum(chunks[:i]) for i in range(len(chunks))]
    whole = len(chunks) == len(SHARES)
    heads = HEADS if whole else ((0,),)
    steps = digits(groups)
    layouts = layouts_of(groups, steps)

    keeps, sends = opening("opening", col_basis, signal, chunks, heads)
    right0, right1, middle, left0, left1, *later = prepare(
        "prepare",
        node_order,
        sum(layouts[0], []),
        sum(layouts[-1], []),
        right_coupling,
        middle_coupling,
        left_coupling,
        list(sends[1:]),
    )
    gots = {}
    for group, send in zip(heads, [sends[0]] + later):
        got = swap(send, "sub", 1)
        for i in group:
            gots[i] = (got, lows[i] - lows[group[0]])

    out, after = None, right0
    waiting, pops, entered = [], 0, 0
    held = []
    while waiting or entered < len(chunks):
        if entered < len(chunks) and (pops >= ENTRY[entered] or not waiting):
            waiting.append((1, entered, [keeps[entered], gots[entered][0]]))
            entered += 1
            continue
        turn = TURNS.get(pops, 0)
        stage, i, blocks = waiting.pop(turn if turn < len(waiting) else 0)
        pops += 1
        wide = chunks[i]
        released = []
        if stage == 1:
            results = level(f"right0_{i}", right0, blocks, gots[i][1], wide, 2, [], after)
            axis, shift, radix = "sub", 1, 2
            if i in WAITS and whole:
                held.append((i, results))
                after = results[0]
                continue
        elif stage == 2:
            count = steps[0][1]
            free = [(j, kept) for j, kept in held if WAITS[j] == i]
            sends = [kept[1] for _, kept in free]
            results = level(f"right1_{i}", right1, blocks, 0, wide, count, sends, after)
            axis, shift, radix = "mid", *steps[0]
            for (j, kept), send in zip(free, results[count:]):
                released.append((2, j, [kept[0], swap(send, "sub", 2)]))
            results = results[:count]
        elif stage < 2 + len(steps):
            step = steps[stage - 2]
            results, _ = regroup(
                f"regroup{stage}_{i}", blocks, layouts[stage - 3], step, block, after
            )
            axis, shift, radix = "mid", *step
        elif stage == 2 + len(steps):
            results = level(f"middle_{i}", middle, blocks, 0, wide, 2, [], after)
            axis, shift, radix = "sub", 1, 2
        elif stage == 3 + len(steps):
            results = level(f"left0_{i}", left0, blocks, 0, wide, 2, [], after)
            axis, shift, radix = "sub", 0, 2
        else:
            name = f"last_{i}"
            out = last(name, left1, row_basis, blocks[:1], blocks[1], out, lows[i], columns, after)
            continue
        after = results[0]
        routes = [value << shift for value in values_of(radix)[1:]]
        moved = [swap(send, axis, route) for send, route in zip(results[1:], routes)]
        waiting.append((stage + 1, i, [results[0]] + moved))
        waiting += released
    return out


def solution(mesh):
    return jax.shard_map(
        local,
        mesh=mesh,
        in_specs=(
            P(("mid", "sub"), None),
            P(("mid", "sub"), None),
            P(("mid", "sub"), None, None, None),
            P(("mid", "sub"), None, None),
            P(("mid", "sub"), None, None, None),
            P(("mid", "sub"), None),
            P(),
        ),
        out_specs=P(("mid", "sub"), None),
        check_vma=False,
    )
```

```python
import jax
import jax.numpy as jnp
from jax import lax
from jax.experimental import pallas as pl
from jax.experimental.pallas import tpu as pltpu
from jax.sharding import PartitionSpec as P

LANES = 128
SHARES = (2, 3, 4)
HEADS = ((0,), (1,), (2,))
TAILS = ((0, 1), (2,))
ENTRY = (0, 0, 1)
SPANS = {}
ROWS = 16
SCOPED = 8 * 2**20
MOST = 213 * 2**18
F32 = jnp.float32
BF16 = jnp.bfloat16
WHOLE = pl.BlockSpec(memory_space=pltpu.VMEM)
SCALARS = pl.BlockSpec(memory_space=pltpu.SMEM)
PLACE = pl.BlockSpec(memory_space=pl.ANY)
HBM = pl.BlockSpec(memory_space=pltpu.HBM)


def shares(columns, weights):
    tiles = columns // LANES
    if tiles < len(weights):
        return [columns]
    edges = [round(tiles * sum(weights[:i]) / sum(weights)) * LANES for i in range(len(weights))]
    edges.append(columns)
    return [high - low for low, high in zip(edges[:-1], edges[1:])]


def swap(block, axis, distance):
    count = lax.axis_size(axis)
    return lax.ppermute(block, axis, [(i, i ^ distance) for i in range(count)])


def swapped(matrix, axis, flag):
    half = matrix.shape[axis] // 2
    low = lax.slice_in_dim(matrix, 0, half, axis=axis)
    high = lax.slice_in_dim(matrix, half, 2 * half, axis=axis)
    return jnp.where(flag == 1, jnp.concatenate([high, low], axis=axis), matrix)


def matmul(left, right):
    return lax.dot_general(left, right, (((1,), (0,)), ((), ())), preferred_element_type=F32)


def span(name):
    flops = SPANS.get(name.split("_")[0], 10**9)
    return pl.CostEstimate(flops=flops, bytes_accessed=0, transcendentals=0)


def call(kernel, name, outs, specs, operands, after, limit=SCOPED, **more):
    extra = [] if after is None else [after]

    def body(*refs):
        kernel(*refs[: len(operands)], *refs[len(operands) + len(extra) :])

    return pl.pallas_call(
        body,
        name=name,
        in_specs=specs + [PLACE] * len(extra),
        out_shape=outs,
        compiler_params=pltpu.CompilerParams(vmem_limit_bytes=limit),
        **more,
    )(*operands, *extra)


def prepare(name, node_order, slots_out, slots_in, right, middle, left, held):
    width = middle.shape[-1]
    groups = node_order.shape[0]
    block = width // groups

    def kernel(node_order, right, middle, left, *refs):
        right0, right1, middle0, left0, left1, *passed = refs[len(held) :]
        for block_in, block_out in zip(refs[: len(held)], passed):
            block_out[...] = block_in[...]
        place, group = lax.axis_index("sub"), lax.axis_index("mid")
        bit0, bit1 = place & 1, place >> 1 & 1
        right0[...] = swapped(swapped(right[0, 0], 1, bit0), 0, bit1)
        place = lax.broadcasted_iota(jnp.int32, (width, 1), 0)
        source = place % block
        for i, slot in enumerate(slots_out):
            piece = node_order[slot ^ group] * block
            source += jnp.where(place // block == i, piece, 0)
        across = lax.broadcasted_iota(jnp.int32, (width, width), 1)
        pick = jnp.where(across == source, 1.0, 0.0).astype(BF16)
        right1[...] = matmul(pick, swapped(right[0, 1], 1, bit1)).astype(BF16)
        place = lax.broadcasted_iota(jnp.int32, (1, width), 1)
        source = place % block
        for i, slot in enumerate(slots_in):
            source += jnp.where(place // block == i, (slot ^ group) * block, 0)
        down = lax.broadcasted_iota(jnp.int32, (width, width), 0)
        pick = jnp.where(down == source, 1.0, 0.0).astype(BF16)
        middle0[...] = swapped(matmul(middle[0], pick).astype(BF16), 0, bit1)
        left0[...] = swapped(swapped(left[0, 0], 1, bit1), 0, bit0)
        left1[...] = swapped(left[0, 1], 1, bit0)

    return call(
        kernel,
        name,
        [jax.ShapeDtypeStruct((width, width), BF16)] * 5
        + [jax.ShapeDtypeStruct(block.shape, BF16) for block in held],
        [SCALARS] + [WHOLE] * (3 + len(held)),
        [node_order, right, middle, left] + held,
        None,
        out_specs=[WHOLE] * (5 + len(held)),
        cost_estimate=span(name),
    )


def row_pieces(rows, pieces):
    return pieces if rows % (pieces * ROWS) == 0 else 1


def opening(name, basis, signal, widths, groups):
    rows, width = basis.shape
    half = width // 2
    pieces = row_pieces(rows, 6)
    depth = rows // pieces
    lows = [sum(widths[:i]) for i in range(len(widths))]
    all_widths = widths + [sum(widths[i] for i in group) for group in groups]

    def kernel(basis, signal, *refs):
        outs, (basis_here, signal_here, arrived, basis_arrived) = refs[:-4], refs[-4:]
        fetch_basis = pltpu.make_async_copy(basis, basis_here, basis_arrived)
        fetch_basis.start()
        copies = []
        for i in range(pieces):
            part = pl.ds(i * depth, depth)
            copies.append(
                pltpu.make_async_copy(signal.at[part], signal_here.at[part], arrived.at[i])
            )
            copies[-1].start()
        fetch_basis.wait()
        flipped = swapped(basis_here[...].T, 0, lax.axis_index("sub") & 1)
        for copy in copies:
            copy.wait()
        for group, send in zip(groups, outs[len(widths) :]):
            for i in group:
                low, wide = lows[i], widths[i]
                total = matmul(flipped, signal_here[:, low : low + wide])
                outs[i][...] = total[:half].astype(BF16)
                place = low - lows[group[0]]
                send[:, place : place + wide] = total[half:].astype(BF16)

    outs = call(
        kernel,
        name,
        [jax.ShapeDtypeStruct((half, wide), BF16) for wide in all_widths],
        [HBM, HBM],
        [basis, signal],
        None,
        limit=MOST,
        out_specs=[WHOLE] * len(all_widths),
        scratch_shapes=[
            pltpu.VMEM((rows, width), BF16),
            pltpu.VMEM(signal.shape, BF16),
            pltpu.SemaphoreType.DMA((pieces,)),
            pltpu.SemaphoreType.DMA,
        ],
        cost_estimate=span(name),
    )
    return outs[: len(widths)], outs[len(widths) :]


def level(name, weight, blocks, low, wide, count, before, after):
    width = weight.shape[0]
    depth = width // count
    ahead = sum(block.shape[1] for block in before)

    def kernel(weight, *refs):
        ins, outs = refs[: len(blocks)], refs[len(blocks) + len(before) :]
        here = [slice(low, low + wide) if ref.shape[1] > wide else slice(None) for ref in ins]
        stacked = jnp.concatenate([ref[:, part] for ref, part in zip(ins, here)], axis=0)
        total = matmul(weight[...], stacked)
        for i, out in enumerate(outs):
            value = total[i * depth : (i + 1) * depth].astype(BF16)
            if before and i == count - 1:
                out[:, :ahead] = refs[len(blocks)][...]
                out[:, ahead:] = value
            else:
                out[...] = value

    widths = [wide] * (count - 1) + [ahead + wide]
    return call(
        kernel,
        name,
        [jax.ShapeDtypeStruct((depth, columns), BF16) for columns in widths],
        [WHOLE] * (1 + len(blocks) + len(before)),
        [weight] + blocks + before,
        after,
        out_specs=[WHOLE] * count,
        cost_estimate=span(name),
    )


def digits(groups):
    bits = groups.bit_length() - 1
    found, shift = [(0, 2)], 1
    while shift < bits:
        count = 2 if shift + 2 <= bits else 1
        found.append((shift, 1 << count))
        shift += count
    return found


def layouts_of(groups, steps):
    layouts = [by_digit(range(groups), steps[0])]
    for step in steps[1:]:
        layouts.append(by_digit(sum(layouts[-1], []), step))
    return layouts


def values_of(radix):
    return [0] + sorted(range(1, radix), key=lambda value: -value.bit_count())


def by_digit(slots, digit):
    shift, radix = digit
    return [[r for r in slots if r >> shift & radix - 1 == value] for value in values_of(radix)]


def regroup(name, blocks, layout, digit, block, after):
    columns = blocks[0].shape[1]
    place = {r: (i, j) for i, held in enumerate(layout) for j, r in enumerate(held)}
    wanted = by_digit(sum(layout, []), digit)

    def sort(values):
        parts = [[values[place[r][0]][place[r][1] * block :][:block] for r in held] for held in wanted]
        return [jnp.concatenate(part, axis=0) for part in parts]

    if block % ROWS:
        return sort(blocks), wanted

    def kernel(*refs):
        for ref, value in zip(refs[len(blocks) :], sort([ref[...] for ref in refs[: len(blocks)]])):
            ref[...] = value

    outs = call(
        kernel,
        name,
        [jax.ShapeDtypeStruct((len(held) * block, columns), BF16) for held in wanted],
        [WHOLE] * len(blocks),
        blocks,
        after,
        out_specs=[WHOLE] * len(wanted),
        cost_estimate=span(name),
    )
    return list(outs), wanted


def last(name, weight, basis, keeps, got, before, low, columns, after):
    rows, width = basis.shape
    wide = got.shape[1]
    pieces = row_pieces(rows, 6)
    depth = rows // pieces
    given = [] if before is None else [before]

    def kernel(weight, basis, got, *refs):
        out, here, left = refs[len(keeps) + len(given) :]
        keep = jnp.concatenate([ref[...] for ref in refs[: len(keeps)]], axis=1)
        stacked = jnp.concatenate([keep, got[...]], axis=0)
        coeffs = matmul(weight[...], stacked).astype(BF16)
        copies = []
        for i in range(pieces):
            part = pl.ds(i * depth, depth)
            here[part, :] = matmul(basis[part, :], coeffs).astype(BF16)
            copy = pltpu.make_async_copy(here.at[part], out.at[part, pl.ds(low, wide)], left.at[i])
            copy.start()
            copies.append(copy)
        for copy in copies:
            copy.wait()

    return call(
        kernel,
        name,
        jax.ShapeDtypeStruct((rows, columns), BF16),
        [WHOLE] * (3 + len(keeps)) + [HBM] * len(given),
        [weight, basis, got] + keeps + given,
        after,
        out_specs=HBM,
        scratch_shapes=[pltpu.VMEM((rows, wide), BF16), pltpu.SemaphoreType.DMA((pieces,))],
        input_output_aliases={3 + len(keeps): 0} if given else {},
        cost_estimate=span(name),
    )


def local(signal, col_basis, right_coupling, middle_coupling, left_coupling, row_basis, node_order):
    groups = lax.axis_size("mid")
    width = col_basis.shape[1]
    block = width // groups
    columns = signal.shape[1]
    chunks = shares(columns, SHARES)
    lows = [sum(chunks[:i]) for i in range(len(chunks))]
    whole = len(chunks) == len(SHARES)
    heads = HEADS if whole else ((0,),)
    tails = TAILS if whole else ((0,),)
    steps = digits(groups)
    layouts = layouts_of(groups, steps)

    keeps, sends = opening("opening", col_basis, signal, chunks, heads)
    right0, right1, middle, left0, left1, *later = prepare(
        "prepare",
        node_order,
        sum(layouts[0], []),
        sum(layouts[-1], []),
        right_coupling,
        middle_coupling,
        left_coupling,
        list(sends[1:]),
    )
    gots = {}
    for group, send in zip(heads, [sends[0]] + later):
        got = swap(send, "sub", 1)
        for i in group:
            gots[i] = (got, lows[i] - lows[group[0]])

    out, after = None, right0
    waiting, pops, entered = [], 0, 0
    parked = {}
    while waiting or entered < len(chunks):
        if entered < len(chunks) and (pops >= ENTRY[entered] or not waiting):
            waiting.append((1, entered, [keeps[entered], gots[entered][0]]))
            entered += 1
            continue
        stage, i, blocks = waiting.pop(0)
        pops += 1
        wide = chunks[i]
        if stage == 1:
            results = level(f"right0_{i}", right0, blocks, gots[i][1], wide, 2, [], after)
            axis, shift, radix = "sub", 1, 2
        elif stage == 2:
            count = steps[0][1]
            results = level(f"right1_{i}", right1, blocks, 0, wide, count, [], after)
            axis, shift, radix = "mid", *steps[0]
        elif stage < 2 + len(steps):
            step = steps[stage - 2]
            results, _ = regroup(
                f"regroup{stage}_{i}", blocks, layouts[stage - 3], step, block, after
            )
            axis, shift, radix = "mid", *step
        elif stage == 2 + len(steps):
            results = level(f"middle_{i}", middle, blocks, 0, wide, 2, [], after)
            axis, shift, radix = "sub", 1, 2
        elif stage == 3 + len(steps):
            group = next(group for group in tails if i in group)
            before = [parked[group[0]][-1]] if i != group[0] else []
            results = level(f"left0_{i}", left0, blocks, 0, wide, 2, before, after)
            axis, shift, radix = "sub", 0, 2
            parked[group[0]] = parked.get(group[0], [])[:-1] + list(results)
            if i != group[-1]:
                after = results[0]
                continue
            results = parked[group[0]]
            got = swap(results[-1], axis, 1)
            waiting.append((stage + 1, group[0], [results[:-1], got]))
            after = results[-2]
            continue
        else:
            name = f"last_{i}"
            out = last(name, left1, row_basis, *blocks, out, lows[i], columns, after)
            continue
        after = results[0]
        routes = [value << shift for value in values_of(radix)[1:]]
        moved = [swap(send, axis, route) for send, route in zip(results[1:], routes)]
        waiting.append((stage + 1, i, [results[0]] + moved))
    return out


def solution(mesh):
    return jax.shard_map(
        local,
        mesh=mesh,
        in_specs=(
            P(("mid", "sub"), None),
            P(("mid", "sub"), None),
            P(("mid", "sub"), None, None, None),
            P(("mid", "sub"), None, None),
            P(("mid", "sub"), None, None, None),
            P(("mid", "sub"), None),
            P(),
        ),
        out_specs=P(("mid", "sub"), None),
        check_vma=False,
    )
```

```python
import jax
import jax.numpy as jnp
from jax import lax
from jax.experimental import pallas as pl
from jax.experimental.pallas import tpu as pltpu
from jax.sharding import PartitionSpec as P

LANES = 128
ENTRY_SHARES = (3, 3, 3)
ENTRY = (0, 0, 1)
MERGED = ((0,), (1,), (2,))
SPLIT = {}
ROWS = 16
SCOPED = 8 * 2**20
MOST = 213 * 2**18
F32 = jnp.float32
BF16 = jnp.bfloat16
WHOLE = pl.BlockSpec(memory_space=pltpu.VMEM)
SCALARS = pl.BlockSpec(memory_space=pltpu.SMEM)
PLACE = pl.BlockSpec(memory_space=pl.ANY)
HBM = pl.BlockSpec(memory_space=pltpu.HBM)


def shares(columns, weights):
    tiles = columns // LANES
    if tiles < len(weights):
        return [columns]
    edges = [round(tiles * sum(weights[:i]) / sum(weights)) * LANES for i in range(len(weights))]
    edges.append(columns)
    return [high - low for low, high in zip(edges[:-1], edges[1:])]


def swap(block, axis, distance):
    count = lax.axis_size(axis)
    return lax.ppermute(block, axis, [(i, i ^ distance) for i in range(count)])


def swapped(matrix, axis, flag):
    half = matrix.shape[axis] // 2
    low = lax.slice_in_dim(matrix, 0, half, axis=axis)
    high = lax.slice_in_dim(matrix, half, 2 * half, axis=axis)
    return jnp.where(flag == 1, jnp.concatenate([high, low], axis=axis), matrix)


def matmul(left, right):
    return lax.dot_general(left, right, (((1,), (0,)), ((), ())), preferred_element_type=F32)


def cost(flops, moved):
    return pl.CostEstimate(flops=flops, bytes_accessed=moved, transcendentals=0)


def call(kernel, name, outs, specs, operands, after, limit=SCOPED, **more):
    extra = [] if after is None else [after]

    def body(*refs):
        kernel(*refs[: len(operands)], *refs[len(operands) + len(extra) :])

    return pl.pallas_call(
        body,
        name=name,
        in_specs=specs + [PLACE] * len(extra),
        out_shape=outs,
        compiler_params=pltpu.CompilerParams(vmem_limit_bytes=limit),
        **more,
    )(*operands, *extra)


def prepare(name, node_order, slots_out, slots_in, right, middle, left, after):
    width = middle.shape[-1]
    groups = node_order.shape[0]
    block = width // groups

    def kernel(node_order, right, middle, left, right0, right1, middle0, left0, left1):
        place, group = lax.axis_index("sub"), lax.axis_index("mid")
        bit0, bit1 = place & 1, place >> 1 & 1
        right0[...] = swapped(swapped(right[0, 0], 1, bit0), 0, bit1)
        place = lax.broadcasted_iota(jnp.int32, (width, 1), 0)
        source = place % block
        for i, slot in enumerate(slots_out):
            piece = node_order[slot ^ group] * block
            source += jnp.where(place // block == i, piece, 0)
        across = lax.broadcasted_iota(jnp.int32, (width, width), 1)
        pick = jnp.where(across == source, 1.0, 0.0).astype(BF16)
        right1[...] = matmul(pick, swapped(right[0, 1], 1, bit1)).astype(BF16)
        place = lax.broadcasted_iota(jnp.int32, (1, width), 1)
        source = place % block
        for i, slot in enumerate(slots_in):
            source += jnp.where(place // block == i, (slot ^ group) * block, 0)
        down = lax.broadcasted_iota(jnp.int32, (width, width), 0)
        pick = jnp.where(down == source, 1.0, 0.0).astype(BF16)
        middle0[...] = swapped(matmul(middle[0], pick).astype(BF16), 0, bit1)
        left0[...] = swapped(swapped(left[0, 0], 1, bit1), 0, bit0)
        left1[...] = swapped(left[0, 1], 1, bit0)

    return call(
        kernel,
        name,
        [jax.ShapeDtypeStruct((width, width), BF16)] * 5,
        [SCALARS] + [WHOLE] * 3,
        [node_order, right, middle, left],
        after,
        out_specs=[WHOLE] * 5,
        cost_estimate=cost(4 * width**3, 20 * width**2),
    )


def row_pieces(rows, pieces):
    return pieces if rows % (pieces * ROWS) == 0 else 1


def opening(name, basis, signal, widths):
    rows, width = basis.shape
    half = width // 2
    pieces = row_pieces(rows, 12)
    depth = rows // pieces
    lows = [sum(widths[:i]) for i in range(len(widths))]

    def kernel(basis, signal, *refs):
        outs, (basis_here, signal_here, arrived, basis_arrived) = refs[:-4], refs[-4:]
        fetch_basis = pltpu.make_async_copy(basis, basis_here, basis_arrived)
        fetch_basis.start()
        copies = []
        for i in range(pieces):
            part = pl.ds(i * depth, depth)
            copies.append(
                pltpu.make_async_copy(signal.at[part], signal_here.at[part], arrived.at[i])
            )
            copies[-1].start()
        fetch_basis.wait()
        flipped = swapped(basis_here[...].T, 0, lax.axis_index("sub") & 1)
        for copy in copies:
            copy.wait()
        for i, (low, wide) in enumerate(zip(lows, widths)):
            total = matmul(flipped, signal_here[:, low : low + wide])
            outs[2 * i][...] = total[:half].astype(BF16)
            outs[2 * i + 1][...] = total[half:].astype(BF16)

    outs = call(
        kernel,
        name,
        [jax.ShapeDtypeStruct((half, wide), BF16) for wide in widths for _ in range(2)],
        [HBM, HBM],
        [basis, signal],
        None,
        limit=MOST,
        out_specs=[WHOLE] * (2 * len(widths)),
        scratch_shapes=[
            pltpu.VMEM((rows, width), BF16),
            pltpu.VMEM(signal.shape, BF16),
            pltpu.SemaphoreType.DMA((pieces,)),
            pltpu.SemaphoreType.DMA,
        ],
        cost_estimate=cost(2 * rows * width * sum(widths), 2 * rows * (sum(widths) + width)),
    )
    return list(zip(outs[0::2], outs[1::2]))


def level(name, weight, chunks, widths, count, after):
    width = weight.shape[0]
    depth = width // count
    columns = sum(widths)
    blocks = len(chunks[0])

    def kernel(weight, *refs):
        ins, outs = refs[: blocks * len(chunks)], refs[blocks * len(chunks) :]
        stacked = [
            jnp.concatenate([ref[...] for ref in ins[i * blocks : (i + 1) * blocks]], axis=0)
            for i in range(len(chunks))
        ]
        total = matmul(weight[...], jnp.concatenate(stacked, axis=1))
        low = 0
        for i, wide in enumerate(widths):
            for j in range(count):
                part = total[j * depth : (j + 1) * depth, low : low + wide]
                outs[i * count + j][...] = part.astype(BF16)
            low += wide

    flat = [block for chunk in chunks for block in chunk]
    outs = call(
        kernel,
        name,
        [jax.ShapeDtypeStruct((depth, wide), BF16) for wide in widths for _ in range(count)],
        [WHOLE] * (1 + len(flat)),
        [weight] + flat,
        after,
        out_specs=[WHOLE] * (count * len(widths)),
        cost_estimate=cost(2 * width * width * columns, 4 * width * columns),
    )
    return [list(outs[i * count : (i + 1) * count]) for i in range(len(widths))]


def digits(groups):
    bits = groups.bit_length() - 1
    found = [(0, 2)]
    while found[-1][0] + (found[-1][1].bit_length() - 1) < bits:
        shift = found[-1][0] + found[-1][1].bit_length() - 1
        found.append((shift, 4 if shift + 2 <= bits else 2))
    return found


def by_digit(slots, digit):
    shift, radix = digit
    return [[r for r in slots if r >> shift & radix - 1 == value] for value in range(radix)]


def regroup(name, blocks, layout, digit, block, after):
    columns = blocks[0].shape[1]
    place = {r: (i, j) for i, held in enumerate(layout) for j, r in enumerate(held)}
    wanted = by_digit(sum(layout, []), digit)

    def sort(values):
        parts = [[values[place[r][0]][place[r][1] * block :][:block] for r in held] for held in wanted]
        return [jnp.concatenate(part, axis=0) for part in parts]

    if block % ROWS:
        return sort(blocks), wanted

    def kernel(*refs):
        for ref, value in zip(refs[len(blocks) :], sort([ref[...] for ref in refs[: len(blocks)]])):
            ref[...] = value

    outs = call(
        kernel,
        name,
        [jax.ShapeDtypeStruct((len(held) * block, columns), BF16) for held in wanted],
        [WHOLE] * len(blocks),
        blocks,
        after,
        out_specs=[WHOLE] * len(wanted),
        cost_estimate=cost(0, 4 * block * len(place) * columns),
    )
    return list(outs), wanted


def last(name, weight, basis, keep, got, before, low, columns, after):
    rows, width = basis.shape
    wide = keep.shape[1]
    pieces = row_pieces(rows, 4)
    depth = rows // pieces
    given = [] if before is None else [before]

    def kernel(weight, basis, keep, got, *refs):
        out, here, left = refs[len(given) :]
        stacked = jnp.concatenate([keep[...], got[...]], axis=0)
        coeffs = matmul(weight[...], stacked).astype(BF16)
        copies = []
        for i in range(pieces):
            part = pl.ds(i * depth, depth)
            here[part, :] = matmul(basis[part, :], coeffs).astype(BF16)
            copy = pltpu.make_async_copy(here.at[part], out.at[part, pl.ds(low, wide)], left.at[i])
            copy.start()
            copies.append(copy)
        for copy in copies:
            copy.wait()

    return call(
        kernel,
        name,
        jax.ShapeDtypeStruct((rows, columns), BF16),
        [WHOLE] * 4 + [HBM] * len(given),
        [weight, basis, keep, got] + given,
        after,
        out_specs=HBM,
        scratch_shapes=[pltpu.VMEM((rows, wide), BF16), pltpu.SemaphoreType.DMA((pieces,))],
        input_output_aliases={4: 0} if given else {},
        cost_estimate=cost(2 * rows * width * wide, 2 * rows * wide),
    )


def local(signal, col_basis, right_coupling, middle_coupling, left_coupling, row_basis, node_order):
    groups = lax.axis_size("mid")
    width = col_basis.shape[1]
    block = width // groups
    columns = signal.shape[1]
    chunks = shares(columns, ENTRY_SHARES)
    starts = [sum(chunks[:i]) for i in range(len(chunks))]
    merged = {i: group for group in MERGED for i in group}
    if len(chunks) < len(ENTRY_SHARES):
        merged = {i: (i,) for i in range(len(chunks))}
    steps = digits(groups)
    layouts = [by_digit(range(groups), steps[0])]
    for step in steps[1:]:
        layouts.append(by_digit(sum(layouts[-1], []), step))

    opened = opening("opening", col_basis, signal, chunks)
    couplings, out, after = None, None, None
    waiting, pops, entered = [], 0, 0
    parked = {}
    while waiting or entered < len(chunks):
        if entered < len(chunks) and (pops >= ENTRY[entered] or not waiting):
            i, entered = entered, entered + 1
            keep, send = opened[i]
            waiting.append((1, (i,), starts[i], [keep, swap(send, "sub", 1)]))
            continue
        stage, ids, low, blocks = waiting.pop(0)
        pops += 1
        wide = blocks[0].shape[1]
        name = "".join(str(i) for i in ids)
        if couplings is None:
            couplings = prepare(
                "prepare",
                node_order,
                sum(layouts[0], []),
                sum(layouts[-1], []),
                right_coupling,
                middle_coupling,
                left_coupling,
                after,
            )
            right0, right1, middle, left0, left1 = couplings
            after = right0
        if stage == 1:
            results = level(f"right0_{name}", right0, [blocks], [wide], 2, after)
            axis, shift = "sub", 1
        elif stage == 2:
            parked[ids[0]] = blocks
            ids = merged[ids[0]]
            if any(i not in parked for i in ids):
                continue
            wide = sum(chunks[i] for i in ids)
            low = starts[ids[0]]
            blocks = [parked[i] for i in ids]
            results = level(f"right1_{name}", right1, blocks, [wide], steps[0][1], after)
            axis, shift = "mid", steps[0][0]
        elif stage < 2 + len(steps):
            step = steps[stage - 2]
            held_as = layouts[stage - 3]
            results = [regroup(f"regroup{stage}_{name}", blocks, held_as, step, block, after)[0]]
            axis, shift = "mid", step[0]
        elif stage == 2 + len(steps):
            widths = shares(wide, SPLIT.get(ids, (1,)))
            results = level(f"middle_{name}", middle, [blocks], widths, 2, after)
            axis, shift = "sub", 1
        elif stage == 3 + len(steps):
            results = level(f"left0_{name}", left0, [blocks], [wide], 2, after)
            axis, shift = "sub", 0
        else:
            out = last(f"last{low}", left1, row_basis, *blocks, out, low, columns, after)
            continue
        after = results[0][0]
        for result in results:
            moved = [swap(send, axis, i + 1 << shift) for i, send in enumerate(result[1:])]
            waiting.append((stage + 1, ids, low, result[:1] + moved))
            low += result[0].shape[1]
    return out


def solution(mesh):
    return jax.shard_map(
        local,
        mesh=mesh,
        in_specs=(
            P(("mid", "sub"), None),
            P(("mid", "sub"), None),
            P(("mid", "sub"), None, None, None),
            P(("mid", "sub"), None, None),
            P(("mid", "sub"), None, None, None),
            P(("mid", "sub"), None),
            P(),
        ),
        out_specs=P(("mid", "sub"), None),
        check_vma=False,
    )
```

```python
import jax
import jax.numpy as jnp
from jax import lax
from jax.experimental import pallas as pl
from jax.experimental.pallas import tpu as pltpu
from jax.sharding import PartitionSpec as P

LANES = 128
SHARES = (3, 3, 3)
HEADS = ((0,), (1,), (2,))
TAILS = ((0, 1), (2,))
ENTRY = (0, 0, 1)
SPANS = {}
ROWS = 16
SCOPED = 8 * 2**20
MOST = 213 * 2**18
F32 = jnp.float32
BF16 = jnp.bfloat16
WHOLE = pl.BlockSpec(memory_space=pltpu.VMEM)
SCALARS = pl.BlockSpec(memory_space=pltpu.SMEM)
PLACE = pl.BlockSpec(memory_space=pl.ANY)
HBM = pl.BlockSpec(memory_space=pltpu.HBM)


def shares(columns, weights):
    tiles = columns // LANES
    if tiles < len(weights):
        return [columns]
    edges = [round(tiles * sum(weights[:i]) / sum(weights)) * LANES for i in range(len(weights))]
    edges.append(columns)
    return [high - low for low, high in zip(edges[:-1], edges[1:])]


def swap(block, axis, distance):
    count = lax.axis_size(axis)
    return lax.ppermute(block, axis, [(i, i ^ distance) for i in range(count)])


def swapped(matrix, axis, flag):
    half = matrix.shape[axis] // 2
    low = lax.slice_in_dim(matrix, 0, half, axis=axis)
    high = lax.slice_in_dim(matrix, half, 2 * half, axis=axis)
    return jnp.where(flag == 1, jnp.concatenate([high, low], axis=axis), matrix)


def matmul(left, right):
    return lax.dot_general(left, right, (((1,), (0,)), ((), ())), preferred_element_type=F32)


def span(name):
    flops = SPANS.get(name.split("_")[0], 0)
    return pl.CostEstimate(flops=flops, bytes_accessed=0, transcendentals=0)


def call(kernel, name, outs, specs, operands, after, limit=SCOPED, **more):
    extra = [] if after is None else [after]

    def body(*refs):
        kernel(*refs[: len(operands)], *refs[len(operands) + len(extra) :])

    return pl.pallas_call(
        body,
        name=name,
        in_specs=specs + [PLACE] * len(extra),
        out_shape=outs,
        compiler_params=pltpu.CompilerParams(vmem_limit_bytes=limit),
        **more,
    )(*operands, *extra)


def prepare(name, node_order, slots_out, slots_in, right, middle, left, held):
    width = middle.shape[-1]
    groups = node_order.shape[0]
    block = width // groups

    def kernel(node_order, right, middle, left, *refs):
        right0, right1, middle0, left0, left1, *passed = refs[len(held) :]
        for block_in, block_out in zip(refs[: len(held)], passed):
            block_out[...] = block_in[...]
        place, group = lax.axis_index("sub"), lax.axis_index("mid")
        bit0, bit1 = place & 1, place >> 1 & 1
        right0[...] = swapped(swapped(right[0, 0], 1, bit0), 0, bit1)
        place = lax.broadcasted_iota(jnp.int32, (width, 1), 0)
        source = place % block
        for i, slot in enumerate(slots_out):
            piece = node_order[slot ^ group] * block
            source += jnp.where(place // block == i, piece, 0)
        across = lax.broadcasted_iota(jnp.int32, (width, width), 1)
        pick = jnp.where(across == source, 1.0, 0.0).astype(BF16)
        right1[...] = matmul(pick, swapped(right[0, 1], 1, bit1)).astype(BF16)
        place = lax.broadcasted_iota(jnp.int32, (1, width), 1)
        source = place % block
        for i, slot in enumerate(slots_in):
            source += jnp.where(place // block == i, (slot ^ group) * block, 0)
        down = lax.broadcasted_iota(jnp.int32, (width, width), 0)
        pick = jnp.where(down == source, 1.0, 0.0).astype(BF16)
        middle0[...] = swapped(matmul(middle[0], pick).astype(BF16), 0, bit1)
        left0[...] = swapped(swapped(left[0, 0], 1, bit1), 0, bit0)
        left1[...] = swapped(left[0, 1], 1, bit0)

    return call(
        kernel,
        name,
        [jax.ShapeDtypeStruct((width, width), BF16)] * 5
        + [jax.ShapeDtypeStruct(block.shape, BF16) for block in held],
        [SCALARS] + [WHOLE] * (3 + len(held)),
        [node_order, right, middle, left] + held,
        None,
        out_specs=[WHOLE] * (5 + len(held)),
        cost_estimate=span(name),
    )


def row_pieces(rows, pieces):
    return pieces if rows % (pieces * ROWS) == 0 else 1


def opening(name, basis, signal, widths, groups):
    rows, width = basis.shape
    half = width // 2
    pieces = row_pieces(rows, 2)
    depth = rows // pieces
    lows = [sum(widths[:i]) for i in range(len(widths))]
    all_widths = widths + [sum(widths[i] for i in group) for group in groups]

    def kernel(basis, signal, *refs):
        outs, (basis_here, signal_here, arrived, basis_arrived) = refs[:-4], refs[-4:]
        fetch_basis = pltpu.make_async_copy(basis, basis_here, basis_arrived)
        fetch_basis.start()
        copies = []
        for i in range(pieces):
            part = pl.ds(i * depth, depth)
            copies.append(
                pltpu.make_async_copy(signal.at[part], signal_here.at[part], arrived.at[i])
            )
            copies[-1].start()
        fetch_basis.wait()
        flipped = swapped(basis_here[...].T, 0, lax.axis_index("sub") & 1)
        for copy in copies:
            copy.wait()
        for group, send in zip(groups, outs[len(widths) :]):
            for i in group:
                low, wide = lows[i], widths[i]
                total = matmul(flipped, signal_here[:, low : low + wide])
                outs[i][...] = total[:half].astype(BF16)
                place = low - lows[group[0]]
                send[:, place : place + wide] = total[half:].astype(BF16)

    outs = call(
        kernel,
        name,
        [jax.ShapeDtypeStruct((half, wide), BF16) for wide in all_widths],
        [HBM, HBM],
        [basis, signal],
        None,
        limit=MOST,
        out_specs=[WHOLE] * len(all_widths),
        scratch_shapes=[
            pltpu.VMEM((rows, width), BF16),
            pltpu.VMEM(signal.shape, BF16),
            pltpu.SemaphoreType.DMA((pieces,)),
            pltpu.SemaphoreType.DMA,
        ],
        cost_estimate=span(name),
    )
    return outs[: len(widths)], outs[len(widths) :]


def level(name, weight, blocks, low, wide, count, before, after):
    width = weight.shape[0]
    depth = width // count
    ahead = sum(block.shape[1] for block in before)

    def kernel(weight, *refs):
        ins, outs = refs[: len(blocks)], refs[len(blocks) + len(before) :]
        here = [slice(low, low + wide) if ref.shape[1] > wide else slice(None) for ref in ins]
        stacked = jnp.concatenate([ref[:, part] for ref, part in zip(ins, here)], axis=0)
        total = matmul(weight[...], stacked)
        for i, out in enumerate(outs):
            value = total[i * depth : (i + 1) * depth].astype(BF16)
            if before and i == count - 1:
                out[:, :ahead] = refs[len(blocks)][...]
                out[:, ahead:] = value
            else:
                out[...] = value

    widths = [wide] * (count - 1) + [ahead + wide]
    return call(
        kernel,
        name,
        [jax.ShapeDtypeStruct((depth, columns), BF16) for columns in widths],
        [WHOLE] * (1 + len(blocks) + len(before)),
        [weight] + blocks + before,
        after,
        out_specs=[WHOLE] * count,
        cost_estimate=span(name),
    )


def digits(groups):
    bits = groups.bit_length() - 1
    found, shift = [(0, 2)], 1
    while shift < bits:
        count = 2 if shift + 2 <= bits else 1
        found.append((shift, 1 << count))
        shift += count
    return found


def layouts_of(groups, steps):
    layouts = [by_digit(range(groups), steps[0])]
    for step in steps[1:]:
        layouts.append(by_digit(sum(layouts[-1], []), step))
    return layouts


def values_of(radix):
    return [0] + sorted(range(1, radix), key=lambda value: -value.bit_count())


def by_digit(slots, digit):
    shift, radix = digit
    return [[r for r in slots if r >> shift & radix - 1 == value] for value in values_of(radix)]


def regroup(name, blocks, layout, digit, block, after):
    columns = blocks[0].shape[1]
    place = {r: (i, j) for i, held in enumerate(layout) for j, r in enumerate(held)}
    wanted = by_digit(sum(layout, []), digit)

    def sort(values):
        parts = [[values[place[r][0]][place[r][1] * block :][:block] for r in held] for held in wanted]
        return [jnp.concatenate(part, axis=0) for part in parts]

    if block % ROWS:
        return sort(blocks), wanted

    def kernel(*refs):
        for ref, value in zip(refs[len(blocks) :], sort([ref[...] for ref in refs[: len(blocks)]])):
            ref[...] = value

    outs = call(
        kernel,
        name,
        [jax.ShapeDtypeStruct((len(held) * block, columns), BF16) for held in wanted],
        [WHOLE] * len(blocks),
        blocks,
        after,
        out_specs=[WHOLE] * len(wanted),
        cost_estimate=span(name),
    )
    return list(outs), wanted


def last(name, weight, basis, keeps, got, before, low, columns, after):
    rows, width = basis.shape
    wide = got.shape[1]
    pieces = row_pieces(rows, 6)
    depth = rows // pieces
    given = [] if before is None else [before]

    def kernel(weight, basis, got, *refs):
        out, here, left = refs[len(keeps) + len(given) :]
        keep = jnp.concatenate([ref[...] for ref in refs[: len(keeps)]], axis=1)
        stacked = jnp.concatenate([keep, got[...]], axis=0)
        coeffs = matmul(weight[...], stacked).astype(BF16)
        copies = []
        for i in range(pieces):
            part = pl.ds(i * depth, depth)
            here[part, :] = matmul(basis[part, :], coeffs).astype(BF16)
            copy = pltpu.make_async_copy(here.at[part], out.at[part, pl.ds(low, wide)], left.at[i])
            copy.start()
            copies.append(copy)
        for copy in copies:
            copy.wait()

    return call(
        kernel,
        name,
        jax.ShapeDtypeStruct((rows, columns), BF16),
        [WHOLE] * (3 + len(keeps)) + [HBM] * len(given),
        [weight, basis, got] + keeps + given,
        after,
        out_specs=HBM,
        scratch_shapes=[pltpu.VMEM((rows, wide), BF16), pltpu.SemaphoreType.DMA((pieces,))],
        input_output_aliases={3 + len(keeps): 0} if given else {},
        cost_estimate=span(name),
    )


def local(signal, col_basis, right_coupling, middle_coupling, left_coupling, row_basis, node_order):
    groups = lax.axis_size("mid")
    width = col_basis.shape[1]
    block = width // groups
    columns = signal.shape[1]
    chunks = shares(columns, SHARES)
    lows = [sum(chunks[:i]) for i in range(len(chunks))]
    whole = len(chunks) == len(SHARES)
    heads = HEADS if whole else ((0,),)
    tails = TAILS if whole else ((0,),)
    steps = digits(groups)
    layouts = layouts_of(groups, steps)

    keeps, sends = opening("opening", col_basis, signal, chunks, heads)
    right0, right1, middle, left0, left1, *later = prepare(
        "prepare",
        node_order,
        sum(layouts[0], []),
        sum(layouts[-1], []),
        right_coupling,
        middle_coupling,
        left_coupling,
        list(sends[1:]),
    )
    gots = {}
    for group, send in zip(heads, [sends[0]] + later):
        got = swap(send, "sub", 1)
        for i in group:
            gots[i] = (got, lows[i] - lows[group[0]])

    out, after = None, right0
    waiting, pops, entered = [], 0, 0
    parked = {}
    while waiting or entered < len(chunks):
        if entered < len(chunks) and (pops >= ENTRY[entered] or not waiting):
            waiting.append((1, entered, [keeps[entered], gots[entered][0]]))
            entered += 1
            continue
        stage, i, blocks = waiting.pop(0)
        pops += 1
        wide = chunks[i]
        if stage == 1:
            results = level(f"right0_{i}", right0, blocks, gots[i][1], wide, 2, [], after)
            axis, shift, radix = "sub", 1, 2
        elif stage == 2:
            count = steps[0][1]
            results = level(f"right1_{i}", right1, blocks, 0, wide, count, [], after)
            axis, shift, radix = "mid", *steps[0]
        elif stage < 2 + len(steps):
            step = steps[stage - 2]
            results, _ = regroup(
                f"regroup{stage}_{i}", blocks, layouts[stage - 3], step, block, after
            )
            axis, shift, radix = "mid", *step
        elif stage == 2 + len(steps):
            results = level(f"middle_{i}", middle, blocks, 0, wide, 2, [], after)
            axis, shift, radix = "sub", 1, 2
        elif stage == 3 + len(steps):
            group = next(group for group in tails if i in group)
            before = [parked[group[0]][-1]] if i != group[0] else []
            results = level(f"left0_{i}", left0, blocks, 0, wide, 2, before, after)
            axis, shift, radix = "sub", 0, 2
            parked[group[0]] = parked.get(group[0], [])[:-1] + list(results)
            if i != group[-1]:
                after = results[0]
                continue
            results = parked[group[0]]
            got = swap(results[-1], axis, 1)
            waiting.append((stage + 1, group[0], [results[:-1], got]))
            after = results[-2]
            continue
        else:
            name = f"last_{i}"
            out = last(name, left1, row_basis, *blocks, out, lows[i], columns, after)
            continue
        after = results[0]
        routes = [value << shift for value in values_of(radix)[1:]]
        moved = [swap(send, axis, route) for send, route in zip(results[1:], routes)]
        waiting.append((stage + 1, i, [results[0]] + moved))
    return out


def solution(mesh):
    return jax.shard_map(
        local,
        mesh=mesh,
        in_specs=(
            P(("mid", "sub"), None),
            P(("mid", "sub"), None),
            P(("mid", "sub"), None, None, None),
            P(("mid", "sub"), None, None),
            P(("mid", "sub"), None, None, None),
            P(("mid", "sub"), None),
            P(),
        ),
        out_specs=P(("mid", "sub"), None),
        check_vma=False,
    )
```

```python
import jax
import jax.numpy as jnp
from jax import lax
from jax.experimental import pallas as pl
from jax.experimental.pallas import tpu as pltpu
from jax.sharding import PartitionSpec as P

LANES = 128
SHARES = (2, 3, 4)
HEADS = ((0,), (1,), (2,))
TAILS = ((0,), (1,), (2,))
ENTRY = (0, 0, 1)
SPANS = {}
ROWS = 16
SCOPED = 8 * 2**20
MOST = 213 * 2**18
F32 = jnp.float32
BF16 = jnp.bfloat16
WHOLE = pl.BlockSpec(memory_space=pltpu.VMEM)
SCALARS = pl.BlockSpec(memory_space=pltpu.SMEM)
PLACE = pl.BlockSpec(memory_space=pl.ANY)
HBM = pl.BlockSpec(memory_space=pltpu.HBM)


def shares(columns, weights):
    tiles = columns // LANES
    if tiles < len(weights):
        return [columns]
    edges = [round(tiles * sum(weights[:i]) / sum(weights)) * LANES for i in range(len(weights))]
    edges.append(columns)
    return [high - low for low, high in zip(edges[:-1], edges[1:])]


def swap(block, axis, distance):
    count = lax.axis_size(axis)
    return lax.ppermute(block, axis, [(i, i ^ distance) for i in range(count)])


def swapped(matrix, axis, flag):
    half = matrix.shape[axis] // 2
    low = lax.slice_in_dim(matrix, 0, half, axis=axis)
    high = lax.slice_in_dim(matrix, half, 2 * half, axis=axis)
    return jnp.where(flag == 1, jnp.concatenate([high, low], axis=axis), matrix)


def matmul(left, right):
    return lax.dot_general(left, right, (((1,), (0,)), ((), ())), preferred_element_type=F32)


def span(name):
    flops = SPANS.get(name.split("_")[0], 10 * 10**8)
    return pl.CostEstimate(flops=flops, bytes_accessed=0, transcendentals=0)


def call(kernel, name, outs, specs, operands, after, limit=SCOPED, **more):
    extra = [] if after is None else [after]

    def body(*refs):
        kernel(*refs[: len(operands)], *refs[len(operands) + len(extra) :])

    return pl.pallas_call(
        body,
        name=name,
        in_specs=specs + [PLACE] * len(extra),
        out_shape=outs,
        compiler_params=pltpu.CompilerParams(vmem_limit_bytes=limit),
        **more,
    )(*operands, *extra)


def prepare(name, node_order, slots_out, slots_in, right, middle, left, held):
    width = middle.shape[-1]
    groups = node_order.shape[0]
    block = width // groups

    def kernel(node_order, right, middle, left, *refs):
        right0, right1, middle0, left0, left1, *passed = refs[len(held) :]
        for block_in, block_out in zip(refs[: len(held)], passed):
            block_out[...] = block_in[...]
        place, group = lax.axis_index("sub"), lax.axis_index("mid")
        bit0, bit1 = place & 1, place >> 1 & 1
        right0[...] = swapped(swapped(right[0, 0], 1, bit0), 0, bit1)
        place = lax.broadcasted_iota(jnp.int32, (width, 1), 0)
        source = place % block
        for i, slot in enumerate(slots_out):
            piece = node_order[slot ^ group] * block
            source += jnp.where(place // block == i, piece, 0)
        across = lax.broadcasted_iota(jnp.int32, (width, width), 1)
        pick = jnp.where(across == source, 1.0, 0.0).astype(BF16)
        right1[...] = matmul(pick, swapped(right[0, 1], 1, bit1)).astype(BF16)
        place = lax.broadcasted_iota(jnp.int32, (1, width), 1)
        source = place % block
        for i, slot in enumerate(slots_in):
            source += jnp.where(place // block == i, (slot ^ group) * block, 0)
        down = lax.broadcasted_iota(jnp.int32, (width, width), 0)
        pick = jnp.where(down == source, 1.0, 0.0).astype(BF16)
        middle0[...] = swapped(matmul(middle[0], pick).astype(BF16), 0, bit1)
        left0[...] = swapped(swapped(left[0, 0], 1, bit1), 0, bit0)
        left1[...] = swapped(left[0, 1], 1, bit0)

    return call(
        kernel,
        name,
        [jax.ShapeDtypeStruct((width, width), BF16)] * 5
        + [jax.ShapeDtypeStruct(block.shape, BF16) for block in held],
        [SCALARS] + [WHOLE] * (3 + len(held)),
        [node_order, right, middle, left] + held,
        None,
        out_specs=[WHOLE] * (5 + len(held)),
        cost_estimate=span(name),
    )


def row_pieces(rows, pieces):
    return pieces if rows % (pieces * ROWS) == 0 else 1


def opening(name, basis, signal, widths, groups):
    rows, width = basis.shape
    half = width // 2
    pieces = row_pieces(rows, 2)
    depth = rows // pieces
    lows = [sum(widths[:i]) for i in range(len(widths))]
    all_widths = widths + [sum(widths[i] for i in group) for group in groups]

    def kernel(basis, signal, *refs):
        outs, (basis_here, signal_here, arrived, basis_arrived) = refs[:-4], refs[-4:]
        fetch_basis = pltpu.make_async_copy(basis, basis_here, basis_arrived)
        fetch_basis.start()
        copies = []
        for i in range(pieces):
            part = pl.ds(i * depth, depth)
            copies.append(
                pltpu.make_async_copy(signal.at[part], signal_here.at[part], arrived.at[i])
            )
            copies[-1].start()
        fetch_basis.wait()
        flipped = swapped(basis_here[...].T, 0, lax.axis_index("sub") & 1)
        for copy in copies:
            copy.wait()
        for group, send in zip(groups, outs[len(widths) :]):
            for i in group:
                low, wide = lows[i], widths[i]
                total = matmul(flipped, signal_here[:, low : low + wide])
                outs[i][...] = total[:half].astype(BF16)
                place = low - lows[group[0]]
                send[:, place : place + wide] = total[half:].astype(BF16)

    outs = call(
        kernel,
        name,
        [jax.ShapeDtypeStruct((half, wide), BF16) for wide in all_widths],
        [HBM, HBM],
        [basis, signal],
        None,
        limit=MOST,
        out_specs=[WHOLE] * len(all_widths),
        scratch_shapes=[
            pltpu.VMEM((rows, width), BF16),
            pltpu.VMEM(signal.shape, BF16),
            pltpu.SemaphoreType.DMA((pieces,)),
            pltpu.SemaphoreType.DMA,
        ],
        cost_estimate=span(name),
    )
    return outs[: len(widths)], outs[len(widths) :]


def level(name, weight, blocks, low, wide, count, before, after):
    width = weight.shape[0]
    depth = width // count
    ahead = sum(block.shape[1] for block in before)

    def kernel(weight, *refs):
        ins, outs = refs[: len(blocks)], refs[len(blocks) + len(before) :]
        here = [slice(low, low + wide) if ref.shape[1] > wide else slice(None) for ref in ins]
        stacked = jnp.concatenate([ref[:, part] for ref, part in zip(ins, here)], axis=0)
        total = matmul(weight[...], stacked)
        for i, out in enumerate(outs):
            value = total[i * depth : (i + 1) * depth].astype(BF16)
            if before and i == count - 1:
                out[:, :ahead] = refs[len(blocks)][...]
                out[:, ahead:] = value
            else:
                out[...] = value

    widths = [wide] * (count - 1) + [ahead + wide]
    return call(
        kernel,
        name,
        [jax.ShapeDtypeStruct((depth, columns), BF16) for columns in widths],
        [WHOLE] * (1 + len(blocks) + len(before)),
        [weight] + blocks + before,
        after,
        out_specs=[WHOLE] * count,
        cost_estimate=span(name),
    )


def digits(groups):
    bits = groups.bit_length() - 1
    found, shift = [(0, 2)], 1
    while shift < bits:
        count = 2 if shift + 2 <= bits else 1
        found.append((shift, 1 << count))
        shift += count
    return found


def layouts_of(groups, steps):
    layouts = [by_digit(range(groups), steps[0])]
    for step in steps[1:]:
        layouts.append(by_digit(sum(layouts[-1], []), step))
    return layouts


def values_of(radix):
    return [0] + sorted(range(1, radix), key=lambda value: -value.bit_count())


def by_digit(slots, digit):
    shift, radix = digit
    return [[r for r in slots if r >> shift & radix - 1 == value] for value in values_of(radix)]


def regroup(name, blocks, layout, digit, block, after):
    columns = blocks[0].shape[1]
    place = {r: (i, j) for i, held in enumerate(layout) for j, r in enumerate(held)}
    wanted = by_digit(sum(layout, []), digit)

    def sort(values):
        parts = [[values[place[r][0]][place[r][1] * block :][:block] for r in held] for held in wanted]
        return [jnp.concatenate(part, axis=0) for part in parts]

    if block % ROWS:
        return sort(blocks), wanted

    def kernel(*refs):
        for ref, value in zip(refs[len(blocks) :], sort([ref[...] for ref in refs[: len(blocks)]])):
            ref[...] = value

    outs = call(
        kernel,
        name,
        [jax.ShapeDtypeStruct((len(held) * block, columns), BF16) for held in wanted],
        [WHOLE] * len(blocks),
        blocks,
        after,
        out_specs=[WHOLE] * len(wanted),
        cost_estimate=span(name),
    )
    return list(outs), wanted


def last(name, weight, basis, keeps, got, before, low, columns, after):
    rows, width = basis.shape
    wide = got.shape[1]
    pieces = row_pieces(rows, 6)
    depth = rows // pieces
    given = [] if before is None else [before]

    def kernel(weight, basis, got, *refs):
        out, here, left = refs[len(keeps) + len(given) :]
        keep = jnp.concatenate([ref[...] for ref in refs[: len(keeps)]], axis=1)
        stacked = jnp.concatenate([keep, got[...]], axis=0)
        coeffs = matmul(weight[...], stacked).astype(BF16)
        copies = []
        for i in range(pieces):
            part = pl.ds(i * depth, depth)
            here[part, :] = matmul(basis[part, :], coeffs).astype(BF16)
            copy = pltpu.make_async_copy(here.at[part], out.at[part, pl.ds(low, wide)], left.at[i])
            copy.start()
            copies.append(copy)
        for copy in copies:
            copy.wait()

    return call(
        kernel,
        name,
        jax.ShapeDtypeStruct((rows, columns), BF16),
        [WHOLE] * (3 + len(keeps)) + [HBM] * len(given),
        [weight, basis, got] + keeps + given,
        after,
        out_specs=HBM,
        scratch_shapes=[pltpu.VMEM((rows, wide), BF16), pltpu.SemaphoreType.DMA((pieces,))],
        input_output_aliases={3 + len(keeps): 0} if given else {},
        cost_estimate=span(name),
    )


def local(signal, col_basis, right_coupling, middle_coupling, left_coupling, row_basis, node_order):
    groups = lax.axis_size("mid")
    width = col_basis.shape[1]
    block = width // groups
    columns = signal.shape[1]
    chunks = shares(columns, SHARES)
    lows = [sum(chunks[:i]) for i in range(len(chunks))]
    whole = len(chunks) == len(SHARES)
    heads = HEADS if whole else ((0,),)
    tails = TAILS if whole else ((0,),)
    steps = digits(groups)
    layouts = layouts_of(groups, steps)

    keeps, sends = opening("opening", col_basis, signal, chunks, heads)
    right0, right1, middle, left0, left1, *later = prepare(
        "prepare",
        node_order,
        sum(layouts[0], []),
        sum(layouts[-1], []),
        right_coupling,
        middle_coupling,
        left_coupling,
        list(sends[1:]),
    )
    gots = {}
    for group, send in zip(heads, [sends[0]] + later):
        got = swap(send, "sub", 1)
        for i in group:
            gots[i] = (got, lows[i] - lows[group[0]])

    out, after = None, right0
    waiting, pops, entered = [], 0, 0
    parked = {}
    while waiting or entered < len(chunks):
        if entered < len(chunks) and (pops >= ENTRY[entered] or not waiting):
            waiting.append((1, entered, [keeps[entered], gots[entered][0]]))
            entered += 1
            continue
        stage, i, blocks = waiting.pop(0)
        pops += 1
        wide = chunks[i]
        if stage == 1:
            results = level(f"right0_{i}", right0, blocks, gots[i][1], wide, 2, [], after)
            axis, shift, radix = "sub", 1, 2
        elif stage == 2:
            count = steps[0][1]
            results = level(f"right1_{i}", right1, blocks, 0, wide, count, [], after)
            axis, shift, radix = "mid", *steps[0]
        elif stage < 2 + len(steps):
            step = steps[stage - 2]
            results, _ = regroup(
                f"regroup{stage}_{i}", blocks, layouts[stage - 3], step, block, after
            )
            axis, shift, radix = "mid", *step
        elif stage == 2 + len(steps):
            results = level(f"middle_{i}", middle, blocks, 0, wide, 2, [], after)
            axis, shift, radix = "sub", 1, 2
        elif stage == 3 + len(steps):
            group = next(group for group in tails if i in group)
            before = [parked[group[0]][-1]] if i != group[0] else []
            results = level(f"left0_{i}", left0, blocks, 0, wide, 2, before, after)
            axis, shift, radix = "sub", 0, 2
            parked[group[0]] = parked.get(group[0], [])[:-1] + list(results)
            if i != group[-1]:
                after = results[0]
                continue
            results = parked[group[0]]
            got = swap(results[-1], axis, 1)
            waiting.append((stage + 1, group[0], [results[:-1], got]))
            after = results[-2]
            continue
        else:
            name = f"last_{i}"
            out = last(name, left1, row_basis, *blocks, out, lows[i], columns, after)
            continue
        after = results[0]
        routes = [value << shift for value in values_of(radix)[1:]]
        moved = [swap(send, axis, route) for send, route in zip(results[1:], routes)]
        waiting.append((stage + 1, i, [results[0]] + moved))
    return out


def solution(mesh):
    return jax.shard_map(
        local,
        mesh=mesh,
        in_specs=(
            P(("mid", "sub"), None),
            P(("mid", "sub"), None),
            P(("mid", "sub"), None, None, None),
            P(("mid", "sub"), None, None),
            P(("mid", "sub"), None, None, None),
            P(("mid", "sub"), None),
            P(),
        ),
        out_specs=P(("mid", "sub"), None),
        check_vma=False,
    )
```

```python
import jax
import jax.numpy as jnp
from jax import lax
from jax.experimental import pallas as pl
from jax.experimental.pallas import tpu as pltpu
from jax.sharding import PartitionSpec as P

LANES = 128
ENTRY_SHARES = (3, 3, 3)
ENTRY = (0, 0, 1)
MERGED = ((0,), (1,), (2,))
SPLIT = {}
ROWS = 16
SCOPED = 8 * 2**20
MOST = 213 * 2**18
F32 = jnp.float32
BF16 = jnp.bfloat16
WHOLE = pl.BlockSpec(memory_space=pltpu.VMEM)
SCALARS = pl.BlockSpec(memory_space=pltpu.SMEM)
PLACE = pl.BlockSpec(memory_space=pl.ANY)
HBM = pl.BlockSpec(memory_space=pltpu.HBM)


def shares(columns, weights):
    tiles = columns // LANES
    if tiles < len(weights):
        return [columns]
    edges = [round(tiles * sum(weights[:i]) / sum(weights)) * LANES for i in range(len(weights))]
    edges.append(columns)
    return [high - low for low, high in zip(edges[:-1], edges[1:])]


def swap(block, axis, distance):
    count = lax.axis_size(axis)
    return lax.ppermute(block, axis, [(i, i ^ distance) for i in range(count)])


def swapped(matrix, axis, flag):
    half = matrix.shape[axis] // 2
    low = lax.slice_in_dim(matrix, 0, half, axis=axis)
    high = lax.slice_in_dim(matrix, half, 2 * half, axis=axis)
    return jnp.where(flag == 1, jnp.concatenate([high, low], axis=axis), matrix)


def matmul(left, right):
    return lax.dot_general(left, right, (((1,), (0,)), ((), ())), preferred_element_type=F32)


def cost(flops, moved):
    return pl.CostEstimate(flops=flops, bytes_accessed=moved, transcendentals=0)


def call(kernel, name, outs, specs, operands, after, limit=SCOPED, **more):
    extra = [] if after is None else [after]

    def body(*refs):
        kernel(*refs[: len(operands)], *refs[len(operands) + len(extra) :])

    return pl.pallas_call(
        body,
        name=name,
        in_specs=specs + [PLACE] * len(extra),
        out_shape=outs,
        compiler_params=pltpu.CompilerParams(vmem_limit_bytes=limit),
        **more,
    )(*operands, *extra)


def prepare(name, node_order, slots_out, slots_in, right, middle, left, after):
    width = middle.shape[-1]
    groups = node_order.shape[0]
    block = width // groups

    def kernel(node_order, right, middle, left, right0, right1, middle0, left0, left1):
        place, group = lax.axis_index("sub"), lax.axis_index("mid")
        bit0, bit1 = place & 1, place >> 1 & 1
        right0[...] = swapped(swapped(right[0, 0], 1, bit0), 0, bit1)
        place = lax.broadcasted_iota(jnp.int32, (width, 1), 0)
        source = place % block
        for i, slot in enumerate(slots_out):
            piece = node_order[slot ^ group] * block
            source += jnp.where(place // block == i, piece, 0)
        across = lax.broadcasted_iota(jnp.int32, (width, width), 1)
        pick = jnp.where(across == source, 1.0, 0.0).astype(BF16)
        right1[...] = matmul(pick, swapped(right[0, 1], 1, bit1)).astype(BF16)
        place = lax.broadcasted_iota(jnp.int32, (1, width), 1)
        source = place % block
        for i, slot in enumerate(slots_in):
            source += jnp.where(place // block == i, (slot ^ group) * block, 0)
        down = lax.broadcasted_iota(jnp.int32, (width, width), 0)
        pick = jnp.where(down == source, 1.0, 0.0).astype(BF16)
        middle0[...] = swapped(matmul(middle[0], pick).astype(BF16), 0, bit1)
        left0[...] = swapped(swapped(left[0, 0], 1, bit1), 0, bit0)
        left1[...] = swapped(left[0, 1], 1, bit0)

    return call(
        kernel,
        name,
        [jax.ShapeDtypeStruct((width, width), BF16)] * 5,
        [SCALARS] + [WHOLE] * 3,
        [node_order, right, middle, left],
        after,
        out_specs=[WHOLE] * 5,
        cost_estimate=cost(4 * width**3, 20 * width**2),
    )


def row_pieces(rows, pieces):
    return pieces if rows % (pieces * ROWS) == 0 else 1


def opening(name, basis, signal, widths):
    rows, width = basis.shape
    half = width // 2
    pieces = row_pieces(rows, 2)
    depth = rows // pieces
    lows = [sum(widths[:i]) for i in range(len(widths))]

    def kernel(basis, signal, *refs):
        outs, (basis_here, signal_here, arrived, basis_arrived) = refs[:-4], refs[-4:]
        fetch_basis = pltpu.make_async_copy(basis, basis_here, basis_arrived)
        fetch_basis.start()
        copies = []
        for i in range(pieces):
            part = pl.ds(i * depth, depth)
            copies.append(
                pltpu.make_async_copy(signal.at[part], signal_here.at[part], arrived.at[i])
            )
            copies[-1].start()
        fetch_basis.wait()
        flipped = swapped(basis_here[...].T, 0, lax.axis_index("sub") & 1)
        for copy in copies:
            copy.wait()
        for i, (low, wide) in enumerate(zip(lows, widths)):
            total = matmul(flipped, signal_here[:, low : low + wide])
            outs[2 * i][...] = total[:half].astype(BF16)
            outs[2 * i + 1][...] = total[half:].astype(BF16)

    outs = call(
        kernel,
        name,
        [jax.ShapeDtypeStruct((half, wide), BF16) for wide in widths for _ in range(2)],
        [HBM, HBM],
        [basis, signal],
        None,
        limit=MOST,
        out_specs=[WHOLE] * (2 * len(widths)),
        scratch_shapes=[
            pltpu.VMEM((rows, width), BF16),
            pltpu.VMEM(signal.shape, BF16),
            pltpu.SemaphoreType.DMA((pieces,)),
            pltpu.SemaphoreType.DMA,
        ],
        cost_estimate=cost(2 * rows * width * sum(widths), 2 * rows * (sum(widths) + width)),
    )
    return list(zip(outs[0::2], outs[1::2]))


def level(name, weight, chunks, widths, count, after):
    width = weight.shape[0]
    depth = width // count
    columns = sum(widths)
    blocks = len(chunks[0])

    def kernel(weight, *refs):
        ins, outs = refs[: blocks * len(chunks)], refs[blocks * len(chunks) :]
        stacked = [
            jnp.concatenate([ref[...] for ref in ins[i * blocks : (i + 1) * blocks]], axis=0)
            for i in range(len(chunks))
        ]
        total = matmul(weight[...], jnp.concatenate(stacked, axis=1))
        low = 0
        for i, wide in enumerate(widths):
            for j in range(count):
                part = total[j * depth : (j + 1) * depth, low : low + wide]
                outs[i * count + j][...] = part.astype(BF16)
            low += wide

    flat = [block for chunk in chunks for block in chunk]
    outs = call(
        kernel,
        name,
        [jax.ShapeDtypeStruct((depth, wide), BF16) for wide in widths for _ in range(count)],
        [WHOLE] * (1 + len(flat)),
        [weight] + flat,
        after,
        out_specs=[WHOLE] * (count * len(widths)),
        cost_estimate=cost(2 * width * width * columns, 4 * width * columns),
    )
    return [list(outs[i * count : (i + 1) * count]) for i in range(len(widths))]


def digits(groups):
    bits = groups.bit_length() - 1
    found = [(0, 2)]
    while found[-1][0] + (found[-1][1].bit_length() - 1) < bits:
        shift = found[-1][0] + found[-1][1].bit_length() - 1
        found.append((shift, 4 if shift + 2 <= bits else 2))
    return found


def by_digit(slots, digit):
    shift, radix = digit
    return [[r for r in slots if r >> shift & radix - 1 == value] for value in range(radix)]


def regroup(name, blocks, layout, digit, block, after):
    columns = blocks[0].shape[1]
    place = {r: (i, j) for i, held in enumerate(layout) for j, r in enumerate(held)}
    wanted = by_digit(sum(layout, []), digit)

    def sort(values):
        parts = [[values[place[r][0]][place[r][1] * block :][:block] for r in held] for held in wanted]
        return [jnp.concatenate(part, axis=0) for part in parts]

    if block % ROWS:
        return sort(blocks), wanted

    def kernel(*refs):
        for ref, value in zip(refs[len(blocks) :], sort([ref[...] for ref in refs[: len(blocks)]])):
            ref[...] = value

    outs = call(
        kernel,
        name,
        [jax.ShapeDtypeStruct((len(held) * block, columns), BF16) for held in wanted],
        [WHOLE] * len(blocks),
        blocks,
        after,
        out_specs=[WHOLE] * len(wanted),
        cost_estimate=cost(0, 4 * block * len(place) * columns),
    )
    return list(outs), wanted


def last(name, weight, basis, keep, got, before, low, columns, after):
    rows, width = basis.shape
    wide = keep.shape[1]
    pieces = row_pieces(rows, 6)
    depth = rows // pieces
    given = [] if before is None else [before]

    def kernel(weight, basis, keep, got, *refs):
        out, here, left = refs[len(given) :]
        stacked = jnp.concatenate([keep[...], got[...]], axis=0)
        coeffs = matmul(weight[...], stacked).astype(BF16)
        copies = []
        for i in range(pieces):
            part = pl.ds(i * depth, depth)
            here[part, :] = matmul(basis[part, :], coeffs).astype(BF16)
            copy = pltpu.make_async_copy(here.at[part], out.at[part, pl.ds(low, wide)], left.at[i])
            copy.start()
            copies.append(copy)
        for copy in copies:
            copy.wait()

    return call(
        kernel,
        name,
        jax.ShapeDtypeStruct((rows, columns), BF16),
        [WHOLE] * 4 + [HBM] * len(given),
        [weight, basis, keep, got] + given,
        after,
        out_specs=HBM,
        scratch_shapes=[pltpu.VMEM((rows, wide), BF16), pltpu.SemaphoreType.DMA((pieces,))],
        input_output_aliases={4: 0} if given else {},
        cost_estimate=cost(2 * rows * width * wide, 2 * rows * wide),
    )


def local(signal, col_basis, right_coupling, middle_coupling, left_coupling, row_basis, node_order):
    groups = lax.axis_size("mid")
    width = col_basis.shape[1]
    block = width // groups
    columns = signal.shape[1]
    chunks = shares(columns, ENTRY_SHARES)
    starts = [sum(chunks[:i]) for i in range(len(chunks))]
    merged = {i: group for group in MERGED for i in group}
    if len(chunks) < len(ENTRY_SHARES):
        merged = {i: (i,) for i in range(len(chunks))}
    steps = digits(groups)
    layouts = [by_digit(range(groups), steps[0])]
    for step in steps[1:]:
        layouts.append(by_digit(sum(layouts[-1], []), step))

    opened = opening("opening", col_basis, signal, chunks)
    couplings, out, after = None, None, None
    waiting, pops, entered = [], 0, 0
    parked = {}
    while waiting or entered < len(chunks):
        if entered < len(chunks) and (pops >= ENTRY[entered] or not waiting):
            i, entered = entered, entered + 1
            keep, send = opened[i]
            waiting.append((1, (i,), starts[i], [keep, swap(send, "sub", 1)]))
            continue
        stage, ids, low, blocks = waiting.pop(0)
        pops += 1
        wide = blocks[0].shape[1]
        name = "".join(str(i) for i in ids)
        if couplings is None:
            couplings = prepare(
                "prepare",
                node_order,
                sum(layouts[0], []),
                sum(layouts[-1], []),
                right_coupling,
                middle_coupling,
                left_coupling,
                after,
            )
            right0, right1, middle, left0, left1 = couplings
            after = right0
        if stage == 1:
            results = level(f"right0_{name}", right0, [blocks], [wide], 2, after)
            axis, shift = "sub", 1
        elif stage == 2:
            parked[ids[0]] = blocks
            ids = merged[ids[0]]
            if any(i not in parked for i in ids):
                continue
            wide = sum(chunks[i] for i in ids)
            low = starts[ids[0]]
            blocks = [parked[i] for i in ids]
            results = level(f"right1_{name}", right1, blocks, [wide], steps[0][1], after)
            axis, shift = "mid", steps[0][0]
        elif stage < 2 + len(steps):
            step = steps[stage - 2]
            held_as = layouts[stage - 3]
            results = [regroup(f"regroup{stage}_{name}", blocks, held_as, step, block, after)[0]]
            axis, shift = "mid", step[0]
        elif stage == 2 + len(steps):
            widths = shares(wide, SPLIT.get(ids, (1,)))
            results = level(f"middle_{name}", middle, [blocks], widths, 2, after)
            axis, shift = "sub", 1
        elif stage == 3 + len(steps):
            results = level(f"left0_{name}", left0, [blocks], [wide], 2, after)
            axis, shift = "sub", 0
        else:
            out = last(f"last{low}", left1, row_basis, *blocks, out, low, columns, after)
            continue
        after = results[0][0]
        for result in results:
            moved = [swap(send, axis, i + 1 << shift) for i, send in enumerate(result[1:])]
            waiting.append((stage + 1, ids, low, result[:1] + moved))
            low += result[0].shape[1]
    return out


def solution(mesh):
    return jax.shard_map(
        local,
        mesh=mesh,
        in_specs=(
            P(("mid", "sub"), None),
            P(("mid", "sub"), None),
            P(("mid", "sub"), None, None, None),
            P(("mid", "sub"), None, None),
            P(("mid", "sub"), None, None, None),
            P(("mid", "sub"), None),
            P(),
        ),
        out_specs=P(("mid", "sub"), None),
        check_vma=False,
    )
```
